128 devices in a mesh: dp: 8 (over x, z_lo), mp: 16 (over z_hi, y, core).
Axes of the slice: x: 4, y: 4, z: 4 (z_hi: 2, z_lo: 2; z = z_hi * 2 + z_lo), core: 2. Of those that a mesh axis runs over, the one named last changes fastest.
Arguments:
- tokens: bfloat16 [16384, 1024], P(('dp', 'mp')), may hold values from -6 to 6
- memory: bfloat16 [16384, 1024], P('dp'), may hold values from -6 to 6
- cotangent: bfloat16 [16384, 1024], P(('dp', 'mp')), may hold values from -6 to 6
- tgt_len: int32 [16], P('dp'), may hold values from 256 to 1024, as said below
- src_len: int32 [16], P('dp'), may hold values from 256 to 1024, as said below
- pair_ids: int32 [16], P('dp'), may hold values from 0 to 63
- loss_weights: int32 [64], replicated, may hold values from 1 to 4
- first_gain: float32 [1024], replicated, may hold values from 0.1 to 1.9
- first_shift: float32 [1024], replicated, may hold values from -1.75 to 1.75
- self_query: bfloat16 [1024, 1024], P(None, 'mp'), may hold values from -0.1875 to 0.1875
- self_query_bias: float32 [1024], P('mp'), may hold values from -3 to 3
- self_key: bfloat16 [1024, 1024], P(None, 'mp'), may hold values from -0.1875 to 0.1875
- self_value: bfloat16 [1024, 1024], P(None, 'mp'), may hold values from -0.1875 to 0.1875
- self_value_bias: float32 [1024], P('mp'), may hold values from -3 to 3
- self_output: bfloat16 [1024, 1024], P('mp'), may hold values from -2.5 to 2.5
- self_output_bias: float32 [1024], replicated, may hold values from -1.75 to 1.75
- second_gain: float32 [1024], replicated, may hold values from 0.1 to 1.9
- second_shift: float32 [1024], replicated, may hold values from -1.75 to 1.75
- cross_query: bfloat16 [1024, 1024], P(None, 'mp'), may hold values from -0.1875 to 0.1875
- cross_query_bias: float32 [1024], P('mp'), may hold values from -3 to 3
- cross_key: bfloat16 [1024, 1024], P(None, 'mp'), may hold values from -0.1875 to 0.1875
- cross_value: bfloat16 [1024, 1024], P(None, 'mp'), may hold values from -0.1875 to 0.1875
- cross_value_bias: float32 [1024], P('mp'), may hold values from -3 to 3
- cross_output: bfloat16 [1024, 1024], P('mp'), may hold values from -2.5 to 2.5
- cross_output_bias: float32 [1024], replicated, may hold values from -1.75 to 1.75
- third_gain: float32 [1024], replicated, may hold values from 0.1 to 1.9
- third_shift: float32 [1024], replicated, may hold values from -1.75 to 1.75
- ffn_in: bfloat16 [1024, 4096], P(None, 'mp'), may hold values from -0.1875 to 0.1875
- ffn_in_bias: float32 [4096], P('mp'), may hold values from -3 to 3
- ffn_out: bfloat16 [4096, 1024], P('mp'), may hold values from -0.125 to 0.125
- ffn_out_bias: float32 [1024], replicated, may hold values from -1.75 to 1.75
Outputs:
- block_out: bfloat16 [16384, 1024], P(('dp', 'mp'))
- tokens_grad: float32 [16384, 1024], P(('dp', 'mp'))
- memory_grad: float32 [16384, 1024], P(('dp', 'mp'))
- first_gain_grad: float32 [1024], replicated
- first_shift_grad: float32 [1024], replicated
- self_query_grad: float32 [1024, 1024], P(None, 'mp')
- self_query_bias_grad: float32 [1024], P('mp')
- self_key_grad: float32 [1024, 1024], P(None, 'mp')
- self_value_grad: float32 [1024, 1024], P(None, 'mp')
- self_value_bias_grad: float32 [1024], P('mp')
- self_output_grad: float32 [1024, 1024], P('mp')
- self_output_bias_grad: float32 [1024], replicated
- second_gain_grad: float32 [1024], replicated
- second_shift_grad: float32 [1024], replicated
- cross_query_grad: float32 [1024, 1024], P(None, 'mp')
- cross_query_bias_grad: float32 [1024], P('mp')
- cross_key_grad: float32 [1024, 1024], P(None, 'mp')
- cross_value_grad: float32 [1024, 1024], P(None, 'mp')
- cross_value_bias_grad: float32 [1024], P('mp')
- cross_output_grad: float32 [1024, 1024], P('mp')
- cross_output_bias_grad: float32 [1024], replicated
- third_gain_grad: float32 [1024], replicated
- third_shift_grad: float32 [1024], replicated
- ffn_in_grad: float32 [1024, 4096], P(None, 'mp')
- ffn_in_bias_grad: float32 [4096], P('mp')
- ffn_out_grad: float32 [4096, 1024], P('mp')
- ffn_out_bias_grad: float32 [1024], replicated
The draws below stay inside these ranges and needn't reach their ends.
Inputs may be any that keep to these rules, and one draw needn't show every extreme that they name: `tgt_len`: in each group of 2 sequences of one index of dp, one drawn from the seed has exactly 1024 tokens. `src_len`: in each group of 2 sequences of one index of dp, one drawn from the seed has exactly 1024 source tokens.
All inputs are finite; a program needn't handle non-finite values.
Results may differ from the reference program's by a relative error of at most 0.025.
Values may be sent and summed in bfloat16 or wider, within the bound.
No kernel may reach another device: no remote copies, remote signals or barrier semaphores. Data moves between devices by JAX's collectives and lax.ppermute only.
A program may use at most 128 MiB of HBM per device.

```python
import jax
import jax.numpy as jnp
from jax import lax

D = 1024
HEADS = 16
HEAD = 64
FF = 4096
LEN = 1024
SRC = 1024
PAIRS = 64
SEQ_DEV = 2
SEQS = 16
TOKENS = 16384
MEMROWS = 16384


def length_draw(key, longest):
    groups = SEQS // SEQ_DEV
    drawn_lengths = jax.random.randint(key, (SEQS,), longest // 4, longest + 1)
    chosen = jax.random.randint(jax.random.fold_in(key, 7), (groups,), 0, SEQ_DEV)
    is_full = jnp.arange(SEQS) % SEQ_DEV == jnp.repeat(chosen, SEQ_DEV)
    return jnp.where(is_full, longest, drawn_lengths).astype(jnp.int32)


def draw_tgt_len(key, part):
    key = jax.random.fold_in(key, 1)
    return length_draw(key, LEN)


def draw_src_len(key, part):
    key = jax.random.fold_in(key, 2)
    return length_draw(key, SRC)


def plant(values, rng, least, top_value):
    shape = values.shape
    spot = [jax.random.randint(jax.random.fold_in(rng, axis), (), 0, shape[axis]) for axis in range(len(shape))]
    values = values.at[tuple(spot)].set(least)
    longest = shape.index(max(shape))
    spot[longest] = (spot[longest] + 1) % shape[longest]
    return values.at[tuple(spot)].set(top_value)


def block_levels(key, extent, cuts, smallest, top_value):
    factor_of, own = 1.0, jax.random.fold_in(key, 6)
    for position, blocks in cuts:
        draws = jnp.exp(jax.random.uniform(jax.random.fold_in(own, position), (blocks,), jnp.float32, smallest / len(cuts), top_value / len(cuts)))
        factor_of = factor_of * jnp.repeat(draws, extent[position] // blocks).reshape([-1 if axis == position else 1 for axis in range(len(extent))])
    return factor_of


def gaussian(own_key, extent, scale, bound, split=(), kind=jnp.bfloat16):
    array = jax.random.normal(own_key, extent, jnp.float32) * scale
    if len(split) > 0:
        array = block_levels(own_key, extent, split, -0.22, 0.18) * array
    return jnp.clip(array, min=-bound, max=bound).astype(kind)


def setup_inputs(seed: int = 0) -> dict:
    key_of = jax.random.split(jax.random.key(seed), 32)
    tokens = gaussian(key_of[0], (TOKENS, D), 1.0, 6.0, ((0, 128),))
    memory = gaussian(key_of[1], (MEMROWS, D), 1.0, 6.0, ((0, 8),))
    cotangent = gaussian(key_of[2], (TOKENS, D), 1.0, 6.0, ((0, 128),))
    tgt_len = draw_tgt_len(jax.random.fold_in(key_of[31], 71), 0)
    src_len = draw_src_len(jax.random.fold_in(key_of[31], 71), 0)
    pair_ids = plant(jax.random.randint(key_of[5], (SEQS,), 0, PAIRS), jax.random.fold_in(key_of[5], 1), 0, PAIRS - 1).astype(jnp.int32)
    loss_weights = plant(jax.random.randint(key_of[6], (PAIRS,), 1, 5), jax.random.fold_in(key_of[6], 1), 1, 4).astype(jnp.int32)
    first_gain = jnp.clip(1.0 + 0.18 * jax.random.normal(key_of[7], (D,), jnp.float32), 0.1, 1.9)
    first_shift = gaussian(key_of[8], (D,), 0.3, 1.75, (), jnp.float32)
    self_query = gaussian(key_of[9], (D, D), D ** -0.5, 0.1875, ((1, 16),))
    self_query_bias = gaussian(key_of[10], (D,), 0.5, 3.0, ((0, 16),), jnp.float32)
    self_key = gaussian(key_of[11], (D, D), D ** -0.5, 0.1875, ((1, 16),))
    self_value = gaussian(key_of[12], (D, D), D ** -0.5, 0.1875, ((1, 16),))
    self_value_bias = gaussian(key_of[13], (D,), 0.5, 3.0, ((0, 16),), jnp.float32)
    self_output = gaussian(key_of[14], (D, D), (5 * D // LEN) ** -0.5, 2.5, ((0, 16),))
    self_output_bias = gaussian(key_of[15], (D,), 0.3, 1.75, (), jnp.float32)
    second_gain = jnp.clip(1.0 + 0.18 * jax.random.normal(key_of[16], (D,), jnp.float32), 0.1, 1.9)
    second_shift = gaussian(key_of[17], (D,), 0.3, 1.75, (), jnp.float32)
    cross_query = gaussian(key_of[18], (D, D), D ** -0.5, 0.1875, ((1, 16),))
    cross_query_bias = gaussian(key_of[19], (D,), 0.5, 3.0, ((0, 16),), jnp.float32)
    cross_key = gaussian(key_of[20], (D, D), D ** -0.5, 0.1875, ((1, 16),))
    cross_value = gaussian(key_of[21], (D, D), D ** -0.5, 0.1875, ((1, 16),))
    cross_value_bias = gaussian(key_of[22], (D,), 0.5, 3.0, ((0, 16),), jnp.float32)
    cross_output = gaussian(key_of[23], (D, D), (5 * D // SRC) ** -0.5, 2.5, ((0, 16),))
    cross_output_bias = gaussian(key_of[24], (D,), 0.3, 1.75, (), jnp.float32)
    third_gain = jnp.clip(1.0 + 0.18 * jax.random.normal(key_of[25], (D,), jnp.float32), 0.1, 1.9)
    third_shift = gaussian(key_of[26], (D,), 0.3, 1.75, (), jnp.float32)
    ffn_in = gaussian(key_of[27], (D, FF), D ** -0.5, 0.1875, ((1, 16),))
    ffn_in_bias = gaussian(key_of[28], (FF,), 0.5, 3.0, ((0, 16),), jnp.float32)
    ffn_out = gaussian(key_of[29], (FF, D), (FF // 2) ** -0.5, 0.125, ((0, 16),))
    ffn_out_bias = gaussian(key_of[30], (D,), 0.3, 1.75, (), jnp.float32)
    return {"tokens": tokens, "memory": memory, "cotangent": cotangent, "tgt_len": tgt_len, "src_len": src_len, "pair_ids": pair_ids, "loss_weights": loss_weights, "first_gain": first_gain, "first_shift": first_shift, "self_query": self_query, "self_query_bias": self_query_bias, "self_key": self_key, "self_value": self_value, "self_value_bias": self_value_bias, "self_output": self_output, "self_output_bias": self_output_bias, "second_gain": second_gain, "second_shift": second_shift, "cross_query": cross_query, "cross_query_bias": cross_query_bias, "cross_key": cross_key, "cross_value": cross_value, "cross_value_bias": cross_value_bias, "cross_output": cross_output, "cross_output_bias": cross_output_bias, "third_gain": third_gain, "third_shift": third_shift, "ffn_in": ffn_in, "ffn_in_bias": ffn_in_bias, "ffn_out": ffn_out, "ffn_out_bias": ffn_out_bias}


@jax.custom_vjp
def low(v):
    return lax.optimization_barrier(v.astype(jnp.bfloat16)).astype(jnp.float32)

@jax.custom_vjp
def low_back(v):
    return v

def low_keep(v):
    return (low(v), None)

def low_pass(kept, grad):
    return (grad,)

def back_keep(v):
    return (v, None)

def back_low(kept, grad):
    return (low(grad),)
low.defvjp(low_keep, low_pass)
low_back.defvjp(back_keep, back_low)

def precise_dot(operand, factor):
    return jnp.dot(operand, factor, precision=lax.Precision.HIGHEST)

def layer_norm(inputs, norm_gain, norm_shift):
    center = inputs - lax.optimization_barrier(jnp.mean(inputs, axis=-1, keepdims=True))
    spread = lax.optimization_barrier(jnp.mean(center * center, axis=-1, keepdims=True))
    return center * lax.rsqrt(spread + 1e-05) * norm_gain + norm_shift

def attention(queries, key_rows, values, length, causal):
    query_len = queries.shape[0]
    key_len = key_rows.shape[0]
    query_heads = queries.reshape(query_len, HEADS, HEAD)
    key_heads = key_rows.reshape(key_len, HEADS, HEAD)
    value_heads = values.reshape(key_len, HEADS, HEAD)
    scores = low_back(jnp.einsum('qhe,khe->hqk', query_heads, key_heads, precision=lax.Precision.HIGHEST))
    key_pos = jnp.arange(key_len)
    allowed = (key_pos < length)[None, :]
    if causal:
        allowed = allowed & (key_pos[None, :] <= jnp.arange(query_len)[:, None])
    scores = jnp.where(allowed[None], scores, -1e+30)
    attn_probs = low(jax.nn.softmax(scores, axis=-1))
    attn_mixed = jnp.einsum('hqk,khe->qhe', attn_probs, value_heads, precision=lax.Precision.HIGHEST)
    return attn_mixed.reshape(query_len, HEADS * HEAD)

def causal_block(packed):
    return attention(packed[0], packed[1], packed[2], packed[3], True)

def source_block(packed):
    return attention(packed[0], packed[1], packed[2], packed[3], False)

def decoder_layer(tgt_len, src_len, tokens, memory, weights):
    first_gain, first_shift, self_query, self_query_bias, self_key, self_value, self_value_bias, self_output, self_output_bias, second_gain, second_shift, cross_query, cross_query_bias, cross_key, cross_value, cross_value_bias, cross_output, cross_output_bias, third_gain, third_shift, ffn_in, ffn_in_bias, ffn_out, ffn_out_bias = weights
    head_scale = HEAD ** (-0.5)
    first = low(layer_norm(tokens, first_gain, first_shift))
    queries = low(low_back(head_scale * (precise_dot(first, self_query) + self_query_bias)))
    key_rows = low(low_back(precise_dot(first, self_key)))
    values = low(low_back(precise_dot(first, self_value) + self_value_bias))
    self_mixed = lax.map(jax.checkpoint(causal_block), (queries.reshape(SEQS, LEN, D), key_rows.reshape(SEQS, LEN, D), values.reshape(SEQS, LEN, D), tgt_len))
    self_mixed = low(low_back(self_mixed.reshape(TOKENS, D)))
    second_resid = tokens + low_back(precise_dot(self_mixed, self_output) + self_output_bias)
    second = low(layer_norm(second_resid, second_gain, second_shift))
    cross_queries = low(low_back(head_scale * (precise_dot(second, cross_query) + cross_query_bias)))
    cross_keys = low(low_back(precise_dot(memory, cross_key)))
    cross_values = low(low_back(precise_dot(memory, cross_value) + cross_value_bias))
    cross_mixed = lax.map(jax.checkpoint(source_block), (cross_queries.reshape(SEQS, LEN, D), cross_keys.reshape(SEQS, SRC, D), cross_values.reshape(SEQS, SRC, D), src_len))
    cross_mixed = low(low_back(cross_mixed.reshape(TOKENS, D)))
    third_resid = second_resid + low_back(precise_dot(cross_mixed, cross_output) + cross_output_bias)
    third = low(layer_norm(third_resid, third_gain, third_shift))
    hidden_pre = low_back(precise_dot(third, ffn_in) + ffn_in_bias)
    hidden = low(jax.nn.gelu(hidden_pre, approximate=True))
    return third_resid + low_back(precise_dot(hidden, ffn_out) + ffn_out_bias)

def reference(tokens, memory, cotangent, tgt_len, src_len, pair_ids, loss_weights, first_gain, first_shift, self_query, self_query_bias, self_key, self_value, self_value_bias, self_output, self_output_bias, second_gain, second_shift, cross_query, cross_query_bias, cross_key, cross_value, cross_value_bias, cross_output, cross_output_bias, third_gain, third_shift, ffn_in, ffn_in_bias, ffn_out, ffn_out_bias):
    weights = tuple((item.astype(jnp.float32) for item in (first_gain, first_shift, self_query, self_query_bias, self_key, self_value, self_value_bias, self_output, self_output_bias, second_gain, second_shift, cross_query, cross_query_bias, cross_key, cross_value, cross_value_bias, cross_output, cross_output_bias, third_gain, third_shift, ffn_in, ffn_in_bias, ffn_out, ffn_out_bias)))
    layer_out, pullback = jax.vjp(lambda inputs, source, params: decoder_layer(tgt_len, src_len, inputs, source, params), tokens.astype(jnp.float32), memory.astype(jnp.float32), weights)
    seq_weight = 0.5 * loss_weights[pair_ids].astype(jnp.float32)
    positions = jnp.arange(LEN)
    row_scale = jnp.where(positions[None, :] < tgt_len[:, None], seq_weight[:, None], 0.0).reshape(TOKENS)
    tokens_grad, memory_grad, grads = pullback(cotangent.astype(jnp.float32) * row_scale[:, None])
    return (layer_out.astype(jnp.bfloat16), tokens_grad, memory_grad, grads[0], grads[1], grads[2], grads[3], grads[4], grads[5], grads[6], grads[7], grads[8], grads[9], grads[10], grads[11], grads[12], grads[13], grads[14], grads[15], grads[16], grads[17], grads[18], grads[19], grads[20], grads[21], grads[22], grads[23])
```

```python
import jax
import jax.numpy as jnp
from jax import lax
from jax.sharding import Mesh, PartitionSpec as P

HEAD = 64
BF = jnp.bfloat16
F32 = jnp.float32


def nn(a, b):
    return jnp.dot(a, b, preferred_element_type=F32)


def nt(a, b):
    return lax.dot_general(a, b, (((1,), (1,)), ((), ())), preferred_element_type=F32)


def tn(a, b):
    return lax.dot_general(a, b, (((0,), (0,)), ((), ())), preferred_element_type=F32)


def ring(n, k):
    return [(i, (i + k) % n) for i in range(n)]


def from_core(v):
    return lax.ppermute(v, "c", ring(2, 1))


def from_half(v):
    return lax.ppermute(v, ("zl", "zh"), [(i, 3 - i) for i in range(4)])


def from_zl(v):
    return lax.ppermute(v, "zl", ring(2, 1))


def sibling_heads(v):
    return jnp.concatenate([v[:, 128:256], v[:, :128], v[:, 384:], v[:, 256:384]], axis=1)


def gather_rel(v, axis="y"):
    return [v] + [lax.ppermute(v, axis, ring(4, 4 - r)) for r in range(1, 4)]


def gather_rows(v):
    return jnp.concatenate(gather_rel(v), axis=0)


def scatter_sum(blocks, axis="y"):
    got = [lax.ppermute(blocks[r], axis, ring(4, r)) for r in range(1, 4)]
    total = blocks[0].astype(F32)
    for g in got:
        total = total + g.astype(F32)
    return total


def scatter_rows(part):
    part = part.astype(BF)
    return scatter_sum([part[r * 128 : (r + 1) * 128] for r in range(4)])


def whole_sum(vectors):
    n = vectors.shape[0]

    def spread(v, axes, count):
        return jnp.sum(lax.all_to_all(jnp.broadcast_to(v[None], (count,) + v.shape), axes, 0, 0), axis=0)

    v = spread(vectors, ("zh", "y", "c"), 16)
    return spread(v, ("x", "zl"), 8)


def pick(index, blocks):
    out = blocks[0]
    for i in range(1, len(blocks)):
        out = jnp.where(index == i, blocks[i], out)
    return out


def grad_sum(parts):
    rows = parts.shape[0] // 4
    low = parts.astype(BF)
    mine = parts[: 2 * rows] + from_core(low[2 * rows :]).astype(F32)
    set_sum = mine[:rows] + from_half(mine[rows:].astype(BF)).astype(F32)
    set_low = set_sum.astype(BF)
    zl = lax.axis_index("zl")
    x = lax.axis_index("x")
    half = rows // 2
    keep = lax.dynamic_slice_in_dim(set_sum, zl * half, half, 0)
    send = lax.dynamic_slice_in_dim(set_low, (1 - zl) * half, half, 0)
    halves = (keep + from_zl(send).astype(F32)).astype(BF)
    quarter = half // 4
    blocks = [lax.dynamic_slice_in_dim(halves, ((x + r) % 4) * quarter, quarter, 0) for r in range(4)]
    piece = scatter_sum(blocks, "x").astype(BF)
    got = gather_rel(piece, "x")
    whole = jnp.zeros((half, parts.shape[1]), BF)
    for r in range(4):
        whole = lax.dynamic_update_slice_in_dim(whole, got[r], ((x + r) % 4) * quarter, 0)
    other = from_zl(whole)
    low_half = jnp.where(zl == 0, whole, other)
    high_half = jnp.where(zl == 0, other, whole)
    return jnp.concatenate([low_half, high_half], axis=0).astype(F32)


def layer_norm(inputs, gain, shift):
    center = inputs - jnp.mean(inputs, axis=-1, keepdims=True)
    inverse = lax.rsqrt(jnp.mean(center * center, axis=-1, keepdims=True) + 1e-05)
    normal = center * inverse
    return normal * gain + shift, normal, inverse


def norm_back(gradient, normal, inverse, gain):
    scaled = gradient * gain
    adjusted = (
        scaled
        - jnp.mean(scaled, axis=-1, keepdims=True)
        - normal * jnp.mean(scaled * normal, axis=-1, keepdims=True)
    )
    return adjusted * inverse, jnp.sum(gradient * normal, axis=0), jnp.sum(gradient, axis=0)


def split_heads(v):
    return v.reshape(v.shape[0], v.shape[1] // HEAD, HEAD)


def attend_forward(queries, keys, values, allowed):
    scores = jnp.einsum("qhe,khe->hqk", split_heads(queries), split_heads(keys), preferred_element_type=F32)
    scores = jnp.where(allowed[None], scores, -1e30)
    highest = jnp.max(scores, axis=-1, keepdims=True)
    raised = jnp.exp(scores - highest)
    totals = jnp.sum(raised, axis=-1, keepdims=True)
    probs = (raised / totals).astype(BF)
    mixed = jnp.einsum("hqk,khe->qhe", probs, split_heads(values), preferred_element_type=F32)
    return mixed.reshape(queries.shape), (highest + jnp.log(totals))[..., 0]


def attend_backward(queries, keys, values, allowed, log_total, mixed_grad):
    qh, kh, gh = split_heads(queries), split_heads(keys), split_heads(mixed_grad)
    scores = jnp.einsum("qhe,khe->hqk", qh, kh, preferred_element_type=F32)
    probs = jnp.where(allowed[None], jnp.exp(scores - log_total[..., None]), 0.0)
    value_grad = jnp.einsum("hqk,qhe->khe", probs.astype(BF), gh, preferred_element_type=F32)
    prob_grad = jnp.einsum("qhe,khe->hqk", gh, split_heads(values), preferred_element_type=F32)
    inner = jnp.sum(probs * prob_grad, axis=-1, keepdims=True)
    score_grad = (probs * (prob_grad - inner)).astype(BF)
    query_grad = jnp.einsum("hqk,khe->qhe", score_grad, kh, preferred_element_type=F32)
    key_grad = jnp.einsum("hqk,qhe->khe", score_grad, qh, preferred_element_type=F32)
    return (
        query_grad.reshape(queries.shape),
        key_grad.reshape(keys.shape),
        value_grad.reshape(keys.shape),
    )


def per_device(
    tokens,
    memory,
    cotangent,
    tgt_len,
    src_len,
    pair_ids,
    loss_weights,
    first_gain,
    first_shift,
    self_query,
    self_query_bias,
    self_key,
    self_value,
    self_value_bias,
    self_output,
    self_output_bias,
    second_gain,
    second_shift,
    cross_query,
    cross_query_bias,
    cross_key,
    cross_value,
    cross_value_bias,
    cross_output,
    cross_output_bias,
    third_gain,
    third_shift,
    ffn_in,
    ffn_in_bias,
    ffn_out,
    ffn_out_bias,
):
    zh = lax.axis_index("zh")
    y = lax.axis_index("y")
    c = lax.axis_index("c")
    scale = HEAD ** (-0.5)

    def sets(v):
        pair = jnp.concatenate([v, from_half(v)], axis=0)
        return jnp.concatenate([pair, from_core(pair)], axis=0)

    def heads_of(packed, count, index):
        return jnp.concatenate(
            [packed[(s * count + index) * 64 : (s * count + index + 1) * 64] for s in range(4)], axis=0
        )

    tok = tokens.astype(F32)
    first_norm, first_normal, first_inverse = layer_norm(tok, first_gain, first_shift)
    first = gather_rows(first_norm.astype(BF))

    pack_one = sets(jnp.concatenate([self_query.T, self_key.T, self_value.T], axis=0))
    wq, wk, wv = (heads_of(pack_one, 3, i) for i in range(3))
    bias_row = jnp.concatenate(
        [self_query_bias, self_value_bias, cross_query_bias, cross_value_bias, ffn_in_bias]
    ).reshape(1, 512)
    biases = sets(bias_row)
    bq, bv, cbq, cbv = (biases[:, i * 64 : (i + 1) * 64].reshape(256) for i in range(4))
    fb = biases[:, 256:].reshape(1024)
    pack_two = sets(
        jnp.concatenate([self_output, cross_query.T, cross_key.T, cross_value.T, cross_output], axis=0)
    )
    wo, cwq, cwk, cwv, cwo = (heads_of(pack_two, 5, i) for i in range(5))
    win = sets(ffn_in.T)
    wout = sets(ffn_out)

    tl = lax.dynamic_index_in_dim(tgt_len, zh, 0, False)
    sl = lax.dynamic_index_in_dim(src_len, zh, 0, False)
    pair = lax.dynamic_index_in_dim(pair_ids, zh, 0, False)
    weight = 0.5 * lax.dynamic_index_in_dim(loss_weights, pair, 0, False).astype(F32)
    own_pos = (2 * y + c) * 128 + jnp.arange(128)
    out_grad = cotangent.astype(F32) * jnp.where(own_pos < tl, weight, 0.0)[:, None]
    out_grad_low = out_grad.astype(BF)
    og = gather_rows(out_grad_low)

    queries = (scale * (nt(first, wq) + bq)).astype(BF)
    keys = nt(first, wk).astype(BF)
    values = (nt(first, wv) + bv).astype(BF)
    kv = jnp.concatenate([keys, values], axis=1)
    kv = jnp.concatenate([kv, sibling_heads(from_core(kv))], axis=0)
    all_keys, all_values = kv[:, :256], kv[:, 256:]
    block = (2 * ((y + jnp.arange(4)) % 4))[:, None] * 128 + jnp.arange(128)[None, :]
    q_pos = (block + c * 128).reshape(512)
    k_pos = jnp.concatenate([q_pos, (block + (1 - c) * 128).reshape(512)])
    causal = (k_pos[None, :] <= q_pos[:, None]) & (k_pos < tl)[None, :]
    self_mixed, self_total = attend_forward(queries, all_keys, all_values, causal)
    self_mixed = self_mixed.astype(BF)
    second_resid = tok + scatter_rows(nn(self_mixed, wo)) + self_output_bias
    second_norm, second_normal, second_inverse = layer_norm(second_resid, second_gain, second_shift)
    second = gather_rows(second_norm.astype(BF))

    mem = lax.dynamic_slice_in_dim(memory, zh * 1024, 1024, 0)
    cross_queries = (scale * (nt(second, cwq) + cbq)).astype(BF)
    cross_keys = nt(mem, cwk).astype(BF)
    cross_values = (nt(mem, cwv) + cbv).astype(BF)
    source = jnp.broadcast_to((jnp.arange(1024) < sl)[None, :], (512, 1024))
    cross_mixed, cross_total = attend_forward(cross_queries, cross_keys, cross_values, source)
    cross_mixed = cross_mixed.astype(BF)
    third_resid = second_resid + scatter_rows(nn(cross_mixed, cwo)) + cross_output_bias
    third_norm, third_normal, third_inverse = layer_norm(third_resid, third_gain, third_shift)
    third = gather_rows(third_norm.astype(BF))

    hidden_pre = nt(third, win) + fb
    gelu_value, gelu_pull = jax.vjp(lambda v: jax.nn.gelu(v, approximate=True), hidden_pre)
    hidden = gelu_value.astype(BF)
    pre_grad = gelu_pull(nt(og, wout))[0].astype(BF)
    third_back = scatter_rows(nn(pre_grad, win))
    layer_out = third_resid + scatter_rows(nn(hidden, wout)) + ffn_out_bias
    block_out = layer_out.astype(BF)
    third_input, third_gain_part, third_shift_part = norm_back(
        third_back, third_normal, third_inverse, third_gain
    )
    third_grad = out_grad + third_input
    third_grad_low = third_grad.astype(BF)
    tg = gather_rows(third_grad_low)
    ffn_in_grad = tn(pre_grad, third)
    ffn_out_grad = tn(hidden, og)
    ffn_in_bias_grad = jnp.sum(pre_grad.astype(F32), axis=0)

    cross_mixed_grad = nt(tg, cwo).astype(BF)
    cq_grad, ck_part, cv_part = attend_backward(
        cross_queries, cross_keys, cross_values, source, cross_total, cross_mixed_grad
    )
    cq_grad = cq_grad.astype(BF)
    second_back = scatter_rows(scale * nn(cq_grad, cwq))
    second_input, second_gain_part, second_shift_part = norm_back(
        second_back, second_normal, second_inverse, second_gain
    )
    second_grad = third_grad + second_input
    second_grad_low = second_grad.astype(BF)
    sg = gather_rows(second_grad_low)

    def by_core(v):
        v = v.reshape(4, 2, 128, v.shape[-1])
        v = jnp.concatenate([v[:, 0].reshape(512, -1), v[:, 1].reshape(512, -1)], axis=0)
        own = lax.dynamic_slice_in_dim(v, c * 512, 512, 0)
        other = lax.dynamic_slice_in_dim(v, (1 - c) * 512, 512, 0)
        return own, other

    ckv = jnp.concatenate([ck_part, cv_part], axis=1)
    ckv_own, ckv_other = by_core(ckv)
    ckv_grad = (ckv_own + sibling_heads(from_core(ckv_other.astype(BF))).astype(F32)).astype(BF)
    ck_grad, cv_grad = ckv_grad[:, :256], ckv_grad[:, 256:]
    mem_own, _ = by_core(mem)
    memory_part = (nn(ck_grad, cwk) + nn(cv_grad, cwv)).astype(BF)
    memory_grad = scatter_sum(
        [lax.dynamic_slice_in_dim(memory_part, ((y + r) % 4) * 128, 128, 0) for r in range(4)]
    )
    cross_output_grad = tn(cross_mixed, tg)
    cross_query_grad = scale * tn(cq_grad, second)
    ckv_weight_grad = tn(ckv_grad, mem_own)
    cross_query_bias_grad = scale * jnp.sum(cq_grad.astype(F32), axis=0)
    cross_value_bias_grad = jnp.sum(cv_grad.astype(F32), axis=0)

    self_mixed_grad = nt(sg, wo).astype(BF)
    q_grad, k_part, v_part = attend_backward(
        queries, all_keys, all_values, causal, self_total, self_mixed_grad
    )
    q_grad = q_grad.astype(BF)
    kv_part = jnp.concatenate([k_part, v_part], axis=1)
    kv_grad = (kv_part[:512] + sibling_heads(from_core(kv_part[512:].astype(BF))).astype(F32)).astype(BF)
    k_grad, v_grad = kv_grad[:, :256], kv_grad[:, 256:]
    first_back = scatter_rows(scale * nn(q_grad, wq) + nn(k_grad, wk) + nn(v_grad, wv))
    first_input, first_gain_part, first_shift_part = norm_back(
        first_back, first_normal, first_inverse, first_gain
    )
    tokens_grad = second_grad + first_input
    self_output_grad = tn(self_mixed, sg)
    self_query_grad = scale * tn(q_grad, first)
    kv_weight_grad = tn(kv_grad, first)
    self_query_bias_grad = scale * jnp.sum(q_grad.astype(F32), axis=0)
    self_value_bias_grad = jnp.sum(v_grad.astype(F32), axis=0)

    def bias_rows(values):
        n = values.shape[1]
        return jnp.pad(values[:, None, :], ((0, 0), (0, 15), (0, 1024 - n)))

    def pack(matrices, bias):
        parts = [m.reshape(4, -1, 1024) for m in matrices]
        if bias is not None:
            parts.append(bias_rows(bias))
        joined = jnp.concatenate(parts, axis=1)
        return joined.reshape(-1, 1024)

    ffn_sum = grad_sum(pack([ffn_in_grad, ffn_out_grad], ffn_in_bias_grad.reshape(4, 256)))
    cross_sum = grad_sum(
        pack(
            [cross_output_grad, cross_query_grad, ckv_weight_grad[:256], ckv_weight_grad[256:]],
            jnp.concatenate(
                [cross_query_bias_grad.reshape(4, 64), cross_value_bias_grad.reshape(4, 64)], axis=1
            ),
        )
    )
    self_sum = grad_sum(
        pack(
            [self_output_grad, self_query_grad, kv_weight_grad[:256], kv_weight_grad[256:]],
            jnp.concatenate(
                [self_query_bias_grad.reshape(4, 64), self_value_bias_grad.reshape(4, 64)], axis=1
            ),
        )
    )
    vectors = whole_sum(
        jnp.stack(
            [
                first_gain_part,
                first_shift_part,
                second_gain_part,
                second_shift_part,
                third_gain_part,
                third_shift_part,
                jnp.sum(out_grad_low.astype(F32), axis=0),
                jnp.sum(third_grad_low.astype(F32), axis=0),
                jnp.sum(second_grad_low.astype(F32), axis=0),
            ]
        )
    )
    return (
        block_out,
        tokens_grad,
        memory_grad,
        vectors[0],
        vectors[1],
        self_sum[64:128].T,
        self_sum[256, :64],
        self_sum[128:192].T,
        self_sum[192:256].T,
        self_sum[256, 64:128],
        self_sum[:64],
        vectors[8],
        vectors[2],
        vectors[3],
        cross_sum[64:128].T,
        cross_sum[256, :64],
        cross_sum[128:192].T,
        cross_sum[192:256].T,
        cross_sum[256, 64:128],
        cross_sum[:64],
        vectors[7],
        vectors[4],
        vectors[5],
        ffn_sum[:256].T,
        ffn_sum[512, :256],
        ffn_sum[256:512],
        vectors[6],
    )


def solution(mesh):
    fine = Mesh(mesh.devices.reshape(4, 2, 2, 4, 2), ("x", "zl", "zh", "y", "c"))
    dp = ("x", "zl")
    mp = ("zh", "y", "c")
    rows = P(dp + mp, None)
    cols = P(None, mp)
    part = P(mp)
    down = P(mp, None)
    whole = P()
    placed = (
        rows,
        P(dp, None),
        rows,
        P(dp),
        P(dp),
        P(dp),
        whole,
        whole,
        whole,
        cols,
        part,
        cols,
        cols,
        part,
        down,
        whole,
        whole,
        whole,
        cols,
        part,
        cols,
        cols,
        part,
        down,
        whole,
        whole,
        whole,
        cols,
        part,
        down,
        whole,
    )
    given = (
        rows,
        rows,
        rows,
        whole,
        whole,
        cols,
        part,
        cols,
        cols,
        part,
        down,
        whole,
        whole,
        whole,
        cols,
        part,
        cols,
        cols,
        part,
        down,
        whole,
        whole,
        whole,
        cols,
        part,
        down,
        whole,
    )
    return jax.shard_map(per_device, mesh=fine, in_specs=placed, out_specs=given, check_vma=False)
```

```python
import functools

import jax
import jax.numpy as jnp
from jax import lax
from jax.experimental import pallas as pl
from jax.experimental.pallas import tpu as pltpu
from jax.sharding import Mesh, PartitionSpec as P

BF = jnp.bfloat16
F32 = jnp.float32
NEG = -1e30
SCALE = 0.125


def nn(a, b):
    return jnp.dot(a, b, preferred_element_type=F32)


def nt(a, b):
    return lax.dot_general(a, b, (((1,), (1,)), ((), ())), preferred_element_type=F32)


def tn(a, b):
    return lax.dot_general(a, b, (((0,), (0,)), ((), ())), preferred_element_type=F32)


def ring(n, k):
    return [(i, (i + k) % n) for i in range(n)]


def from_core(v):
    return lax.ppermute(v, "c", ring(2, 1))


def from_half(v):
    return lax.ppermute(v, ("zl", "zh"), [(i, 3 - i) for i in range(4)])


def gather_rel(v):
    return [v] + [lax.ppermute(v, "y", ring(4, 4 - r)) for r in range(1, 4)]


def scatter_rel(blocks):
    return [blocks[0]] + [lax.ppermute(blocks[r], "y", ring(4, r)) for r in range(1, 4)]


def exchange(v, axes):
    return lax.all_to_all(v, axes, 0, 0)


class Far:
    def __init__(self, array, start=0, rows=None, row=None, block=None):
        self.array = array
        self.row = row
        self.block = block
        self.start = start
        self.rows = array.shape[0] if rows is None else rows
        self.shape = (self.rows,) + array.shape[1:]
        if array.ndim == 4 and rows is not None:
            self.shape = (array.shape[0], rows, array.shape[3])
        elif array.ndim == 4:
            self.shape = array.shape
        if block is not None:
            self.array = array.reshape((array.shape[0] // block, block) + array.shape[1:])
            self.shape = (array.shape[0] // block,) + self.shape


def far(*arrays):
    return [Far(v) for v in arrays]


class Arriving:
    def __init__(self, ref, copy):
        self.ref = ref
        self.copy = copy
        self.shape = ref.shape

    def here(self):
        if self.copy is not None:
            self.copy.wait()
            self.copy = None
        return self.ref

    def __getitem__(self, index):
        return self.here()[index]


class Leaving:
    def __init__(self, ref, copy):
        self.ref = ref
        self.copy = copy
        self.started = False
        self.shape = ref.shape
        self.dtype = ref.dtype

    def __getitem__(self, index):
        return self.ref[index]

    def __setitem__(self, index, value):
        assert not self.started
        self.ref[index] = value

    @property
    def at(self):
        return self.ref.at

    def leave(self):
        if not self.started:
            self.started = True
            self.copy.start()


def leave(*refs):
    for ref in refs:
        ref.leave()


def whole_block(shape):
    return pl.BlockSpec(shape, lambda i: (0,) * len(shape), pipeline_mode=pl.Buffered(1))


def run(kernel, outs, scalars, inputs, scratch=(), vmem=60, lazy=False):
    body, us = kernel
    away = [isinstance(v, Far) for v in inputs]
    specs = [pl.BlockSpec(memory_space=pltpu.HBM) if a else whole_block(v.shape) for a, v in zip(away, inputs)]
    arrays = [v.array if a else v for a, v in zip(away, inputs)]
    staged = [pltpu.VMEM(v.shape, v.array.dtype) for a, v in zip(away, inputs) if a]
    shapes = [jax.ShapeDtypeStruct(s, d) for s, d in outs]
    back = [len(s) > 1 for s, _ in outs]
    held = [pltpu.VMEM(s, d) for (s, d), b in zip(outs, back) if b]
    scratch = list(scratch)

    def whole_body(sc, *refs):
        count = len(inputs)
        given, rest = list(refs[:count]), refs[count:]
        results, rest = list(rest[: len(outs)]), rest[len(outs) :]
        own, rest = rest[: len(scratch)], rest[len(scratch) :]
        kept, rest = rest[: len(held)], rest[len(held) :]
        leaving = []
        for i in range(len(outs)):
            if back[i]:
                n = len(leaving)
                leaving.append(Leaving(kept[n], pltpu.make_async_copy(kept[n], results[i], rest[-1].at[len(staged) + n])))
                results[i] = leaving[-1]
        copies = []
        for i, v in enumerate(inputs):
            if not away[i]:
                continue
            n = len(copies)
            source = given[i]
            if v.array.ndim == 4:
                if v.shape != v.array.shape:
                    source = given[i].at[:, 0, pl.ds(v.start, v.rows)]
            elif v.block is not None:
                source = given[i].at[:, pl.ds(v.start, v.rows)]
            elif v.row is None and v.shape != v.array.shape:
                source = given[i].at[pl.ds(v.start, v.rows)]
            elif v.row is not None:
                source = given[i].at[pl.ds(pl.multiple_of(sc[v.row] * v.rows, v.rows), v.rows)]
            copies.append(Arriving(rest[n], pltpu.make_async_copy(source, rest[n], rest[-1].at[n])))
            given[i] = copies[-1]
        for v in copies:
            v.copy.start()
        if not lazy:
            for v in copies:
                v.here()
        body(sc, *given, *results, *own)
        for v in copies:
            v.here()
        leave(*leaving)
        for v in leaving:
            v.copy.wait()

    scratch_shapes = scratch + held + staged + [pltpu.SemaphoreType.DMA((max(len(staged) + len(held), 1),))]
    return pl.pallas_call(
        whole_body,
        out_shape=shapes,
        in_specs=[pl.BlockSpec(memory_space=pltpu.SMEM)] + specs,
        out_specs=[
            pl.BlockSpec(memory_space=pltpu.HBM) if b else whole_block(s.shape) for b, s in zip(back, shapes)
        ],
        grid=(1,),
        scratch_shapes=scratch_shapes,
        compiler_params=pltpu.CompilerParams(vmem_limit_bytes=vmem * 2**20),
        cost_estimate=pl.CostEstimate(flops=int(us * 1.15e9), bytes_accessed=0, transcendentals=0),
    )(scalars, *arrays)


def rows_at(start, count):
    return pl.ds(pl.multiple_of(start, count), count)


def row(ref):
    return ref[...].reshape(1, -1)


def normal_of(v):
    center = v - jnp.mean(v, axis=-1, keepdims=True)
    inverse = lax.rsqrt(jnp.mean(center * center, axis=-1, keepdims=True) + 1e-05)
    return center * inverse, inverse


def norm_back(gradient, normal, inverse, gain):
    scaled = gradient * gain
    adjusted = (
        scaled
        - jnp.mean(scaled, axis=-1, keepdims=True)
        - normal * jnp.mean(scaled * normal, axis=-1, keepdims=True)
    )
    return adjusted * inverse


def col_sum(v):
    return jnp.sum(v, axis=0, keepdims=True)


def set_places(sc):
    c, zh = sc[1], sc[2]
    return [2 * zh + c, 2 * (1 - zh) + c, 2 * zh + 1 - c, 2 * (1 - zh) + 1 - c]


def head_masks(width=256):
    lane = lax.broadcasted_iota(jnp.int32, (1, width), 1) // 64
    return [lane == h for h in range(4)]


def scalar_kernel(ids, tgt_len, src_len, pair_ids, loss_weights, out):
    for i in range(3):
        out[i] = ids[i]
    out[3] = tgt_len[ids[2]]
    out[4] = src_len[ids[2]]
    out[5] = loss_weights[pair_ids[ids[2]]]
    out[6] = 0
    out[7] = 0


VECTORS = ("first_gain", "first_shift", "self_output_bias", "second_gain", "second_shift")
VECTORS += ("cross_output_bias", "third_gain", "third_shift", "ffn_out_bias")


def vector(vecs, name):
    i = VECTORS.index(name)
    return vecs[i : i + 1, :]


def pack_kernel(sc, q, k, v, cq, ck, cv, o, co, qb, vb, cqb, cvb, fb, *refs):
    vectors, (one, wow, vecs) = refs[: len(VECTORS)], refs[len(VECTORS) :]
    for i, m in enumerate((q, k, v)):
        one[i * 64 : (i + 1) * 64, :] = m[...]
    for i, m in enumerate((cq, ck, cv)):
        one[208 + i * 64 : 272 + i * 64, :] = m[...]
    vec = jnp.concatenate([row(qb), row(vb), row(cqb), row(cvb), row(fb)], axis=1)
    high = vec.astype(BF).astype(F32)
    both = jnp.concatenate([high, vec - high], axis=1)
    first = lax.broadcasted_iota(jnp.int32, (16, 1024), 0) == 0
    one[192:208, :] = jnp.where(first, both, 0.0).astype(BF)
    wow[0:64, :] = o[...]
    wow[64:128, :] = co[...]
    for i, v in enumerate(vectors):
        vecs[i : i + 1, :] = row(v)
    vecs[len(VECTORS) : 16, :] = jnp.zeros((16 - len(VECTORS), 1024), F32)


def pack_more_kernel(sc, fin, fout, out):
    out[0:256, :] = fin[...].astype(F32).T.astype(BF)
    out[256:512, :] = fout[...]


def qkv_kernel(sc, t0, t1, t2, t3, vecs, a0, a1, a2, a3, first, tok, q, kv, w, bias):
    gain, shift = vector(vecs, "first_gain"), vector(vecs, "first_shift")
    for r, t in enumerate((t0, t1, t2, t3)):
        place = rows_at(lax.rem(sc[0] + r, 4) * 128, 128)
        tok[place, :] = t[...]
        normal, _ = normal_of(t[...].astype(F32))
        first[place, :] = (normal * gain + shift).astype(BF)
    for part, place in zip((a0, a1, a2, a3), set_places(sc)):
        for m in range(3):
            w[rows_at(m * 256 + place * 64, 64), :] = part[m * 64 : (m + 1) * 64, :]
        vec = part[192:208, :].astype(F32)[0:1, :]
        bias[pl.ds(place, 1), :] = vec[:, :512] + vec[:, 512:]
    x = first[...]

    def bias_of(i):
        return jnp.concatenate([bias[h : h + 1, i * 64 : (i + 1) * 64] for h in range(4)], axis=1)

    leave(first, tok, w, bias)
    kv[:, 0:256] = nt(x, w[256:512, :]).astype(BF)
    kv[:, 256:512] = (nt(x, w[512:768, :]) + bias_of(1)).astype(BF)
    leave(kv)
    q[...] = (SCALE * (nt(x, w[0:256, :]) + bias_of(0))).astype(BF)


def source_kernel(sc, mem, a0, a1, a2, a3, bias, ckv, w, own):
    for part, place in zip((a0, a1, a2, a3), set_places(sc)):
        for m in range(3):
            w[rows_at(m * 256 + place * 64, 64), :] = part[m * 64 : (m + 1) * 64, :]
    vb = jnp.concatenate([bias[h : h + 1, 192:256] for h in range(4)], axis=1)
    ckv[:, 0:256] = nt(mem[...], w[256:512, :]).astype(BF)
    ckv[:, 256:512] = (nt(mem[...], w[512:768, :]) + vb).astype(BF)
    for j in range(4):
        own[j * 128 : (j + 1) * 128, :] = mem[rows_at((2 * j + sc[1]) * 128, 128), :]


def key_bias(core, length, axis):
    k = lax.broadcasted_iota(jnp.int32, (1, 512) if axis == 1 else (512, 1), axis)
    position = ((k >> 7) * 2 + core) * 128 + (k & 127)
    return jnp.where(position < length, 0.0, NEG)


def diagonal_bias(key_core, query_core, transposed):
    q = lax.broadcasted_iota(jnp.int32, (256, 256), 1 if transposed else 0)
    k = lax.broadcasted_iota(jnp.int32, (256, 256), 0 if transposed else 1)
    q = ((q >> 7) * 2 + query_core) * 128 + (q & 127)
    k = ((k >> 7) * 2 + key_core) * 128 + (k & 127)
    return jnp.where(k <= q, 0.0, NEG)


def attend(q_rows, sources, biases):
    masks = head_masks()
    lane = lax.broadcasted_iota(jnp.int32, (1, 128), 1)
    count = q_rows.shape[0]
    mixed = jnp.zeros((count, 256), F32)
    totals = jnp.zeros((count, 128), F32)
    for h in range(4):
        qh = jnp.where(masks[h], q_rows, jnp.zeros_like(q_rows))
        scores = [nt(qh, k) + b for (k, _), b in zip(sources, biases)]
        top = functools.reduce(jnp.maximum, [jnp.max(s, axis=1, keepdims=True) for s in scores])
        raised = [jnp.exp(s - top) for s in scores]
        total = sum(jnp.sum(p, axis=1, keepdims=True) for p in raised)
        out = sum(nn(p.astype(BF), v) for p, (_, v) in zip(raised, sources))
        mixed = jnp.where(masks[h], out * (1.0 / total), mixed)
        totals = jnp.where(lane == h, top + jnp.log(total), totals)
    return mixed, totals


def causal_biases(sc, axis):
    c, length = sc[1], sc[3]
    transposed = axis == 0
    return (
        [key_bias(c, length, axis), key_bias(1 - c, length, axis)],
        [diagonal_bias(c, c, transposed), diagonal_bias(1 - c, c, transposed)],
    )


def pair_bias(length_bias, diagonal, a, axis):
    if axis == 1:
        last = length_bias[:, a * 256 : (a + 1) * 256] + diagonal
        if a == 0:
            return last
        return jnp.concatenate([jnp.broadcast_to(length_bias[:, 0:256], (256, 256)), last], axis=1)
    last = length_bias[a * 256 : (a + 1) * 256, :] + diagonal
    if a == 0:
        return last
    return jnp.concatenate([jnp.broadcast_to(length_bias[0:256, :], (256, 256)), last], axis=0)


def self_forward_kernel(sc, q, kvo, kvs, mixed, totals, stat):
    lengths, diagonals = causal_biases(sc, 1)
    for a in range(2):
        n = (a + 1) * 256
        sources = [(kvo[0:n, 0:256], kvo[0:n, 256:512]), (kvs[0:n, 0:256], kvs[0:n, 256:512])]
        biases = [pair_bias(lengths[i], diagonals[i], a, 1) for i in range(2)]
        out, total = attend(q[a * 256 : (a + 1) * 256, :], sources, biases)
        mixed[a * 256 : (a + 1) * 256, :] = out.astype(BF)
        stat[a * 256 : (a + 1) * 256, :] = total
    totals[...] = stat[...].T[0:8, :]


def cross_forward_kernel(sc, q, ckv, mixed, totals, stat):
    key = lax.broadcasted_iota(jnp.int32, (1, 1024), 1)
    bias = jnp.where(key < sc[4], 0.0, NEG)
    for a in range(2):
        out, total = attend(q[a * 256 : (a + 1) * 256, :], [(ckv[:, 0:256], ckv[:, 256:512])], [bias])
        mixed[a * 256 : (a + 1) * 256, :] = out.astype(BF)
        stat[a * 256 : (a + 1) * 256, :] = total
    totals[...] = stat[...].T[0:8, :]


def chip_rows(sc, whole, order):
    for r in range(4):
        chip = lax.rem(sc[0] + r, 4)
        for z in range(2):
            for core in range(2):
                place = r * 256 + z * 128 + core * 64
                order[place : place + 64, :] = whole[z * 8 + chip * 2 + core]


def head_rows(sc, whole, order):
    for r in range(4):
        chip = lax.rem(sc[0] + r, 4)
        for z in range(2):
            order[r * 256 + z * 128 : r * 256 + (z + 1) * 128, :] = whole[rows_at(z * 512 + chip * 128, 128), :]


def second_kernel(
    sc, m0, m1, m2, m3, wo, tok, vecs, cw, bias, second, resid, cq, wo_own, order
):
    ob, gain, shift = (vector(vecs, n) for n in ("self_output_bias", "second_gain", "second_shift"))
    chip_rows(sc, wo, order)
    wo_own[...] = order[0:256, :]
    resid[...] = nn(jnp.concatenate([m0[...], m1[...], m2[...], m3[...]], axis=1), order[...])
    for j in range(4):
        place = slice(j * 128, (j + 1) * 128)
        v = tok[place, :].astype(F32) + (resid[place, :] + ob)
        resid[place, :] = v
        normal, _ = normal_of(v)
        second[place, :] = (normal * gain + shift).astype(BF)
    leave(second, resid, wo_own)
    qb = jnp.concatenate([bias[h : h + 1, 128:192] for h in range(4)], axis=1)
    cq[...] = (SCALE * (nt(second[...], cw[0:256, :]) + qb)).astype(BF)


def upstream_kernel(sc, c0, c1, c2, c3, w0, w1, w2, w3, og, up):
    weight = 0.5 * sc[5].astype(F32)
    for r, t in enumerate((c0, c1, c2, c3)):
        chip = lax.rem(sc[0] + r, 4)
        position = (2 * chip + sc[1]) * 128 + lax.broadcasted_iota(jnp.int32, (128, 1), 0)
        og[rows_at(chip * 128, 128), :] = (t[...].astype(F32) * jnp.where(position < sc[3], weight, 0.0)).astype(BF)
    for s, w in enumerate((w0, w1, w2, w3)):
        up[:, s * 256 : (s + 1) * 256] = nt(og[...], w[...]).astype(BF)


def ffn_kernel(
    sc, m0, m1, m2, m3, wco, resid, vecs, up, w0, w1, w2, w3, bias,
    third, hidden, pre, back0, back1, back2, back3, own, wco_own, order, work,
):
    y = sc[0]
    ob, gain, shift = (vector(vecs, n) for n in ("cross_output_bias", "third_gain", "third_shift"))
    chip_rows(sc, wco, order)
    wco_own[...] = order[0:256, :]
    work[...] = nn(jnp.concatenate([m0[...], m1[...], m2[...], m3[...]], axis=1), order[...])
    for s, w in enumerate((w0, w1, w2, w3)):
        order[s * 256 : (s + 1) * 256, :] = w[...]
    for j in range(4):
        place = slice(j * 128, (j + 1) * 128)
        v = resid[place, :] + (work[place, :] + ob)
        work[place, :] = v
        normal, _ = normal_of(v)
        third[place, :] = (normal * gain + shift).astype(BF)
    own[...] = work[rows_at(y * 128, 128), :]
    leave(third, own, wco_own)
    places = set_places(sc)
    for s in range(4):
        cols = slice(s * 256, (s + 1) * 256)
        u = nt(third[...], order[cols, :]) + bias[pl.ds(places[s], 1), 256:512]
        square = u * u
        t = jnp.tanh(0.7978845608028654 * (u + 0.044715 * (square * u)))
        hidden[:, cols] = (0.5 * u * (1.0 + t)).astype(BF)
        slope = 0.5 * (1.0 + t) + 0.5 * u * (1.0 - t * t) * (0.7978845608028654 * (1.0 + 0.134145 * square))
        pre[:, cols] = (up[:, cols].astype(F32) * slope).astype(BF)
    leave(hidden, pre)
    store_rel(sc, nn(pre[...], order[...]), work, (back0, back1, back2, back3))


def store_rel(sc, value, work, outs):
    work[...] = value
    for r, out in enumerate(outs):
        out[...] = work[rows_at(lax.rem(sc[0] + r, 4) * 128, 128), :].astype(BF)


def total_of(parts):
    p = [v[...].astype(F32) for v in parts]
    return (p[0] + p[1]) + (p[2] + p[3])


def late_rows_kernel(sc, p0, p1, p2, p3, own, vecs, out, mem):
    total = total_of((p0, p1, p2, p3))
    out[...] = (own[...] + (total[0:128, :] + vector(vecs, "ffn_out_bias"))).astype(BF)
    mem[...] = total[128:256, :]


def split_rows(values):
    high = values.astype(BF).astype(F32)
    return jnp.concatenate([high, values - high, jnp.zeros((12, values.shape[1]), F32)], axis=0).astype(BF)


def joined_rows(block):
    f = block.astype(F32)
    return f[0:2, :] + f[2:4, :]


def third_grad_kernel(sc, p0, p1, p2, p3, own, cot, vecs, grad, low):
    position = (2 * sc[0] + sc[1]) * 128 + lax.broadcasted_iota(jnp.int32, (128, 1), 0)
    og = cot[...].astype(F32) * jnp.where(position < sc[3], 0.5 * sc[5].astype(F32), 0.0)
    back = total_of((p0, p1, p2, p3))
    normal, inverse = normal_of(own[...])
    total = og + norm_back(back, normal, inverse, vector(vecs, "third_gain"))
    grad[...] = total
    low[0:128, :] = total.astype(BF)
    low[128:144, :] = split_rows(jnp.concatenate([col_sum(back * normal), col_sum(back)], axis=0))


def masked_stack(v, stack):
    masks = head_masks()
    for a in range(2):
        rows = v[a * 256 : (a + 1) * 256, :]
        for h in range(4):
            stack[a, h * 256 : (h + 1) * 256, :] = jnp.where(masks[h], rows, jnp.zeros_like(rows))


def delta_of(mixed, grad):
    head = lax.broadcasted_iota(jnp.int32, (8, 256), 0)
    lane = lax.broadcasted_iota(jnp.int32, (8, 256), 1) // 64
    ones = jnp.where(head == lane, 1.0, 0.0)
    product = mixed.astype(F32) * grad.astype(F32)
    return lax.dot_general(
        ones, product, (((1,), (1,)), ((), ())), preferred_element_type=F32, precision=lax.Precision.HIGHEST
    )


def pair_backward(a, q_stack, g_stack, totals, delta, keys, values, bias, probs, scores):
    masks = head_masks()
    cols = slice(a * 256, (a + 1) * 256)
    dq = jnp.zeros((256, 256), F32)
    for h in range(4):
        place = slice(h * 256, (h + 1) * 256)
        s = nt(keys, q_stack[a, place, :]) + bias
        p = jnp.exp(s - totals[h : h + 1, cols])
        ds = (p * (nt(values, g_stack[a, place, :]) - delta[h : h + 1, cols])).astype(BF)
        probs[:, place] = p.astype(BF)
        scores[:, place] = ds
        dq = jnp.where(masks[h], tn(ds, keys), dq)
    return dq


def cross_backward_kernel(
    sc, t0, t1, t2, t3, wco, cq, ckv, mixed, totals, og, tg, dq, own, other, vec,
    q_stack, g_stack, probs, scores, delta, part,
):
    norm_sums = jnp.zeros((2, 1024), F32)
    for r, t in enumerate((t0, t1, t2, t3)):
        tg[rows_at(lax.rem(sc[0] + r, 4) * 128, 128), :] = t[0:128, :]
        norm_sums = norm_sums + joined_rows(t[128:144, :])
    vec[0:2, :] = norm_sums
    vec[2:3, :] = col_sum(og[...].astype(F32))
    vec[3:4, :] = col_sum(tg[...].astype(F32))
    vec[4:8, :] = jnp.zeros((4, 1024), F32)
    leave(tg, vec)
    g = nt(tg[...], wco[...]).astype(BF)
    delta[...] = delta_of(mixed[...], g)
    masked_stack(g, g_stack)
    masked_stack(cq[...], q_stack)
    key = lax.broadcasted_iota(jnp.int32, (1024, 1), 0)
    bias = jnp.where(key < sc[4], 0.0, NEG)
    for a in range(2):
        grad = pair_backward(
            a, q_stack, g_stack, totals, delta, ckv[:, 0:256], ckv[:, 256:512], bias, probs.at[a], scores.at[a]
        )
        dq[a * 256 : (a + 1) * 256, :] = grad.astype(BF)
    leave(dq)
    part[:, 0:256] = nn(scores[0], q_stack[0]) + nn(scores[1], q_stack[1])
    part[:, 256:512] = nn(probs[0], g_stack[0]) + nn(probs[1], g_stack[1])
    for j in range(4):
        place = slice(j * 128, (j + 1) * 128)
        own[place, :] = part[rows_at((2 * j + sc[1]) * 128, 128), :]
        other[place, :] = part[rows_at((2 * j + 1 - sc[1]) * 128, 128), :].astype(BF)


def second_grad_kernel(
    sc, d0, d1, d2, d3, whole, resid, vecs, tg, tg_own, wo,
    low, grad_own, g, vec, order, work,
):
    gain = vector(vecs, "second_gain")
    head_rows(sc, whole, order)
    work[...] = nn(jnp.concatenate([d0[...], d1[...], d2[...], d3[...]], axis=1), order[...])
    sums = [jnp.zeros((1, 1024), F32)] * 3
    for j in range(4):
        place = slice(j * 128, (j + 1) * 128)
        normal, inverse = normal_of(resid[place, :])
        back = SCALE * work[place, :]
        v = norm_back(back, normal, inverse, gain)
        work[place, :] = v
        rounded = (tg[place, :].astype(F32) + v).astype(BF)
        low[place, :] = rounded
        for i, add in enumerate((back * normal, back, rounded.astype(F32))):
            sums[i] = sums[i] + col_sum(add)
    leave(low)
    g[...] = nt(low[...], wo[...]).astype(BF)
    leave(g)
    grad_own[...] = tg_own[...] + work[rows_at(sc[0] * 128, 128), :]
    vec[...] = jnp.concatenate(sums + [jnp.zeros((5, 1024), F32)], axis=0)


def self_backward_kernel(
    sc, g, q, kvo, kvs, mixed, totals, dq, own, other, q_stack, g_stack, p0, s0, p1, s1, delta
):
    delta[...] = delta_of(mixed[...], g[...])
    masked_stack(g[...], g_stack)
    masked_stack(q[...], q_stack)
    lengths, diagonals = causal_biases(sc, 0)
    for a in range(2):
        n = (a + 1) * 256
        probs, scores = ((p0, s0), (p1, s1))[a]
        grad = jnp.zeros((256, 256), F32)
        for i, kv in enumerate((kvo, kvs)):
            bias = pair_bias(lengths[i], diagonals[i], a, 0)
            grad = grad + pair_backward(
                a, q_stack, g_stack, totals, delta, kv[0:n, 0:256], kv[0:n, 256:512], bias, probs.at[i], scores.at[i]
            )
        dq[a * 256 : (a + 1) * 256, :] = grad.astype(BF)
    leave(dq)
    for i, out in ((1, other), (0, own)):
        kind = out.dtype
        for cols, first, second, stack in (
            (slice(0, 256), s0, s1, q_stack),
            (slice(256, 512), p0, p1, g_stack),
        ):
            out[0:256, cols] = (nn(first[i], stack[0]) + nn(second[i, 0:256, :], stack[1])).astype(kind)
            out[256:512, cols] = nn(second[i, 256:512, :], stack[1]).astype(kind)
        leave(out)


def first_back_kernel(sc, dq, dkv, w, vec, got, b0, b1, b2, b3, work):
    part = SCALE * nn(dq[...], w[0:256, :]) + nn(dkv[:, 0:256], w[256:512, :]) + nn(dkv[:, 256:512], w[512:768, :])
    store_rel(sc, part, work, [b.at[0:128] for b in (b0, b1, b2, b3)])
    other = jnp.concatenate([got[i].astype(F32) for i in range(8)], axis=1)
    rows = split_rows(vec[0:2, :] + other[4:6, :] + other[6:8, :])
    for b in (b0, b1, b2, b3):
        b[128:144, :] = rows


def tokens_grad_kernel(sc, p0, p1, p2, p3, tokens, vecs, grad, out, vec):
    parts = (p0, p1, p2, p3)
    vec[...] = split_rows(sum(joined_rows(p[128:144, :]) for p in parts))
    normal, inverse = normal_of(tokens[...].astype(F32))
    out[...] = grad[...] + norm_back(
        total_of([p[0:128, :] for p in parts]), normal, inverse, vector(vecs, "first_gain")
    )


def memory_back_kernel(sc, own, other, w, hidden, w0, w1, w2, w3, grad, b0, b1, b2, b3, order, work):
    outs = (b0, b1, b2, b3)
    for s, part in enumerate((w0, w1, w2, w3)):
        order[s * 256 : (s + 1) * 256, :] = part[...]
    store_rel(sc, nn(hidden[...], order[...]), work, [b.at[0:128] for b in outs])
    grad[...] = (own[...] + other[...].astype(F32)).astype(BF)
    leave(grad)
    value = nn(grad[:, 0:256], w[0:256, :]) + nn(grad[:, 256:512], w[256:512, :])
    store_rel(sc, value, work, [b.at[128:256] for b in outs])


def core_columns(sc, v, core):
    f = v.astype(F32)
    low = jnp.concatenate([f[:, 0:64], f[:, 128:192]], axis=1)
    high = jnp.concatenate([f[:, 64:128], f[:, 192:256]], axis=1)
    return jnp.where(core == 0, low, high).astype(v.dtype)


def store_pieces(out, z, start, block):
    for i in range(8):
        out[i, z, start : start + block.shape[0], :] = block[:, i * 128 : (i + 1) * 128].astype(BF)


def store_bias(out, z, start, values, vectors=()):
    wide = jnp.concatenate([values, jnp.zeros((1, 1024 - values.shape[1]), F32)], axis=1)
    rows = [wide] + list(vectors)
    rows.append(jnp.zeros((16 - sum(v.shape[0] for v in rows), 1024), F32))
    store_pieces(out, z, start, jnp.concatenate(rows, axis=0))


def ffn_weight_kernel(sc, pre, third, hidden, og, keep, send):
    zh = sc[2]
    for s in range(4):
        out = keep if s < 2 else send
        z = zh if s % 2 == 0 else 1 - zh
        cols = slice(s * 256, (s + 1) * 256)
        store_pieces(out, z, 0, tn(pre[:, cols], third[...]))
        store_pieces(out, z, 256, tn(hidden[:, cols], og[...]))
        store_bias(out, z, 512, col_sum(pre[:, cols].astype(F32)))


def cross_weight_kernel(sc, mixed, tg, dq, second, dkv, mem, vec, keep, send):
    for out, core in ((keep, sc[1]), (send, 1 - sc[1])):
        dqc = core_columns(sc, dq[...], core)
        dvc = core_columns(sc, dkv[:, 256:512], core)
        o = tn(core_columns(sc, mixed[...], core), tg[...])
        q = SCALE * tn(dqc, second[...])
        k = tn(core_columns(sc, dkv[:, 0:256], core), mem[...])
        v = tn(dvc, mem[...])
        qb = SCALE * col_sum(dqc.astype(F32))
        vb = col_sum(dvc.astype(F32))
        for z in range(2):
            place = slice(z * 64, (z + 1) * 64)
            for i, m in enumerate((o, q, k, v)):
                store_pieces(out, z, i * 64, m[place, :])
            store_bias(out, z, 256, jnp.concatenate([qb[:, place], vb[:, place]], axis=1), [vec[0:4, :]])


def self_weight_kernel(sc, dq, own, other, tok, w, mixed, sg, vecs, vec2, dkv, keep, send, vec, normal, product):
    gain, shift = vector(vecs, "first_gain"), vector(vecs, "first_shift")
    dkv[...] = (own[...] + other[...].astype(F32)).astype(BF)
    leave(dkv)
    for j in range(4):
        place = slice(j * 128, (j + 1) * 128)
        normal[place, :] = normal_of(tok[place, :].astype(F32))[0].astype(BF)
    ones = jnp.ones((8, 512), BF)
    gain_sum = jnp.zeros((1, 1024), F32)
    shift_sum = jnp.zeros((1, 1024), F32)
    q_bias = v_bias = None
    for m, (grad, factor) in enumerate(((dq[...], SCALE), (dkv[:, 0:256], 1.0), (dkv[:, 256:512], 1.0))):
        sums = factor * tn(grad, ones.T)[:, 0:1]
        product[...] = factor * tn(grad, normal[...])
        weight = w[m * 256 : (m + 1) * 256, :].astype(F32)
        gain_sum = gain_sum + col_sum(weight * product[...])
        shift_sum = shift_sum + col_sum(weight * sums)
        total = product[...] * gain + sums * shift
        product[...] = total
        for z in range(2):
            for out, core in ((keep, sc[1]), (send, 1 - sc[1])):
                store_pieces(out, z, (m + 1) * 64, product[rows_at((2 * z + core) * 64, 64), :])
        if m != 1:
            flat = factor * nn(ones, grad)[0:1, :]
            if m == 0:
                q_bias = flat
            else:
                v_bias = flat
    sums_rows = split_rows(jnp.concatenate([gain_sum, shift_sum], axis=0))[0:4, :].astype(F32)
    product[...] = tn(mixed[...], sg[...])
    for z in range(2):
        for out, core in ((keep, sc[1]), (send, 1 - sc[1])):
            store_pieces(out, z, 0, product[rows_at((2 * z + core) * 64, 64), :])
            sides = [
                jnp.concatenate([v[:, s * 64 : (s + 1) * 64] for v in (q_bias, v_bias)], axis=1)
                for s in (2 * z, 2 * z + 1)
            ]
            store_bias(out, z, 256, jnp.where(core == 0, sides[0], sides[1]), [vec2[0:3, :], sums_rows])
    vec[...] = jnp.concatenate([gain_sum, shift_sum, jnp.zeros((6, 1024), F32)], axis=0)


def add_kernel(sc, *refs):
    out, start = refs[-1], 0
    for a, b in zip(refs[:-1:2], refs[1:-1:2]):
        rows = a.shape[2]
        for i in range(8):
            out[i, :, start : start + rows, :] = (a[i].astype(F32) + b[i].astype(F32)).astype(BF)
        start += rows


def piece_sum(got):
    total = got[0].astype(F32)
    for i in range(1, 16):
        total = total + got[i].astype(F32)
    return total.astype(BF)


def spread_kernel(sc, got, out):
    total = piece_sum(got)
    for i in range(8):
        out[i] = total


def spread_more_kernel(sc, got, vec, half, out):
    total = piece_sum(got)
    rows = split_rows(joined_rows(vec[...]) + joined_rows(half[...])).astype(F32)[0:4, :]
    rows = jnp.concatenate([rows[:, i * 128 : (i + 1) * 128] for i in range(8)], axis=0).astype(BF)
    for i in range(8):
        out[i, 0:544, :] = total
        out[i, 544:576, :] = rows


def ffn_result_kernel(sc, got, fin, fout, fb):
    for i in range(8):
        fin[i * 128 : (i + 1) * 128, :] = got[i, 0:256, :].astype(F32).T
        fout[:, i * 128 : (i + 1) * 128] = got[i, 256:512, :].astype(F32)
    fb[...] = jnp.concatenate([got[i, 512:528, :].astype(F32)[0:1, :] for i in range(2)], axis=1).reshape(256)


def heads_result_kernel(sc, got, *outs):
    heads_result(3, 0, got, *outs[:9])
    heads_result(4, 272, got, *outs[9:19])
    rows = sum(got[i, 544:576, :].astype(F32) for i in range(8))
    for k in range(2):
        both = [rows[i * 4 + k : i * 4 + k + 1, :] + rows[i * 4 + k + 2 : i * 4 + k + 3, :] for i in range(8)]
        outs[19 + k][...] = jnp.concatenate(both, axis=1).reshape(1024)


def heads_result(count, start, got, o, q, k, v, qb, vb, *vectors):
    for m, out in enumerate((o, q, k, v)):
        for i in range(8):
            out[:, i * 128 : (i + 1) * 128] = got[i, start + m * 64 : start + (m + 1) * 64, :].astype(F32)
        leave(out)
    rows = jnp.concatenate([got[i, start + 256 : start + 272, :].astype(F32) for i in range(8)], axis=1)
    qb[...] = rows[0:1, 0:64].reshape(64)
    vb[...] = rows[0:1, 64:128].reshape(64)
    for i in range(count):
        vectors[i][...] = rows[i + 1 : i + 2, :].reshape(1024)


def core_sum(sc, *pairs):
    rows = sum(keep.shape[2] for keep, _ in pairs)
    return run((add_kernel, 4.8), [((8, 2, rows, 128), BF)], sc, far(*[v for pair in pairs for v in pair]))[0]


def pieces(both):
    return exchange(both.reshape((16,) + both.shape[2:]), ("x", "zl", "zh"))


def per_device(
    tokens,
    memory,
    cotangent,
    tgt_len,
    src_len,
    pair_ids,
    loss_weights,
    first_gain,
    first_shift,
    self_query,
    self_query_bias,
    self_key,
    self_value,
    self_value_bias,
    self_output,
    self_output_bias,
    second_gain,
    second_shift,
    cross_query,
    cross_query_bias,
    cross_key,
    cross_value,
    cross_value_bias,
    cross_output,
    cross_output_bias,
    third_gain,
    third_shift,
    ffn_in,
    ffn_in_bias,
    ffn_out,
    ffn_out_bias,
):
    ids = jnp.stack([lax.axis_index("y"), lax.axis_index("c"), lax.axis_index("zh")]).astype(jnp.int32)
    sc = pl.pallas_call(
        scalar_kernel,
        out_shape=jax.ShapeDtypeStruct((8,), jnp.int32),
        in_specs=[pl.BlockSpec(memory_space=pltpu.SMEM)] * 5,
        out_specs=pl.BlockSpec(memory_space=pltpu.SMEM),
    )(ids, tgt_len, src_len, pair_ids, loss_weights)

    def after(v, *others):
        return lax.optimization_barrier((v,) + others)[0]

    tok_blocks = gather_rel(tokens)
    given = {
        "first_gain": first_gain,
        "first_shift": first_shift,
        "self_output_bias": self_output_bias,
        "second_gain": second_gain,
        "second_shift": second_shift,
        "cross_output_bias": cross_output_bias,
        "third_gain": third_gain,
        "third_shift": third_shift,
        "ffn_out_bias": ffn_out_bias,
    }
    one, wow, vecs = run(
        (pack_kernel, 3.3),
        [((400, 1024), BF), ((128, 1024), BF), ((16, 1024), F32)],
        sc,
        far(self_query.T, self_key.T, self_value.T, cross_query.T, cross_key.T, cross_value.T)
        + far(self_output, cross_output)
        + [self_query_bias, self_value_bias, cross_query_bias, cross_value_bias, ffn_in_bias]
        + [given[n] for n in VECTORS],
        vmem=60,
    )
    one_half = from_half(one)
    one_core = from_core(one)
    (more,) = run(
        (pack_more_kernel, 3),
        [((512, 1024), BF)],
        sc,
        far(ffn_in, ffn_out),
        vmem=60,
    )
    whole_wow = lax.all_gather(wow, ("zh", "y", "c"), axis=0, tiled=True)
    whole_cross_query = lax.all_gather(after(cross_query.T, whole_wow), ("zh", "y", "c"), axis=0, tiled=True)
    one_core_half = from_core(after(one_half, *tok_blocks))

    def one_parts(start, rows):
        return [Far(v, start, rows) for v in (one, one_half, one_core, one_core_half)]

    first, tok, q, kv, w, bias = run(
        (qkv_kernel, 5.3),
        [((512, 1024), BF), ((512, 1024), BF), ((512, 256), BF), ((512, 512), BF), ((768, 1024), BF), ((4, 512), F32)],
        sc,
        far(*tok_blocks, vecs) + one_parts(0, 208),
        lazy=True,
    )
    kvs = from_core(kv)
    more_half = from_half(after(more, first))
    cot_blocks = gather_rel(after(cotangent, first))
    self_mixed, self_totals = run(
        (self_forward_kernel, 5.8),
        [((512, 256), BF), ((8, 512), F32)],
        sc,
        far(q, kv, kvs),
        [pltpu.VMEM((512, 128), F32)],
    )
    mixed_blocks = gather_rel(self_mixed)
    more_core = from_core(after(more, self_mixed))

    ckv, cw, mem_own = run(
        (source_kernel, 6),
        [((1024, 512), BF), ((768, 1024), BF), ((512, 1024), BF)],
        sc,
        [Far(memory, 0, 1024, row=2)] + one_parts(208, 192) + [Far(bias)],
    )
    second, resid, cq, wo_own = run(
        (second_kernel, 8),
        [((512, 1024), BF), ((512, 1024), F32), ((512, 256), BF), ((256, 1024), BF)],
        sc,
        far(*mixed_blocks) + [Far(whole_wow, 0, 64, block=128)] + far(tok, vecs) + [Far(cw, 0, 256), Far(bias)],
        [pltpu.VMEM((1024, 1024), BF)],
        lazy=True,
    )
    more_core_half = from_core(after(more_half, cq))

    def more_parts(start, rows):
        return [Far(v, start, rows) for v in (more, more_half, more_core, more_core_half)]

    cross_mixed, cross_totals = run(
        (cross_forward_kernel, 6),
        [((512, 256), BF), ((8, 512), F32)],
        sc,
        far(cq, ckv),
        [pltpu.VMEM((512, 128), F32)],
    )
    cross_blocks = gather_rel(cross_mixed)

    og, up = run(
        (upstream_kernel, 5),
        [((512, 1024), BF), ((512, 1024), BF)],
        sc,
        far(*cot_blocks) + more_parts(256, 256),
    )
    rows_out = [((128, 1024), BF)] * 4
    third, hidden, pre, b0, b1, b2, b3, resid_own, wco_own = run(
        (ffn_kernel, 11.5),
        [((512, 1024), BF)] * 3 + rows_out + [((128, 1024), F32), ((256, 1024), BF)],
        sc,
        far(*cross_blocks) + [Far(whole_wow, 64, 64, block=128)] + far(resid, vecs, up) + more_parts(0, 256) + [Far(bias)],
        [pltpu.VMEM((1024, 1024), BF), pltpu.VMEM((512, 1024), F32)],
    )
    third_parts = scatter_rel([b0, b1, b2, b3])
    ffn_keep, ffn_send = run(
        (ffn_weight_kernel, 7),
        [((8, 2, 528, 128), BF)] * 2,
        sc,
        far(pre, third, hidden, og),
        lazy=True,
    )
    third_grad, third_low = run(
        (third_grad_kernel, 3.8),
        [((128, 1024), F32), ((144, 1024), BF)],
        sc,
        far(*third_parts, resid_own, cotangent, vecs),
    )
    tg_blocks = gather_rel(third_low)
    ffn_both = core_sum(sc, (ffn_keep, from_core(ffn_send)))

    tg, cdq, ckv_own, ckv_other, third_vec = run(
        (cross_backward_kernel, 13),
        [((512, 1024), BF), ((512, 256), BF), ((512, 512), F32), ((512, 512), BF), ((8, 1024), F32)],
        sc,
        far(*tg_blocks, wco_own, cq, ckv, cross_mixed, cross_totals, og),
        [
            pltpu.VMEM((2, 1024, 256), BF),
            pltpu.VMEM((2, 1024, 256), BF),
            pltpu.VMEM((2, 1024, 1024), BF),
            pltpu.VMEM((2, 1024, 1024), BF),
            pltpu.VMEM((8, 512), F32),
            pltpu.VMEM((1024, 512), F32),
        ],
    )
    cdq_blocks = gather_rel(cdq)
    ckv_got = from_core(ckv_other)
    ckv_grad, *late_part = run(
        (memory_back_kernel, 7.5),
        [((512, 512), BF)] + [((256, 1024), BF)] * 4,
        sc,
        far(ckv_own, ckv_got) + [Far(cw, 256, 512), Far(hidden)] + more_parts(256, 256),
        [pltpu.VMEM((1024, 1024), BF), pltpu.VMEM((512, 1024), F32)],
    )
    cross_keep, cross_send = run(
        (cross_weight_kernel, 6.3),
        [((8, 2, 272, 128), BF)] * 2,
        sc,
        far(cross_mixed, tg, cdq, second, ckv_grad, mem_own, third_vec),
    )
    cross_recv = from_core(cross_send)
    (ffn_copies,) = run((spread_kernel, 3.7), [((8, 528, 128), BF)], sc, far(pieces(ffn_both)))
    sg, second_grad, self_grad, second_vec = run(
        (second_grad_kernel, 8.5),
        [((512, 1024), BF), ((128, 1024), F32), ((512, 256), BF), ((8, 1024), F32)],
        sc,
        far(*cdq_blocks, whole_cross_query, resid, vecs, tg, third_grad, after(wo_own, cross_keep, ffn_both)),
        [pltpu.VMEM((1024, 1024), BF), pltpu.VMEM((512, 1024), F32)],
    )
    late_part = lax.optimization_barrier(tuple(late_part) + tuple(cdq_blocks))[:4]
    late_parts = scatter_rel(late_part)

    dq, kv_own, kv_other = run(
        (self_backward_kernel, 12),
        [((512, 256), BF), ((512, 512), F32), ((512, 512), BF)],
        sc,
        far(self_grad, q, kv, kvs, self_mixed, self_totals),
        [
            pltpu.VMEM((2, 1024, 256), BF),
            pltpu.VMEM((2, 1024, 256), BF),
            pltpu.VMEM((2, 256, 1024), BF),
            pltpu.VMEM((2, 256, 1024), BF),
            pltpu.VMEM((2, 512, 1024), BF),
            pltpu.VMEM((2, 512, 1024), BF),
            pltpu.VMEM((8, 512), F32),
        ],
    )
    kv_got = from_core(kv_other)
    block_out, memory_grad = run(
        (late_rows_kernel, 3.5), [((128, 1024), BF), ((128, 1024), F32)], sc, far(*late_parts, resid_own, vecs)
    )
    ffn_got = exchange(ffn_copies, ("x", "zl"))
    dkv, self_keep, self_send, first_vec = run(
        (self_weight_kernel, 8),
        [((512, 512), BF), ((8, 2, 272, 128), BF), ((8, 2, 272, 128), BF), ((8, 1024), F32)],
        sc,
        far(dq, kv_own, kv_got, after(tok, block_out, ffn_got), w, self_mixed, sg, vecs, second_vec),
        [pltpu.VMEM((512, 1024), BF), pltpu.VMEM((256, 1024), F32)],
    )
    self_recv = from_core(self_send)
    first_part = run(
        (first_back_kernel, 5),
        [((144, 1024), BF)] * 4,
        sc,
        far(dq, dkv, w, first_vec) + [Far(self_recv, 256, 16)],
        [pltpu.VMEM((512, 1024), F32)],
    )
    first_parts = scatter_rel(first_part)
    (self_both,) = run(
        (add_kernel, 5),
        [((8, 2, 544, 128), BF)],
        sc,
        far(after(self_keep, ffn_got), self_recv, cross_keep, cross_recv),
    )
    tokens_grad, vec_own = run(
        (tokens_grad_kernel, 3.5), [((128, 1024), F32), ((16, 1024), BF)], sc, far(*first_parts, tokens, vecs, second_grad)
    )
    ffn_in_grad, ffn_out_grad, ffn_in_bias_grad = run(
        (ffn_result_kernel, 4), [((1024, 256), F32), ((256, 1024), F32), ((256,), F32)], sc, far(ffn_got)
    )
    heads_out = [((64, 1024), F32)] * 4 + [((64,), F32)] * 2
    self_pieces = after(pieces(self_both), tokens_grad, ffn_in_grad)
    (self_copies,) = run(
        (spread_more_kernel, 4), [((8, 576, 128), BF)], sc, far(self_pieces, vec_own, from_half(vec_own))
    )
    self_got = exchange(self_copies, ("x", "zl"))
    heads_out = heads_out + [((1024,), F32)] * 3 + heads_out + [((1024,), F32)] * 6
    outs = run((heads_result_kernel, 4), heads_out, sc, far(self_got))
    self_out, cross_out = outs[:9], outs[9:]
    return (
        block_out,
        tokens_grad,
        memory_grad,
        cross_out[10],
        cross_out[11],
        self_out[1].T,
        self_out[4],
        self_out[2].T,
        self_out[3].T,
        self_out[5],
        self_out[0],
        self_out[8],
        self_out[6],
        self_out[7],
        cross_out[1].T,
        cross_out[4],
        cross_out[2].T,
        cross_out[3].T,
        cross_out[5],
        cross_out[0],
        cross_out[9],
        cross_out[6],
        cross_out[7],
        ffn_in_grad,
        ffn_in_bias_grad,
        ffn_out_grad,
        cross_out[8],
    )


def solution(mesh):
    fine = Mesh(mesh.devices.reshape(4, 2, 2, 4, 2), ("x", "zl", "zh", "y", "c"))
    dp = ("x", "zl")
    mp = ("zh", "y", "c")
    rows, cols, part, down, whole = P(dp + mp, None), P(None, mp), P(mp), P(mp, None), P()
    placed = (rows, P(dp, None), rows, P(dp), P(dp), P(dp), whole, whole, whole)
    placed += (cols, part, cols, cols, part, down, whole, whole, whole)
    placed += (cols, part, cols, cols, part, down, whole, whole, whole)
    placed += (cols, part, down, whole)
    attention = (cols, part, cols, cols, part, down, whole)
    given = (rows, rows, rows, whole, whole) + attention + (whole, whole) + attention + (whole, whole)
    given += (cols, part, down, whole)
    return jax.shard_map(per_device, mesh=fine, in_specs=placed, out_specs=given, check_vma=False)
```

```python
import functools

import jax
import jax.numpy as jnp
from jax import lax
from jax.experimental import pallas as pl
from jax.experimental.pallas import tpu as pltpu
from jax.sharding import Mesh, PartitionSpec as P

BF = jnp.bfloat16
F32 = jnp.float32
NEG = -1e30
SCALE = 0.125


def nn(a, b):
    return jnp.dot(a, b, preferred_element_type=F32)


def nt(a, b):
    return lax.dot_general(a, b, (((1,), (1,)), ((), ())), preferred_element_type=F32)


def tn(a, b):
    return lax.dot_general(a, b, (((0,), (0,)), ((), ())), preferred_element_type=F32)


def ring(n, k):
    return [(i, (i + k) % n) for i in range(n)]


def from_core(v):
    return lax.ppermute(v, "c", ring(2, 1))


def from_half(v):
    return lax.ppermute(v, ("zl", "zh"), [(i, 3 - i) for i in range(4)])


def gather_rel(v):
    return [v] + [lax.ppermute(v, "y", ring(4, 4 - r)) for r in range(1, 4)]


def scatter_rel(blocks):
    return [blocks[0]] + [lax.ppermute(blocks[r], "y", ring(4, r)) for r in range(1, 4)]


def exchange(v, axes):
    return lax.all_to_all(v, axes, 0, 0)


class Far:
    def __init__(self, array, start=0, rows=None, row=None, block=None):
        self.array = array
        self.row = row
        self.block = block
        self.start = start
        self.rows = array.shape[0] if rows is None else rows
        self.shape = (self.rows,) + array.shape[1:]
        if array.ndim > 2:
            self.shape = array.shape if rows is None else (array.shape[0], rows) + array.shape[2:]
        if block is not None:
            self.array = array.reshape((array.shape[0] // block, block) + array.shape[1:])
            self.shape = (array.shape[0] // block,) + self.shape


def far(*arrays):
    return [Far(v) for v in arrays]


class Arriving:
    def __init__(self, ref, copy):
        self.ref = ref
        self.copy = copy
        self.shape = ref.shape

    def here(self):
        if self.copy is not None:
            self.copy.wait()
            self.copy = None
        return self.ref

    def __getitem__(self, index):
        return self.here()[index]


class Leaving:
    def __init__(self, ref, copy):
        self.ref = ref
        self.copy = copy
        self.started = False
        self.shape = ref.shape
        self.dtype = ref.dtype

    def __getitem__(self, index):
        return self.ref[index]

    def __setitem__(self, index, value):
        assert not self.started
        self.ref[index] = value

    @property
    def at(self):
        return self.ref.at

    def leave(self):
        if not self.started:
            self.started = True
            self.copy.start()


def leave(*refs):
    for ref in refs:
        ref.leave()


def whole_block(shape):
    return pl.BlockSpec(shape, lambda i: (0,) * len(shape), pipeline_mode=pl.Buffered(1))


def run(kernel, outs, scalars, inputs, scratch=(), vmem=60, lazy=False):
    body, us = kernel
    away = [isinstance(v, Far) for v in inputs]
    specs = [pl.BlockSpec(memory_space=pltpu.HBM) if a else whole_block(v.shape) for a, v in zip(away, inputs)]
    arrays = [v.array if a else v for a, v in zip(away, inputs)]
    staged = [pltpu.VMEM(v.shape, v.array.dtype) for a, v in zip(away, inputs) if a]
    shapes = [jax.ShapeDtypeStruct(s, d) for s, d in outs]
    back = [len(s) > 1 for s, _ in outs]
    held = [pltpu.VMEM(s, d) for (s, d), b in zip(outs, back) if b]
    scratch = list(scratch)

    def whole_body(sc, *refs):
        count = len(inputs)
        given, rest = list(refs[:count]), refs[count:]
        results, rest = list(rest[: len(outs)]), rest[len(outs) :]
        own, rest = rest[: len(scratch)], rest[len(scratch) :]
        kept, rest = rest[: len(held)], rest[len(held) :]
        leaving = []
        for i in range(len(outs)):
            if back[i]:
                n = len(leaving)
                leaving.append(Leaving(kept[n], pltpu.make_async_copy(kept[n], results[i], rest[-1].at[len(staged) + n])))
                results[i] = leaving[-1]
        copies = []
        for i, v in enumerate(inputs):
            if not away[i]:
                continue
            n = len(copies)
            source = given[i]
            if v.array.ndim > 2 and v.shape == v.array.shape:
                pass
            elif v.array.ndim > 2:
                source = given[i].at[:, pl.ds(v.start, v.rows)]
            elif v.row is None and v.shape != v.array.shape:
                source = given[i].at[pl.ds(v.start, v.rows)]
            elif v.row is not None:
                source = given[i].at[pl.ds(pl.multiple_of(sc[v.row] * v.rows, v.rows), v.rows)]
            copies.append(Arriving(rest[n], pltpu.make_async_copy(source, rest[n], rest[-1].at[n])))
            given[i] = copies[-1]
        for v in copies:
            v.copy.start()
        if not lazy:
            for v in copies:
                v.here()
        body(sc, *given, *results, *own)
        for v in copies:
            v.here()
        leave(*leaving)
        for v in leaving:
            v.copy.wait()

    scratch_shapes = scratch + held + staged + [pltpu.SemaphoreType.DMA((max(len(staged) + len(held), 1),))]
    return pl.pallas_call(
        whole_body,
        out_shape=shapes,
        in_specs=[pl.BlockSpec(memory_space=pltpu.SMEM)] + specs,
        out_specs=[
            pl.BlockSpec(memory_space=pltpu.HBM) if b else whole_block(s.shape) for b, s in zip(back, shapes)
        ],
        grid=(1,),
        scratch_shapes=scratch_shapes,
        compiler_params=pltpu.CompilerParams(vmem_limit_bytes=vmem * 2**20),
        cost_estimate=pl.CostEstimate(flops=int(us * 1.15e9), bytes_accessed=0, transcendentals=0),
    )(scalars, *arrays)


def rows_at(start, count):
    return pl.ds(pl.multiple_of(start, count), count)


def row(ref):
    return ref[...].reshape(1, -1)


def normal_of(v):
    center = v - jnp.mean(v, axis=-1, keepdims=True)
    inverse = lax.rsqrt(jnp.mean(center * center, axis=-1, keepdims=True) + 1e-05)
    return center * inverse, inverse


def norm_back(gradient, normal, inverse, gain):
    scaled = gradient * gain
    adjusted = (
        scaled
        - jnp.mean(scaled, axis=-1, keepdims=True)
        - normal * jnp.mean(scaled * normal, axis=-1, keepdims=True)
    )
    return adjusted * inverse


def col_sum(v):
    return jnp.sum(v, axis=0, keepdims=True)


def set_places(sc):
    c, zh = sc[1], sc[2]
    return [2 * zh + c, 2 * (1 - zh) + c, 2 * zh + 1 - c, 2 * (1 - zh) + 1 - c]


def head_masks(width=256):
    lane = lax.broadcasted_iota(jnp.int32, (1, width), 1) // 64
    return [lane == h for h in range(4)]


def scalar_kernel(ids, tgt_len, src_len, pair_ids, loss_weights, out):
    for i in range(3):
        out[i] = ids[i]
    out[3] = tgt_len[ids[2]]
    out[4] = src_len[ids[2]]
    out[5] = loss_weights[pair_ids[ids[2]]]
    out[6] = ids[3]
    out[7] = ids[4]


VECTORS = ("first_gain", "first_shift", "self_output_bias", "second_gain", "second_shift")
VECTORS += ("cross_output_bias", "third_gain", "third_shift", "ffn_out_bias")


def vector(vecs, name):
    i = VECTORS.index(name)
    return vecs[i : i + 1, :]


def pack_kernel(sc, q, k, v, cq, ck, cv, o, co, qb, vb, cqb, cvb, fb, *refs):
    vectors, (one, wow, vecs) = refs[: len(VECTORS)], refs[len(VECTORS) :]
    for i, m in enumerate((q, k, v)):
        one[i * 64 : (i + 1) * 64, :] = m[...]
    for i, m in enumerate((cq, ck, cv)):
        one[208 + i * 64 : 272 + i * 64, :] = m[...]
    vec = jnp.concatenate([row(qb), row(vb), row(cqb), row(cvb), row(fb)], axis=1)
    high = vec.astype(BF).astype(F32)
    both = jnp.concatenate([high, vec - high], axis=1)
    first = lax.broadcasted_iota(jnp.int32, (16, 1024), 0) == 0
    one[192:208, :] = jnp.where(first, both, 0.0).astype(BF)
    wow[0:64, :] = o[...]
    wow[64:128, :] = co[...]
    for i, v in enumerate(vectors):
        vecs[i : i + 1, :] = row(v)
    vecs[len(VECTORS) : 16, :] = jnp.zeros((16 - len(VECTORS), 1024), F32)


def pack_more_kernel(sc, fin, fout, out):
    out[0:256, :] = fin[...].astype(F32).T.astype(BF)
    out[256:512, :] = fout[...]


def qkv_kernel(sc, t0, t1, t2, t3, vecs, a0, a1, a2, a3, first, tok, q, kv, w, bias):
    gain, shift = vector(vecs, "first_gain"), vector(vecs, "first_shift")
    for r, t in enumerate((t0, t1, t2, t3)):
        place = rows_at(lax.rem(sc[0] + r, 4) * 128, 128)
        tok[place, :] = t[...]
        normal, _ = normal_of(t[...].astype(F32))
        first[place, :] = (normal * gain + shift).astype(BF)
    for part, place in zip((a0, a1, a2, a3), set_places(sc)):
        for m in range(3):
            w[rows_at(m * 256 + place * 64, 64), :] = part[m * 64 : (m + 1) * 64, :]
        vec = part[192:208, :].astype(F32)[0:1, :]
        bias[pl.ds(place, 1), :] = vec[:, :512] + vec[:, 512:]
    x = first[...]

    def bias_of(i):
        return jnp.concatenate([bias[h : h + 1, i * 64 : (i + 1) * 64] for h in range(4)], axis=1)

    leave(first, tok, w, bias)
    kv[:, 0:256] = nt(x, w[256:512, :]).astype(BF)
    kv[:, 256:512] = (nt(x, w[512:768, :]) + bias_of(1)).astype(BF)
    leave(kv)
    q[...] = (SCALE * (nt(x, w[0:256, :]) + bias_of(0))).astype(BF)


def source_kernel(sc, mem, a0, a1, a2, a3, bias, ckv, w, own):
    for part, place in zip((a0, a1, a2, a3), set_places(sc)):
        for m in range(3):
            w[rows_at(m * 256 + place * 64, 64), :] = part[m * 64 : (m + 1) * 64, :]
    vb = jnp.concatenate([bias[h : h + 1, 192:256] for h in range(4)], axis=1)
    ckv[:, 0:256] = nt(mem[...], w[256:512, :]).astype(BF)
    ckv[:, 256:512] = (nt(mem[...], w[512:768, :]) + vb).astype(BF)
    for j in range(4):
        own[j * 128 : (j + 1) * 128, :] = mem[rows_at((2 * j + sc[1]) * 128, 128), :]


def key_bias(core, length, axis):
    k = lax.broadcasted_iota(jnp.int32, (1, 512) if axis == 1 else (512, 1), axis)
    position = ((k >> 7) * 2 + core) * 128 + (k & 127)
    return jnp.where(position < length, 0.0, NEG)


def diagonal_bias(key_core, query_core, transposed):
    q = lax.broadcasted_iota(jnp.int32, (256, 256), 1 if transposed else 0)
    k = lax.broadcasted_iota(jnp.int32, (256, 256), 0 if transposed else 1)
    q = ((q >> 7) * 2 + query_core) * 128 + (q & 127)
    k = ((k >> 7) * 2 + key_core) * 128 + (k & 127)
    return jnp.where(k <= q, 0.0, NEG)


def attend(q_rows, sources, biases):
    masks = head_masks()
    lane = lax.broadcasted_iota(jnp.int32, (1, 128), 1)
    count = q_rows.shape[0]
    mixed = jnp.zeros((count, 256), F32)
    totals = jnp.zeros((count, 128), F32)
    for h in range(4):
        qh = jnp.where(masks[h], q_rows, jnp.zeros_like(q_rows))
        scores = [nt(qh, k) + b for (k, _), b in zip(sources, biases)]
        top = functools.reduce(jnp.maximum, [jnp.max(s, axis=1, keepdims=True) for s in scores])
        raised = [jnp.exp(s - top) for s in scores]
        total = sum(jnp.sum(p, axis=1, keepdims=True) for p in raised)
        out = sum(nn(p.astype(BF), v) for p, (_, v) in zip(raised, sources))
        mixed = jnp.where(masks[h], out * (1.0 / total), mixed)
        totals = jnp.where(lane == h, top + jnp.log(total), totals)
    return mixed, totals


def causal_biases(sc, axis):
    c, length = sc[1], sc[3]
    transposed = axis == 0
    return (
        [key_bias(c, length, axis), key_bias(1 - c, length, axis)],
        [diagonal_bias(c, c, transposed), diagonal_bias(1 - c, c, transposed)],
    )


def pair_bias(length_bias, diagonal, a, axis):
    if axis == 1:
        last = length_bias[:, a * 256 : (a + 1) * 256] + diagonal
        if a == 0:
            return last
        return jnp.concatenate([jnp.broadcast_to(length_bias[:, 0:256], (256, 256)), last], axis=1)
    last = length_bias[a * 256 : (a + 1) * 256, :] + diagonal
    if a == 0:
        return last
    return jnp.concatenate([jnp.broadcast_to(length_bias[0:256, :], (256, 256)), last], axis=0)


def self_forward_kernel(sc, q, kvo, kvs, mixed, totals, stat):
    lengths, diagonals = causal_biases(sc, 1)
    for a in range(2):
        n = (a + 1) * 256
        sources = [(kvo[0:n, 0:256], kvo[0:n, 256:512]), (kvs[0:n, 0:256], kvs[0:n, 256:512])]
        biases = [pair_bias(lengths[i], diagonals[i], a, 1) for i in range(2)]
        out, total = attend(q[a * 256 : (a + 1) * 256, :], sources, biases)
        mixed[a * 256 : (a + 1) * 256, :] = out.astype(BF)
        stat[a * 256 : (a + 1) * 256, :] = total
    totals[...] = stat[...].T[0:8, :]


def cross_forward_kernel(sc, q, ckv, mixed, totals, stat):
    key = lax.broadcasted_iota(jnp.int32, (1, 1024), 1)
    bias = jnp.where(key < sc[4], 0.0, NEG)
    for a in range(2):
        out, total = attend(q[a * 256 : (a + 1) * 256, :], [(ckv[:, 0:256], ckv[:, 256:512])], [bias])
        mixed[a * 256 : (a + 1) * 256, :] = out.astype(BF)
        stat[a * 256 : (a + 1) * 256, :] = total
    totals[...] = stat[...].T[0:8, :]


def chip_rows(sc, whole, order):
    for r in range(4):
        chip = lax.rem(sc[0] + r, 4)
        for z in range(2):
            for core in range(2):
                place = r * 256 + z * 128 + core * 64
                order[place : place + 64, :] = whole[z * 8 + chip * 2 + core]


def set_rows(sc, sets, order):
    for r in range(4):
        chip = lax.rem(sc[0] + r, 4)
        for part, place in zip(sets, set_places(sc)):
            order[rows_at(r * 256 + place * 64, 64), :] = part[chip]


def second_kernel(
    sc, m0, m1, m2, m3, wo, tok, vecs, cw, bias, second, resid, cq, wo_own, order
):
    ob, gain, shift = (vector(vecs, n) for n in ("self_output_bias", "second_gain", "second_shift"))
    chip_rows(sc, wo, order)
    wo_own[...] = order[0:256, :]
    resid[...] = nn(jnp.concatenate([m0[...], m1[...], m2[...], m3[...]], axis=1), order[...])
    for j in range(4):
        place = slice(j * 128, (j + 1) * 128)
        v = tok[place, :].astype(F32) + (resid[place, :] + ob)
        resid[place, :] = v
        normal, _ = normal_of(v)
        second[place, :] = (normal * gain + shift).astype(BF)
    leave(second, resid, wo_own)
    qb = jnp.concatenate([bias[h : h + 1, 128:192] for h in range(4)], axis=1)
    cq[...] = (SCALE * (nt(second[...], cw[0:256, :]) + qb)).astype(BF)


def upstream_kernel(sc, c0, c1, c2, c3, w0, w1, w2, w3, og, up):
    weight = 0.5 * sc[5].astype(F32)
    for r, t in enumerate((c0, c1, c2, c3)):
        chip = lax.rem(sc[0] + r, 4)
        position = (2 * chip + sc[1]) * 128 + lax.broadcasted_iota(jnp.int32, (128, 1), 0)
        og[rows_at(chip * 128, 128), :] = (t[...].astype(F32) * jnp.where(position < sc[3], weight, 0.0)).astype(BF)
    for s, w in enumerate((w0, w1, w2, w3)):
        up[:, s * 256 : (s + 1) * 256] = nt(og[...], w[...]).astype(BF)


def ffn_kernel(
    sc, m0, m1, m2, m3, wco, resid, vecs, up, w0, w1, w2, w3, bias,
    third, hidden, pre, back0, back1, back2, back3, own, wco_own, order, work,
):
    y = sc[0]
    ob, gain, shift = (vector(vecs, n) for n in ("cross_output_bias", "third_gain", "third_shift"))
    chip_rows(sc, wco, order)
    wco_own[...] = order[0:256, :]
    work[...] = nn(jnp.concatenate([m0[...], m1[...], m2[...], m3[...]], axis=1), order[...])
    for s, w in enumerate((w0, w1, w2, w3)):
        order[s * 256 : (s + 1) * 256, :] = w[...]
    for j in range(4):
        place = slice(j * 128, (j + 1) * 128)
        v = resid[place, :] + (work[place, :] + ob)
        work[place, :] = v
        normal, _ = normal_of(v)
        third[place, :] = (normal * gain + shift).astype(BF)
    own[...] = work[rows_at(y * 128, 128), :]
    leave(third, own, wco_own)
    places = set_places(sc)
    for s in range(4):
        cols = slice(s * 256, (s + 1) * 256)
        u = nt(third[...], order[cols, :]) + bias[pl.ds(places[s], 1), 256:512]
        square = u * u
        t = jnp.tanh(0.7978845608028654 * (u + 0.044715 * (square * u)))
        hidden[:, cols] = (0.5 * u * (1.0 + t)).astype(BF)
        slope = 0.5 * (1.0 + t) + 0.5 * u * (1.0 - t * t) * (0.7978845608028654 * (1.0 + 0.134145 * square))
        pre[:, cols] = (up[:, cols].astype(F32) * slope).astype(BF)
    leave(hidden, pre)
    store_rel(sc, nn(pre[...], order[...]), work, (back0, back1, back2, back3))


def store_rel(sc, value, work, outs):
    work[...] = value
    for r, out in enumerate(outs):
        out[...] = work[rows_at(lax.rem(sc[0] + r, 4) * 128, 128), :].astype(BF)


def total_of(parts):
    p = [v[...].astype(F32) for v in parts]
    return (p[0] + p[1]) + (p[2] + p[3])


def late_rows_kernel(sc, p0, p1, p2, p3, own, vecs, out, mem):
    total = total_of((p0, p1, p2, p3))
    out[...] = (own[...] + (total[0:128, :] + vector(vecs, "ffn_out_bias"))).astype(BF)
    mem[...] = total[128:256, :]


def split_rows(values):
    high = values.astype(BF).astype(F32)
    return jnp.concatenate([high, values - high, jnp.zeros((12, values.shape[1]), F32)], axis=0).astype(BF)


def joined_rows(block):
    f = block.astype(F32)
    return f[0:2, :] + f[2:4, :]


def third_grad_kernel(sc, p0, p1, p2, p3, own, cot, vecs, grad, low):
    position = (2 * sc[0] + sc[1]) * 128 + lax.broadcasted_iota(jnp.int32, (128, 1), 0)
    og = cot[...].astype(F32) * jnp.where(position < sc[3], 0.5 * sc[5].astype(F32), 0.0)
    back = total_of((p0, p1, p2, p3))
    normal, inverse = normal_of(own[...])
    total = og + norm_back(back, normal, inverse, vector(vecs, "third_gain"))
    grad[...] = total
    low[0:128, :] = total.astype(BF)
    low[128:144, :] = split_rows(jnp.concatenate([col_sum(back * normal), col_sum(back)], axis=0))


def masked_stack(v, stack):
    masks = head_masks()
    for a in range(2):
        rows = v[a * 256 : (a + 1) * 256, :]
        for h in range(4):
            stack[a, h * 256 : (h + 1) * 256, :] = jnp.where(masks[h], rows, jnp.zeros_like(rows))


def delta_of(mixed, grad):
    head = lax.broadcasted_iota(jnp.int32, (8, 256), 0)
    lane = lax.broadcasted_iota(jnp.int32, (8, 256), 1) // 64
    ones = jnp.where(head == lane, 1.0, 0.0)
    product = mixed.astype(F32) * grad.astype(F32)
    return lax.dot_general(
        ones, product, (((1,), (1,)), ((), ())), preferred_element_type=F32, precision=lax.Precision.HIGHEST
    )


def pair_backward(a, q_stack, g_stack, totals, delta, keys, values, keys_t, bias, probs, scores):
    cols = slice(a * 256, (a + 1) * 256)
    dq = []
    for h in range(4):
        place = slice(h * 256, (h + 1) * 256)
        s = nt(keys, q_stack[a, place, :]) + bias
        p = jnp.exp(s - totals[h : h + 1, cols])
        ds = (p * (nt(values, g_stack[a, place, :]) - delta[h : h + 1, cols])).astype(BF)
        probs[:, place] = p.astype(BF)
        scores[:, place] = ds
        dq.append(nn(keys_t[h * 64 : (h + 1) * 64, :], ds))
    return jnp.concatenate(dq, axis=0)


def cross_backward_kernel(
    sc, t0, t1, t2, t3, wco, cq, ckv, mixed, totals, og, tg, dq, own, other, vec,
    q_stack, g_stack, probs, scores, delta, part,
):
    norm_sums = jnp.zeros((2, 1024), F32)
    for r, t in enumerate((t0, t1, t2, t3)):
        tg[rows_at(lax.rem(sc[0] + r, 4) * 128, 128), :] = t[0:128, :]
        norm_sums = norm_sums + joined_rows(t[128:144, :])
    vec[0:2, :] = norm_sums
    vec[2:3, :] = col_sum(og[...].astype(F32))
    vec[3:4, :] = col_sum(tg[...].astype(F32))
    vec[4:8, :] = jnp.zeros((4, 1024), F32)
    leave(tg, vec)
    g = nt(tg[...], wco[...]).astype(BF)
    delta[...] = delta_of(mixed[...], g)
    masked_stack(g, g_stack)
    masked_stack(cq[...], q_stack)
    key = lax.broadcasted_iota(jnp.int32, (1024, 1), 0)
    bias = jnp.where(key < sc[4], 0.0, NEG)
    keys_t = ckv[:, 0:256].T
    for a in range(2):
        grad = pair_backward(
            a, q_stack, g_stack, totals, delta, ckv[:, 0:256], ckv[:, 256:512], keys_t, bias, probs.at[a], scores.at[a]
        )
        dq[a * 256 : (a + 1) * 256, :] = grad.T.astype(BF)
    leave(dq)
    part[:, 0:256] = nn(scores[0], q_stack[0]) + nn(scores[1], q_stack[1])
    part[:, 256:512] = nn(probs[0], g_stack[0]) + nn(probs[1], g_stack[1])
    for j in range(4):
        place = slice(j * 128, (j + 1) * 128)
        own[place, :] = part[rows_at((2 * j + sc[1]) * 128, 128), :]
        other[place, :] = part[rows_at((2 * j + 1 - sc[1]) * 128, 128), :].astype(BF)


def second_grad_kernel(
    sc, d0, d1, d2, d3, a0, a1, a2, a3, resid, vecs, tg, tg_own, wo,
    low, grad_own, g, vec, order, work,
):
    gain = vector(vecs, "second_gain")
    set_rows(sc, (a0, a1, a2, a3), order)
    work[...] = nn(jnp.concatenate([d0[...], d1[...], d2[...], d3[...]], axis=1), order[...])
    sums = [jnp.zeros((1, 1024), F32)] * 3
    for j in range(4):
        place = slice(j * 128, (j + 1) * 128)
        normal, inverse = normal_of(resid[place, :])
        back = SCALE * work[place, :]
        v = norm_back(back, normal, inverse, gain)
        work[place, :] = v
        rounded = (tg[place, :].astype(F32) + v).astype(BF)
        low[place, :] = rounded
        for i, add in enumerate((back * normal, back, rounded.astype(F32))):
            sums[i] = sums[i] + col_sum(add)
    leave(low)
    g[...] = nt(low[...], wo[...]).astype(BF)
    leave(g)
    grad_own[...] = tg_own[...] + work[rows_at(sc[0] * 128, 128), :]
    vec[...] = jnp.concatenate(sums + [jnp.zeros((5, 1024), F32)], axis=0)


def self_backward_kernel(
    sc, g, q, kvo, kvs, mixed, totals, dq, own, other, q_stack, g_stack, p0, s0, p1, s1, delta
):
    delta[...] = delta_of(mixed[...], g[...])
    masked_stack(g[...], g_stack)
    masked_stack(q[...], q_stack)
    lengths, diagonals = causal_biases(sc, 0)
    keys_t = [kv[:, 0:256].T for kv in (kvo, kvs)]
    for a in range(2):
        n = (a + 1) * 256
        probs, scores = ((p0, s0), (p1, s1))[a]
        grad = jnp.zeros((256, 256), F32)
        for i, kv in enumerate((kvo, kvs)):
            bias = pair_bias(lengths[i], diagonals[i], a, 0)
            grad = grad + pair_backward(
                a, q_stack, g_stack, totals, delta, kv[0:n, 0:256], kv[0:n, 256:512], keys_t[i][:, 0:n], bias,
                probs.at[i], scores.at[i],
            )
        dq[a * 256 : (a + 1) * 256, :] = grad.T.astype(BF)
    leave(dq)
    for i, out in ((1, other), (0, own)):
        kind = out.dtype
        for cols, first, second, stack in (
            (slice(0, 256), s0, s1, q_stack),
            (slice(256, 512), p0, p1, g_stack),
        ):
            out[0:256, cols] = (nn(first[i], stack[0]) + nn(second[i, 0:256, :], stack[1])).astype(kind)
            out[256:512, cols] = nn(second[i, 256:512, :], stack[1]).astype(kind)
        leave(out)


def first_back_kernel(sc, dq, dkv, w, b0, b1, b2, b3, work):
    part = SCALE * nn(dq[...], w[0:256, :]) + nn(dkv[:, 0:256], w[256:512, :]) + nn(dkv[:, 256:512], w[512:768, :])
    store_rel(sc, part, work, (b0, b1, b2, b3))


def tokens_grad_kernel(sc, p0, p1, p2, p3, tokens, vecs, grad, out):
    normal, inverse = normal_of(tokens[...].astype(F32))
    out[...] = grad[...] + norm_back(
        total_of((p0, p1, p2, p3)), normal, inverse, vector(vecs, "first_gain")
    )


def memory_back_kernel(sc, grad, w, hidden, w0, w1, w2, w3, b0, b1, b2, b3, order, work):
    outs = (b0, b1, b2, b3)
    for s, part in enumerate((w0, w1, w2, w3)):
        order[s * 256 : (s + 1) * 256, :] = part[...]
    store_rel(sc, nn(hidden[...], order[...]), work, [b.at[0:128] for b in outs])
    value = nn(grad[:, 0:256], w[0:256, :]) + nn(grad[:, 256:512], w[256:512, :])
    store_rel(sc, value, work, [b.at[128:256] for b in outs])


def store_pieces(out, z, start, block):
    for i in range(8):
        out[i, z, start : start + block.shape[0], :] = block[:, i * 128 : (i + 1) * 128].astype(BF)


def store_bias(out, z, start, values, vectors=()):
    wide = jnp.concatenate([values, jnp.zeros((1, 1024 - values.shape[1]), F32)], axis=1)
    rows = [wide] + list(vectors)
    rows.append(jnp.zeros((16 - sum(v.shape[0] for v in rows), 1024), F32))
    store_pieces(out, z, start, jnp.concatenate(rows, axis=0))


def ffn_weight_kernel(sc, pre, third, hidden, og, keep, send):
    zh = sc[2]
    for s in range(4):
        out = keep if s < 2 else send
        z = zh if s % 2 == 0 else 1 - zh
        cols = slice(s * 256, (s + 1) * 256)
        store_pieces(out, z, 0, tn(pre[:, cols], third[...]))
        store_pieces(out, z, 256, tn(hidden[:, cols], og[...]))
        store_bias(out, z, 512, col_sum(pre[:, cols].astype(F32)))


def cross_weight_kernel(sc, own, other, mixed, tg, dq, second, mem, vec, dkv, keep, send, product):
    dkv[...] = (own[...] + other[...].astype(F32)).astype(BF)
    leave(dkv)
    sides = ((keep, sc[1]), (send, 1 - sc[1]))
    ones = jnp.ones((8, 512), BF)
    q_bias = SCALE * nn(ones, dq[...])[0:1, :]
    v_bias = nn(ones, dkv[:, 256:512])[0:1, :]
    for m in range(4):
        if m == 0:
            product[...] = tn(mixed[...], tg[...])
        elif m == 1:
            product[...] = SCALE * tn(dq[...], second[...])
        else:
            product[...] = tn(dkv[:, (m - 2) * 256 : (m - 1) * 256], mem[...])
        for z in range(2):
            for out, core in sides:
                store_pieces(out, z, m * 64, product[rows_at((2 * z + core) * 64, 64), :])
    for z in range(2):
        for out, core in sides:
            store_head_bias(out, z, core, q_bias, v_bias, [vec[0:4, :]])


def store_head_bias(out, z, core, q_bias, v_bias, vectors):
    rows = [
        jnp.concatenate([v[:, s * 64 : (s + 1) * 64] for v in (q_bias, v_bias)], axis=1) for s in (2 * z, 2 * z + 1)
    ]
    store_bias(out, z, 256, jnp.where(core == 0, rows[0], rows[1]), vectors)


def self_weight_kernel(sc, dq, own, other, tok, w, mixed, sg, vecs, vec2, dkv, keep, send, vec, normal, product):
    gain, shift = vector(vecs, "first_gain"), vector(vecs, "first_shift")
    dkv[...] = (own[...] + other[...].astype(F32)).astype(BF)
    leave(dkv)
    for j in range(4):
        place = slice(j * 128, (j + 1) * 128)
        normal[place, :] = normal_of(tok[place, :].astype(F32))[0].astype(BF)
    ones = jnp.ones((8, 512), BF)
    gain_sum = jnp.zeros((1, 1024), F32)
    shift_sum = jnp.zeros((1, 1024), F32)
    q_bias = v_bias = None
    for m, (grad, factor) in enumerate(((dq[...], SCALE), (dkv[:, 0:256], 1.0), (dkv[:, 256:512], 1.0))):
        sums = factor * tn(grad, ones.T)[:, 0:1]
        product[...] = factor * tn(grad, normal[...])
        weight = w[m * 256 : (m + 1) * 256, :].astype(F32)
        gain_sum = gain_sum + col_sum(weight * product[...])
        shift_sum = shift_sum + col_sum(weight * sums)
        total = product[...] * gain + sums * shift
        product[...] = total
        for z in range(2):
            for out, core in ((keep, sc[1]), (send, 1 - sc[1])):
                store_pieces(out, z, (m + 1) * 64, product[rows_at((2 * z + core) * 64, 64), :])
        if m != 1:
            flat = factor * nn(ones, grad)[0:1, :]
            if m == 0:
                q_bias = flat
            else:
                v_bias = flat
    sums_rows = split_rows(jnp.concatenate([gain_sum, shift_sum], axis=0))[0:4, :].astype(F32)
    product[...] = tn(mixed[...], sg[...])
    for z in range(2):
        for out, core in ((keep, sc[1]), (send, 1 - sc[1])):
            store_pieces(out, z, 0, product[rows_at((2 * z + core) * 64, 64), :])
            store_head_bias(out, z, core, q_bias, v_bias, [vec2[0:3, :], sums_rows])
    vec[...] = jnp.concatenate([gain_sum, shift_sum, jnp.zeros((6, 1024), F32)], axis=0)


def add_kernel(sc, *refs):
    out, start = refs[-1], 0
    for a, b in zip(refs[:-1:2], refs[1:-1:2]):
        rows = a.shape[2]
        for i in range(8):
            out[i, :, start : start + rows, :] = (a[i].astype(F32) + b[i].astype(F32)).astype(BF)
        start += rows


def piece_sum(got):
    total = got[0].astype(F32)
    for i in range(1, 16):
        total = total + got[i].astype(F32)
    return total.astype(BF)


def sum_kernel(sc, ffn, cross, out):
    out[0:528, :] = piece_sum(ffn)
    out[528:800, :] = piece_sum(cross)


def spread_kernel(sc, *refs):
    start, out = 0, refs[-1]
    for got in refs[:-1]:
        total = piece_sum(got) if len(got.shape) == 3 else got[...]
        rows = total.shape[0]
        for i in range(8):
            out[i, start : start + rows, :] = total
        start += rows


def ffn_result(got, start, fin, fout, fb):
    for i in range(8):
        fout[:, i * 128 : (i + 1) * 128] = got[i, start + 256 : start + 512, :].astype(F32)
    leave(fout)
    for i in range(8):
        fin[i * 128 : (i + 1) * 128, :] = got[i, start : start + 256, :].astype(F32).T
    leave(fin)
    rows = [got[i, start + 512 : start + 528, :].astype(F32)[0:1, :] for i in range(2)]
    fb[...] = jnp.concatenate(rows, axis=1).reshape(256)


def first_sums_kernel(sc, got, out):
    rows = jnp.concatenate([got[i].astype(F32) for i in range(8)], axis=1)
    out[...] = split_rows(rows[4:6, :] + rows[6:8, :])


def first_total_kernel(sc, v0, v1, v2, v3, gain, shift):
    total = sum(joined_rows(v[...]) for v in (v0, v1, v2, v3))
    gain[...] = total[0:1, :].reshape(1024)
    shift[...] = total[1:2, :].reshape(1024)


def result_kernel(sc, got, *outs):
    ffn_result(got, 272, *outs[:3])
    heads_result(3, 0, got, *outs[3:12])
    heads_result(4, 800, got, *outs[12:])


def heads_result(count, start, got, o, q, k, v, qb, vb, *vectors):
    for m, out in enumerate((o, q, k, v)):
        for i in range(8):
            out[:, i * 128 : (i + 1) * 128] = got[i, start + m * 64 : start + (m + 1) * 64, :].astype(F32)
        leave(out)
    rows = jnp.concatenate([got[i, start + 256 : start + 272, :].astype(F32) for i in range(8)], axis=1)
    qb[...] = rows[0:1, 0:64].reshape(64)
    vb[...] = rows[0:1, 64:128].reshape(64)
    for i in range(count):
        vectors[i][...] = rows[i + 1 : i + 2, :].reshape(1024)


def core_sum(sc, *pairs, us=4.8):
    rows = sum(keep.shape[2] for keep, _ in pairs)
    return run((add_kernel, us), [((8, 2, rows, 128), BF)], sc, far(*[v for pair in pairs for v in pair]))[0]


def pieces(both):
    return exchange(both.reshape((16,) + both.shape[2:]), ("x", "zl", "zh"))


def per_device(
    tokens,
    memory,
    cotangent,
    tgt_len,
    src_len,
    pair_ids,
    loss_weights,
    first_gain,
    first_shift,
    self_query,
    self_query_bias,
    self_key,
    self_value,
    self_value_bias,
    self_output,
    self_output_bias,
    second_gain,
    second_shift,
    cross_query,
    cross_query_bias,
    cross_key,
    cross_value,
    cross_value_bias,
    cross_output,
    cross_output_bias,
    third_gain,
    third_shift,
    ffn_in,
    ffn_in_bias,
    ffn_out,
    ffn_out_bias,
):
    ids = jnp.stack([lax.axis_index("y"), lax.axis_index("c"), lax.axis_index("zh")] + [lax.axis_index("x"), lax.axis_index("zl")]).astype(jnp.int32)
    sc = pl.pallas_call(
        scalar_kernel,
        out_shape=jax.ShapeDtypeStruct((8,), jnp.int32),
        in_specs=[pl.BlockSpec(memory_space=pltpu.SMEM)] * 5,
        out_specs=pl.BlockSpec(memory_space=pltpu.SMEM),
    )(ids, tgt_len, src_len, pair_ids, loss_weights)

    def after(v, *others):
        return lax.optimization_barrier((v,) + others)[0]

    tok_blocks = gather_rel(tokens)
    given = {
        "first_gain": first_gain,
        "first_shift": first_shift,
        "self_output_bias": self_output_bias,
        "second_gain": second_gain,
        "second_shift": second_shift,
        "cross_output_bias": cross_output_bias,
        "third_gain": third_gain,
        "third_shift": third_shift,
        "ffn_out_bias": ffn_out_bias,
    }
    one, wow, vecs = run(
        (pack_kernel, 3.3),
        [((400, 1024), BF), ((128, 1024), BF), ((16, 1024), F32)],
        sc,
        far(self_query.T, self_key.T, self_value.T, cross_query.T, cross_key.T, cross_value.T)
        + far(self_output, cross_output)
        + [self_query_bias, self_value_bias, cross_query_bias, cross_value_bias, ffn_in_bias]
        + [given[n] for n in VECTORS],
        vmem=60,
    )
    one_half = from_half(one)
    one_core = from_core(one)
    (more,) = run(
        (pack_more_kernel, 3),
        [((512, 1024), BF)],
        sc,
        far(ffn_in, ffn_out),
        vmem=60,
    )
    whole_wow = lax.all_gather(wow, ("zh", "y", "c"), axis=0, tiled=True)
    wide = jnp.concatenate([one[208:272], one_half[208:272]], axis=0)
    query_own = lax.all_gather(after(wide, whole_wow), "y", axis=0, tiled=True)
    query_core = from_core(query_own)
    query_sets = [(query_own, 0), (query_own, 64), (query_core, 0), (query_core, 64)]
    one_core_half = from_core(after(one_half, more, *tok_blocks))

    def one_parts(start, rows):
        return [Far(v, start, rows) for v in (one, one_half, one_core, one_core_half)]

    first, tok, q, kv, w, bias = run(
        (qkv_kernel, 5.3),
        [((512, 1024), BF), ((512, 1024), BF), ((512, 256), BF), ((512, 512), BF), ((768, 1024), BF), ((4, 512), F32)],
        sc,
        far(*tok_blocks, after(vecs, wide)) + one_parts(0, 208),
        lazy=True,
    )
    kvs = from_core(kv)
    self_mixed, self_totals = run(
        (self_forward_kernel, 5.8),
        [((512, 256), BF), ((8, 512), F32)],
        sc,
        far(q, kv, kvs),
        [pltpu.VMEM((512, 128), F32)],
    )
    mixed_blocks = gather_rel(self_mixed)
    more_half = from_half(after(more, self_mixed))
    cot_blocks = gather_rel(after(cotangent, *mixed_blocks))
    more_core = from_core(after(more, self_mixed))

    ckv, cw, mem_own = run(
        (source_kernel, 6),
        [((1024, 512), BF), ((768, 1024), BF), ((512, 1024), BF)],
        sc,
        [Far(memory, 0, 1024, row=2)] + one_parts(208, 192) + [Far(bias)],
    )
    second, resid, cq, wo_own = run(
        (second_kernel, 8),
        [((512, 1024), BF), ((512, 1024), F32), ((512, 256), BF), ((256, 1024), BF)],
        sc,
        far(*mixed_blocks) + [Far(whole_wow, 0, 64, block=128)] + far(tok, vecs) + [Far(cw, 0, 256), Far(bias)],
        [pltpu.VMEM((1024, 1024), BF)],
        lazy=True,
    )
    cross_mixed, cross_totals = run(
        (cross_forward_kernel, 6),
        [((512, 256), BF), ((8, 512), F32)],
        sc,
        far(after(cq, *cot_blocks), ckv),
        [pltpu.VMEM((512, 128), F32)],
    )
    cross_blocks = gather_rel(cross_mixed)
    more_core_half = from_core(after(more_half, cross_mixed))

    def more_parts(start, rows):
        return [Far(v, start, rows) for v in (more, more_half, more_core, more_core_half)]

    og, up = run(
        (upstream_kernel, 5),
        [((512, 1024), BF), ((512, 1024), BF)],
        sc,
        far(*cot_blocks) + more_parts(256, 256),
    )
    rows_out = [((128, 1024), BF)] * 4
    third, hidden, pre, b0, b1, b2, b3, resid_own, wco_own = run(
        (ffn_kernel, 11.5),
        [((512, 1024), BF)] * 3 + rows_out + [((128, 1024), F32), ((256, 1024), BF)],
        sc,
        far(*cross_blocks) + [Far(whole_wow, 64, 64, block=128)] + far(resid, vecs, up) + more_parts(0, 256) + [Far(bias)],
        [pltpu.VMEM((1024, 1024), BF), pltpu.VMEM((512, 1024), F32)],
    )
    third_parts = scatter_rel([b0, b1, b2, b3])
    ffn_keep, ffn_send = run(
        (ffn_weight_kernel, 7),
        [((8, 2, 528, 128), BF)] * 2,
        sc,
        far(pre, third, hidden, og),
        lazy=True,
    )
    third_grad, third_low = run(
        (third_grad_kernel, 20),
        [((128, 1024), F32), ((144, 1024), BF)],
        sc,
        far(*third_parts, resid_own, cotangent, vecs),
    )
    tg_blocks = gather_rel(third_low)
    ffn_both = core_sum(sc, (ffn_keep, from_core(ffn_send)))

    tg, cdq, ckv_own, ckv_other, third_vec = run(
        (cross_backward_kernel, 1.5),
        [((512, 1024), BF), ((512, 256), BF), ((512, 512), F32), ((512, 512), BF), ((8, 1024), F32)],
        sc,
        far(*tg_blocks, wco_own, cq, ckv, cross_mixed, after(cross_totals, ffn_both, query_core), og),
        [
            pltpu.VMEM((2, 1024, 256), BF),
            pltpu.VMEM((2, 1024, 256), BF),
            pltpu.VMEM((2, 1024, 1024), BF),
            pltpu.VMEM((2, 1024, 1024), BF),
            pltpu.VMEM((8, 512), F32),
            pltpu.VMEM((1024, 512), F32),
        ],
    )
    cdq_blocks = gather_rel(cdq)
    ckv_got = from_core(ckv_other)
    ckv_grad, cross_keep, cross_send = run(
        (cross_weight_kernel, 1.5),
        [((512, 512), BF)] + [((8, 2, 272, 128), BF)] * 2,
        sc,
        far(ckv_own, ckv_got, cross_mixed, tg, cdq, second, mem_own, third_vec),
        [pltpu.VMEM((256, 1024), F32)],
    )
    cross_both = core_sum(sc, (cross_keep, from_core(cross_send)), us=1.5)
    ffn_pieces = pieces(ffn_both)
    cross_pieces = pieces(after(cross_both, ffn_pieces))
    sg, second_grad, self_grad, second_vec = run(
        (second_grad_kernel, 8.5),
        [((512, 1024), BF), ((128, 1024), F32), ((512, 256), BF), ((8, 1024), F32)],
        sc,
        far(*cdq_blocks) + [Far(v, s, 64, block=128) for v, s in query_sets] + far(resid, vecs, tg, third_grad, after(wo_own, cross_both, ffn_pieces)),
        [pltpu.VMEM((1024, 1024), BF), pltpu.VMEM((512, 1024), F32)],
    )

    dq, kv_own, kv_other = run(
        (self_backward_kernel, 12),
        [((512, 256), BF), ((512, 512), F32), ((512, 512), BF)],
        sc,
        far(self_grad, q, kv, kvs, self_mixed, self_totals),
        [
            pltpu.VMEM((2, 1024, 256), BF),
            pltpu.VMEM((2, 1024, 256), BF),
            pltpu.VMEM((2, 256, 1024), BF),
            pltpu.VMEM((2, 256, 1024), BF),
            pltpu.VMEM((2, 512, 1024), BF),
            pltpu.VMEM((2, 512, 1024), BF),
            pltpu.VMEM((8, 512), F32),
        ],
    )
    kv_got = from_core(kv_other)
    dkv, self_keep, self_send, first_vec = run(
        (self_weight_kernel, 8),
        [((512, 512), BF), ((8, 2, 272, 128), BF), ((8, 2, 272, 128), BF), ((8, 1024), F32)],
        sc,
        far(dq, kv_own, kv_got, after(tok, cross_pieces), w, self_mixed, sg, vecs, second_vec),
        [pltpu.VMEM((512, 1024), BF), pltpu.VMEM((256, 1024), F32)],
    )
    self_recv = from_core(self_send)
    late_part = run(
        (memory_back_kernel, 2),
        [((256, 1024), BF)] * 4,
        sc,
        far(after(ckv_grad, self_recv)) + [Far(cw, 256, 512), Far(hidden)] + more_parts(256, 256),
        [pltpu.VMEM((1024, 1024), BF), pltpu.VMEM((512, 1024), F32)],
    )
    late_parts = scatter_rel(late_part)
    first_part = run(
        (first_back_kernel, 2),
        rows_out,
        sc,
        far(dq, after(dkv, self_recv, late_part[0]), w),
        [pltpu.VMEM((512, 1024), F32)],
    )
    first_parts = scatter_rel(first_part)
    self_both = core_sum(sc, (self_keep, self_recv))
    (tokens_grad,) = run(
        (tokens_grad_kernel, 15), [((128, 1024), F32)], sc, far(*first_parts, tokens, vecs, second_grad)
    )
    (early_piece,) = run(
        (sum_kernel, 2), [((800, 128), BF)], sc, far(after(ffn_pieces, self_both), cross_pieces)
    )
    (copies,) = run(
        (spread_kernel, 4), [((8, 1072, 128), BF)], sc, far(after(pieces(self_both), first_part[0]), early_piece)
    )
    got = exchange(copies, ("x", "zl"))
    block_out, memory_grad = run(
        (late_rows_kernel, 15), [((128, 1024), BF), ((128, 1024), F32)], sc, far(*late_parts, resid_own, vecs)
    )
    (first_sums,) = run((first_sums_kernel, 1.5), [((16, 1024), BF)], sc, [Far(after(got, block_out), 256, 16)])
    first_gain_grad, first_shift_grad = run(
        (first_total_kernel, 1.5), [((1024,), F32)] * 2, sc, far(*gather_rel(first_sums))
    )
    heads_out = [((64, 1024), F32)] * 4 + [((64,), F32)] * 2
    heads_out = heads_out + [((1024,), F32)] * 3 + heads_out + [((1024,), F32)] * 4
    heads_out = [((1024, 256), F32), ((256, 1024), F32), ((256,), F32)] + heads_out
    ffn_in_grad, ffn_out_grad, ffn_in_bias_grad, *outs = run((result_kernel, 7), heads_out, sc, far(got))
    self_out, cross_out = outs[:9], outs[9:]
    return (
        block_out,
        tokens_grad,
        memory_grad,
        first_gain_grad,
        first_shift_grad,
        self_out[1].T,
        self_out[4],
        self_out[2].T,
        self_out[3].T,
        self_out[5],
        self_out[0],
        self_out[8],
        self_out[6],
        self_out[7],
        cross_out[1].T,
        cross_out[4],
        cross_out[2].T,
        cross_out[3].T,
        cross_out[5],
        cross_out[0],
        cross_out[9],
        cross_out[6],
        cross_out[7],
        ffn_in_grad,
        ffn_in_bias_grad,
        ffn_out_grad,
        cross_out[8],
    )


def solution(mesh):
    fine = Mesh(mesh.devices.reshape(4, 2, 2, 4, 2), ("x", "zl", "zh", "y", "c"))
    dp = ("x", "zl")
    mp = ("zh", "y", "c")
    rows, cols, part, down, whole = P(dp + mp, None), P(None, mp), P(mp), P(mp, None), P()
    placed = (rows, P(dp, None), rows, P(dp), P(dp), P(dp), whole, whole, whole)
    placed += (cols, part, cols, cols, part, down, whole, whole, whole)
    placed += (cols, part, cols, cols, part, down, whole, whole, whole)
    placed += (cols, part, down, whole)
    attention = (cols, part, cols, cols, part, down, whole)
    given = (rows, rows, rows, whole, whole) + attention + (whole, whole) + attention + (whole, whole)
    given += (cols, part, down, whole)
    return jax.shard_map(per_device, mesh=fine, in_specs=placed, out_specs=given, check_vma=False)
```

```python
import functools

import jax
import jax.numpy as jnp
from jax import lax
from jax.experimental import pallas as pl
from jax.experimental.pallas import tpu as pltpu
from jax.sharding import Mesh, PartitionSpec as P

BF = jnp.bfloat16
F32 = jnp.float32
NEG = -1e30
SCALE = 0.125


def nn(a, b):
    return jnp.dot(a, b, preferred_element_type=F32)


def nt(a, b):
    return lax.dot_general(a, b, (((1,), (1,)), ((), ())), preferred_element_type=F32)


def tn(a, b):
    return lax.dot_general(a, b, (((0,), (0,)), ((), ())), preferred_element_type=F32)


def ring(n, k):
    return [(i, (i + k) % n) for i in range(n)]


def from_core(v):
    return lax.ppermute(v, "c", ring(2, 1))


def from_half(v):
    return lax.ppermute(v, ("zl", "zh"), [(i, 3 - i) for i in range(4)])


def gather_rel(v):
    return [v] + [lax.ppermute(v, "y", ring(4, 4 - r)) for r in range(1, 4)]


def scatter_rel(blocks):
    return [blocks[0]] + [lax.ppermute(blocks[r], "y", ring(4, r)) for r in range(1, 4)]


def exchange(v, axes):
    return lax.all_to_all(v, axes, 0, 0)


class Far:
    def __init__(self, array, start=0, rows=None, row=None, block=None):
        self.array = array
        self.row = row
        self.block = block
        self.start = start
        self.rows = array.shape[0] if rows is None else rows
        self.shape = (self.rows,) + array.shape[1:]
        if array.ndim > 2:
            self.shape = array.shape if rows is None else (array.shape[0], rows) + array.shape[2:]
        if block is not None:
            self.array = array.reshape((array.shape[0] // block, block) + array.shape[1:])
            self.shape = (array.shape[0] // block,) + self.shape


def far(*arrays):
    return [Far(v) for v in arrays]


class Arriving:
    def __init__(self, ref, copy):
        self.ref = ref
        self.copy = copy
        self.shape = ref.shape

    def here(self):
        if self.copy is not None:
            self.copy.wait()
            self.copy = None
        return self.ref

    def __getitem__(self, index):
        return self.here()[index]


class Leaving:
    def __init__(self, ref, copy):
        self.ref = ref
        self.copy = copy
        self.started = False
        self.shape = ref.shape
        self.dtype = ref.dtype

    def __getitem__(self, index):
        return self.ref[index]

    def __setitem__(self, index, value):
        assert not self.started
        self.ref[index] = value

    @property
    def at(self):
        return self.ref.at

    def leave(self):
        if not self.started:
            self.started = True
            self.copy.start()


def leave(*refs):
    for ref in refs:
        ref.leave()


def whole_block(shape):
    return pl.BlockSpec(shape, lambda i: (0,) * len(shape), pipeline_mode=pl.Buffered(1))


def run(kernel, outs, scalars, inputs, scratch=(), vmem=60, lazy=False):
    body, us = kernel
    away = [isinstance(v, Far) for v in inputs]
    specs = [pl.BlockSpec(memory_space=pltpu.HBM) if a else whole_block(v.shape) for a, v in zip(away, inputs)]
    arrays = [v.array if a else v for a, v in zip(away, inputs)]
    staged = [pltpu.VMEM(v.shape, v.array.dtype) for a, v in zip(away, inputs) if a]
    shapes = [jax.ShapeDtypeStruct(s, d) for s, d in outs]
    back = [len(s) > 1 for s, _ in outs]
    held = [pltpu.VMEM(s, d) for (s, d), b in zip(outs, back) if b]
    scratch = list(scratch)

    def whole_body(sc, *refs):
        count = len(inputs)
        given, rest = list(refs[:count]), refs[count:]
        results, rest = list(rest[: len(outs)]), rest[len(outs) :]
        own, rest = rest[: len(scratch)], rest[len(scratch) :]
        kept, rest = rest[: len(held)], rest[len(held) :]
        leaving = []
        for i in range(len(outs)):
            if back[i]:
                n = len(leaving)
                leaving.append(Leaving(kept[n], pltpu.make_async_copy(kept[n], results[i], rest[-1].at[len(staged) + n])))
                results[i] = leaving[-1]
        copies = []
        for i, v in enumerate(inputs):
            if not away[i]:
                continue
            n = len(copies)
            source = given[i]
            if v.array.ndim > 2 and v.shape == v.array.shape:
                pass
            elif v.array.ndim > 2:
                source = given[i].at[:, pl.ds(v.start, v.rows)]
            elif v.row is None and v.shape != v.array.shape:
                source = given[i].at[pl.ds(v.start, v.rows)]
            elif v.row is not None:
                source = given[i].at[pl.ds(pl.multiple_of(sc[v.row] * v.rows, v.rows), v.rows)]
            copies.append(Arriving(rest[n], pltpu.make_async_copy(source, rest[n], rest[-1].at[n])))
            given[i] = copies[-1]
        for v in copies:
            v.copy.start()
        if not lazy:
            for v in copies:
                v.here()
        body(sc, *given, *results, *own)
        for v in copies:
            v.here()
        leave(*leaving)
        for v in leaving:
            v.copy.wait()

    scratch_shapes = scratch + held + staged + [pltpu.SemaphoreType.DMA((max(len(staged) + len(held), 1),))]
    return pl.pallas_call(
        whole_body,
        out_shape=shapes,
        in_specs=[pl.BlockSpec(memory_space=pltpu.SMEM)] + specs,
        out_specs=[
            pl.BlockSpec(memory_space=pltpu.HBM) if b else whole_block(s.shape) for b, s in zip(back, shapes)
        ],
        grid=(1,),
        scratch_shapes=scratch_shapes,
        compiler_params=pltpu.CompilerParams(vmem_limit_bytes=vmem * 2**20),
        cost_estimate=pl.CostEstimate(flops=int(us * 1.15e9), bytes_accessed=0, transcendentals=0),
    )(scalars, *arrays)


def rows_at(start, count):
    return pl.ds(pl.multiple_of(start, count), count)


def row(ref):
    return ref[...].reshape(1, -1)


def normal_of(v):
    center = v - jnp.mean(v, axis=-1, keepdims=True)
    inverse = lax.rsqrt(jnp.mean(center * center, axis=-1, keepdims=True) + 1e-05)
    return center * inverse, inverse


def norm_back(gradient, normal, inverse, gain):
    scaled = gradient * gain
    adjusted = (
        scaled
        - jnp.mean(scaled, axis=-1, keepdims=True)
        - normal * jnp.mean(scaled * normal, axis=-1, keepdims=True)
    )
    return adjusted * inverse


def col_sum(v):
    return jnp.sum(v, axis=0, keepdims=True)


def set_places(sc):
    c, zh = sc[1], sc[2]
    return [2 * zh + c, 2 * (1 - zh) + c, 2 * zh + 1 - c, 2 * (1 - zh) + 1 - c]


def head_masks(width=256):
    lane = lax.broadcasted_iota(jnp.int32, (1, width), 1) // 64
    return [lane == h for h in range(4)]


def scalar_kernel(ids, tgt_len, src_len, pair_ids, loss_weights, out):
    for i in range(3):
        out[i] = ids[i]
    out[3] = tgt_len[ids[2]]
    out[4] = src_len[ids[2]]
    out[5] = loss_weights[pair_ids[ids[2]]]
    out[6] = ids[3]
    out[7] = ids[4]


VECTORS = ("first_gain", "first_shift", "self_output_bias", "second_gain", "second_shift")
VECTORS += ("cross_output_bias", "third_gain", "third_shift", "ffn_out_bias")


def vector(vecs, name):
    i = VECTORS.index(name)
    return vecs[i : i + 1, :]


def pack_kernel(sc, q, k, v, cq, ck, cv, o, co, qb, vb, cqb, cvb, fb, *refs):
    vectors, (one, wow, vecs) = refs[: len(VECTORS)], refs[len(VECTORS) :]
    for i, m in enumerate((q, k, v)):
        one[i * 64 : (i + 1) * 64, :] = m[...]
    for i, m in enumerate((cq, ck, cv)):
        one[208 + i * 64 : 272 + i * 64, :] = m[...]
    vec = jnp.concatenate([row(qb), row(vb), row(cqb), row(cvb), row(fb)], axis=1)
    high = vec.astype(BF).astype(F32)
    both = jnp.concatenate([high, vec - high], axis=1)
    first = lax.broadcasted_iota(jnp.int32, (16, 1024), 0) == 0
    one[192:208, :] = jnp.where(first, both, 0.0).astype(BF)
    wow[0:64, :] = o[...]
    wow[64:128, :] = co[...]
    for i, v in enumerate(vectors):
        vecs[i : i + 1, :] = row(v)
    vecs[len(VECTORS) : 16, :] = jnp.zeros((16 - len(VECTORS), 1024), F32)


def pack_more_kernel(sc, fin, fout, out):
    out[0:256, :] = fin[...].astype(F32).T.astype(BF)
    out[256:512, :] = fout[...]


def qkv_kernel(sc, t0, t1, t2, t3, vecs, a0, a1, a2, a3, first, tok, q, kv, w, bias):
    gain, shift = vector(vecs, "first_gain"), vector(vecs, "first_shift")
    for r, t in enumerate((t0, t1, t2, t3)):
        place = rows_at(lax.rem(sc[0] + r, 4) * 128, 128)
        tok[place, :] = t[...]
        normal, _ = normal_of(t[...].astype(F32))
        first[place, :] = (normal * gain + shift).astype(BF)
    for part, place in zip((a0, a1, a2, a3), set_places(sc)):
        for m in range(3):
            w[rows_at(m * 256 + place * 64, 64), :] = part[m * 64 : (m + 1) * 64, :]
        vec = part[192:208, :].astype(F32)[0:1, :]
        bias[pl.ds(place, 1), :] = vec[:, :512] + vec[:, 512:]
    x = first[...]

    def bias_of(i):
        return jnp.concatenate([bias[h : h + 1, i * 64 : (i + 1) * 64] for h in range(4)], axis=1)

    leave(first, tok, w, bias)
    kv[:, 0:256] = nt(x, w[256:512, :]).astype(BF)
    kv[:, 256:512] = (nt(x, w[512:768, :]) + bias_of(1)).astype(BF)
    leave(kv)
    q[...] = (SCALE * (nt(x, w[0:256, :]) + bias_of(0))).astype(BF)


def source_kernel(sc, mem, a0, a1, a2, a3, bias, ckv, w, own):
    for part, place in zip((a0, a1, a2, a3), set_places(sc)):
        for m in range(3):
            w[rows_at(m * 256 + place * 64, 64), :] = part[m * 64 : (m + 1) * 64, :]
    vb = jnp.concatenate([bias[h : h + 1, 192:256] for h in range(4)], axis=1)
    ckv[:, 0:256] = nt(mem[...], w[256:512, :]).astype(BF)
    ckv[:, 256:512] = (nt(mem[...], w[512:768, :]) + vb).astype(BF)
    for j in range(4):
        own[j * 128 : (j + 1) * 128, :] = mem[rows_at((2 * j + sc[1]) * 128, 128), :]


def key_bias(core, length, axis):
    k = lax.broadcasted_iota(jnp.int32, (1, 512) if axis == 1 else (512, 1), axis)
    position = ((k >> 7) * 2 + core) * 128 + (k & 127)
    return jnp.where(position < length, 0.0, NEG)


def diagonal_bias(key_core, query_core, transposed):
    q = lax.broadcasted_iota(jnp.int32, (256, 256), 1 if transposed else 0)
    k = lax.broadcasted_iota(jnp.int32, (256, 256), 0 if transposed else 1)
    q = ((q >> 7) * 2 + query_core) * 128 + (q & 127)
    k = ((k >> 7) * 2 + key_core) * 128 + (k & 127)
    return jnp.where(k <= q, 0.0, NEG)


def attend(q_rows, sources, biases):
    masks = head_masks()
    lane = lax.broadcasted_iota(jnp.int32, (1, 128), 1)
    count = q_rows.shape[0]
    mixed = jnp.zeros((count, 256), F32)
    totals = jnp.zeros((count, 128), F32)
    for h in range(4):
        qh = jnp.where(masks[h], q_rows, jnp.zeros_like(q_rows))
        scores = [nt(qh, k) + b for (k, _), b in zip(sources, biases)]
        top = functools.reduce(jnp.maximum, [jnp.max(s, axis=1, keepdims=True) for s in scores])
        raised = [jnp.exp(s - top) for s in scores]
        total = sum(jnp.sum(p, axis=1, keepdims=True) for p in raised)
        out = sum(nn(p.astype(BF), v) for p, (_, v) in zip(raised, sources))
        mixed = jnp.where(masks[h], out * (1.0 / total), mixed)
        totals = jnp.where(lane == h, top + jnp.log(total), totals)
    return mixed, totals


def causal_biases(sc, axis):
    c, length = sc[1], sc[3]
    transposed = axis == 0
    return (
        [key_bias(c, length, axis), key_bias(1 - c, length, axis)],
        [diagonal_bias(c, c, transposed), diagonal_bias(1 - c, c, transposed)],
    )


def pair_bias(length_bias, diagonal, a, axis):
    if axis == 1:
        last = length_bias[:, a * 256 : (a + 1) * 256] + diagonal
        if a == 0:
            return last
        return jnp.concatenate([jnp.broadcast_to(length_bias[:, 0:256], (256, 256)), last], axis=1)
    last = length_bias[a * 256 : (a + 1) * 256, :] + diagonal
    if a == 0:
        return last
    return jnp.concatenate([jnp.broadcast_to(length_bias[0:256, :], (256, 256)), last], axis=0)


def self_forward_kernel(sc, q, kvo, kvs, mixed, totals, stat):
    lengths, diagonals = causal_biases(sc, 1)
    for a in range(2):
        n = (a + 1) * 256
        sources = [(kvo[0:n, 0:256], kvo[0:n, 256:512]), (kvs[0:n, 0:256], kvs[0:n, 256:512])]
        biases = [pair_bias(lengths[i], diagonals[i], a, 1) for i in range(2)]
        out, total = attend(q[a * 256 : (a + 1) * 256, :], sources, biases)
        mixed[a * 256 : (a + 1) * 256, :] = out.astype(BF)
        stat[a * 256 : (a + 1) * 256, :] = total
    totals[...] = stat[...].T[0:8, :]


def cross_forward_kernel(sc, q, ckv, mixed, totals, stat):
    key = lax.broadcasted_iota(jnp.int32, (1, 1024), 1)
    bias = jnp.where(key < sc[4], 0.0, NEG)
    for a in range(2):
        out, total = attend(q[a * 256 : (a + 1) * 256, :], [(ckv[:, 0:256], ckv[:, 256:512])], [bias])
        mixed[a * 256 : (a + 1) * 256, :] = out.astype(BF)
        stat[a * 256 : (a + 1) * 256, :] = total
    totals[...] = stat[...].T[0:8, :]


def chip_rows(sc, whole, order):
    for r in range(4):
        chip = lax.rem(sc[0] + r, 4)
        for z in range(2):
            for core in range(2):
                place = r * 256 + z * 128 + core * 64
                order[place : place + 64, :] = whole[z * 8 + chip * 2 + core]


def set_rows(sc, sets, order):
    for r in range(4):
        chip = lax.rem(sc[0] + r, 4)
        for part, place in zip(sets, set_places(sc)):
            order[rows_at(r * 256 + place * 64, 64), :] = part[chip]


def second_kernel(
    sc, m0, m1, m2, m3, wo, tok, vecs, cw, bias, second, resid, cq, wo_own, order, work
):
    ob, gain, shift = (vector(vecs, n) for n in ("self_output_bias", "second_gain", "second_shift"))
    chip_rows(sc, wo, order)
    wo_own[...] = order[0:256, :]
    work[...] = nn(jnp.concatenate([m0[...], m1[...], m2[...], m3[...]], axis=1), order[...])
    for j in range(4):
        place = slice(j * 128, (j + 1) * 128)
        v = tok[place, :].astype(F32) + (work[place, :] + ob)
        resid[place, :] = v.astype(BF)
        normal, _ = normal_of(v)
        second[place, :] = (normal * gain + shift).astype(BF)
    leave(second, resid, wo_own)
    qb = jnp.concatenate([bias[h : h + 1, 128:192] for h in range(4)], axis=1)
    cq[...] = (SCALE * (nt(second[...], cw[0:256, :]) + qb)).astype(BF)


def upstream_kernel(sc, c0, c1, c2, c3, w0, w1, w2, w3, og, up):
    weight = 0.5 * sc[5].astype(F32)
    for r, t in enumerate((c0, c1, c2, c3)):
        chip = lax.rem(sc[0] + r, 4)
        position = (2 * chip + sc[1]) * 128 + lax.broadcasted_iota(jnp.int32, (128, 1), 0)
        og[rows_at(chip * 128, 128), :] = (t[...].astype(F32) * jnp.where(position < sc[3], weight, 0.0)).astype(BF)
    for s, w in enumerate((w0, w1, w2, w3)):
        up[:, s * 256 : (s + 1) * 256] = nt(og[...], w[...]).astype(BF)


def ffn_kernel(
    sc, m0, m1, m2, m3, wco, resid, vecs, up, w0, w1, w2, w3, bias,
    third, hidden, pre, back0, back1, back2, back3, own, wco_own, order, work,
):
    y = sc[0]
    ob, gain, shift = (vector(vecs, n) for n in ("cross_output_bias", "third_gain", "third_shift"))
    chip_rows(sc, wco, order)
    wco_own[...] = order[0:256, :]
    work[...] = nn(jnp.concatenate([m0[...], m1[...], m2[...], m3[...]], axis=1), order[...])
    for s, w in enumerate((w0, w1, w2, w3)):
        order[s * 256 : (s + 1) * 256, :] = w[...]
    for j in range(4):
        place = slice(j * 128, (j + 1) * 128)
        v = resid[place, :].astype(F32) + (work[place, :] + ob)
        work[place, :] = v
        normal, _ = normal_of(v)
        third[place, :] = (normal * gain + shift).astype(BF)
    own[...] = work[rows_at(y * 128, 128), :]
    leave(third, own, wco_own)
    places = set_places(sc)
    for s in range(4):
        cols = slice(s * 256, (s + 1) * 256)
        u = nt(third[...], order[cols, :]) + bias[pl.ds(places[s], 1), 256:512]
        square = u * u
        t = jnp.tanh(0.7978845608028654 * (u + 0.044715 * (square * u)))
        hidden[:, cols] = (0.5 * u * (1.0 + t)).astype(BF)
        slope = 0.5 * (1.0 + t) + 0.5 * u * (1.0 - t * t) * (0.7978845608028654 * (1.0 + 0.134145 * square))
        pre[:, cols] = (up[:, cols].astype(F32) * slope).astype(BF)
    leave(hidden, pre)
    store_rel(sc, nn(pre[...], order[...]), work, (back0, back1, back2, back3))


def store_rel(sc, value, work, outs):
    work[...] = value
    for r, out in enumerate(outs):
        out[...] = work[rows_at(lax.rem(sc[0] + r, 4) * 128, 128), :].astype(BF)


def total_of(parts):
    p = [v[...].astype(F32) for v in parts]
    return (p[0] + p[1]) + (p[2] + p[3])


def late_rows_kernel(sc, p0, p1, p2, p3, own, vecs, out, mem):
    total = total_of((p0, p1, p2, p3))
    out[...] = (own[...] + (total[0:128, :] + vector(vecs, "ffn_out_bias"))).astype(BF)
    mem[...] = total[128:256, :]


def split_rows(values):
    high = values.astype(BF).astype(F32)
    return jnp.concatenate([high, values - high, jnp.zeros((12, values.shape[1]), F32)], axis=0).astype(BF)


def joined_rows(block):
    f = block.astype(F32)
    return f[0:2, :] + f[2:4, :]


def third_grad_kernel(sc, p0, p1, p2, p3, own, cot, vecs, grad, low):
    position = (2 * sc[0] + sc[1]) * 128 + lax.broadcasted_iota(jnp.int32, (128, 1), 0)
    og = cot[...].astype(F32) * jnp.where(position < sc[3], 0.5 * sc[5].astype(F32), 0.0)
    back = total_of((p0, p1, p2, p3))
    normal, inverse = normal_of(own[...])
    total = og + norm_back(back, normal, inverse, vector(vecs, "third_gain"))
    grad[...] = total
    low[0:128, :] = total.astype(BF)
    low[128:144, :] = split_rows(jnp.concatenate([col_sum(back * normal), col_sum(back)], axis=0))


def masked_stack(v, stack):
    masks = head_masks()
    for a in range(2):
        rows = v[a * 256 : (a + 1) * 256, :]
        for h in range(4):
            stack[a, h * 256 : (h + 1) * 256, :] = jnp.where(masks[h], rows, jnp.zeros_like(rows))


def delta_of(mixed, grad):
    head = lax.broadcasted_iota(jnp.int32, (8, 256), 0)
    lane = lax.broadcasted_iota(jnp.int32, (8, 256), 1) // 64
    ones = jnp.where(head == lane, 1.0, 0.0)
    product = mixed.astype(F32) * grad.astype(F32)
    return lax.dot_general(
        ones, product, (((1,), (1,)), ((), ())), preferred_element_type=F32, precision=lax.Precision.HIGHEST
    )


def pair_backward(a, q_stack, g_stack, totals, delta, keys, values, keys_t, bias, probs, scores):
    cols = slice(a * 256, (a + 1) * 256)
    dq = []
    for h in range(4):
        place = slice(h * 256, (h + 1) * 256)
        qh, gh = q_stack[a, place, :], g_stack[a, place, :]
        for k in range(keys.shape[0] // 256):
            some = slice(k * 256, (k + 1) * 256)
            s = nt(keys[some, :], qh) + bias[some, :]
            p = jnp.exp(s - totals[h : h + 1, cols])
            ds = (p * (nt(values[some, :], gh) - delta[h : h + 1, cols])).astype(BF)
            probs[some, place] = p.astype(BF)
            scores[some, place] = ds
        dq.append(nn(keys_t[h * 64 : (h + 1) * 64, :], scores[:, place]))
    return jnp.concatenate(dq, axis=0)


def cross_backward_kernel(
    sc, t0, t1, t2, t3, wco, cq, ckv, mixed, totals, og, tg, dq, own, other, vec,
    q_stack, g_stack, probs, scores, delta, part,
):
    norm_sums = jnp.zeros((2, 1024), F32)
    for r, t in enumerate((t0, t1, t2, t3)):
        tg[rows_at(lax.rem(sc[0] + r, 4) * 128, 128), :] = t[0:128, :]
        norm_sums = norm_sums + joined_rows(t[128:144, :])
    vec[0:2, :] = norm_sums
    vec[2:3, :] = col_sum(og[...].astype(F32))
    vec[3:4, :] = col_sum(tg[...].astype(F32))
    vec[4:8, :] = jnp.zeros((4, 1024), F32)
    leave(tg, vec)
    g = nt(tg[...], wco[...]).astype(BF)
    delta[...] = delta_of(mixed[...], g)
    masked_stack(g, g_stack)
    masked_stack(cq[...], q_stack)
    key = lax.broadcasted_iota(jnp.int32, (1024, 1), 0)
    bias = jnp.where(key < sc[4], 0.0, NEG)
    keys_t = ckv[:, 0:256].T
    for a in range(2):
        grad = pair_backward(
            a, q_stack, g_stack, totals, delta, ckv[:, 0:256], ckv[:, 256:512], keys_t, bias, probs.at[a], scores.at[a]
        )
        dq[a * 256 : (a + 1) * 256, :] = grad.T.astype(BF)
    leave(dq)
    part[:, 0:256] = nn(scores[0], q_stack[0]) + nn(scores[1], q_stack[1])
    part[:, 256:512] = nn(probs[0], g_stack[0]) + nn(probs[1], g_stack[1])
    for j in range(4):
        place = slice(j * 128, (j + 1) * 128)
        own[place, :] = part[rows_at((2 * j + sc[1]) * 128, 128), :].astype(BF)
        other[place, :] = part[rows_at((2 * j + 1 - sc[1]) * 128, 128), :].astype(BF)


def second_grad_kernel(
    sc, d0, d1, d2, d3, a0, a1, a2, a3, resid, vecs, tg, tg_own, wo,
    low, grad_own, g, vec, order, work,
):
    gain = vector(vecs, "second_gain")
    set_rows(sc, (a0, a1, a2, a3), order)
    work[...] = nn(jnp.concatenate([d0[...], d1[...], d2[...], d3[...]], axis=1), order[...])
    sums = [jnp.zeros((1, 1024), F32)] * 3
    for j in range(4):
        place = slice(j * 128, (j + 1) * 128)
        normal, inverse = normal_of(resid[place, :].astype(F32))
        back = SCALE * work[place, :]
        v = norm_back(back, normal, inverse, gain)
        work[place, :] = v
        rounded = (tg[place, :].astype(F32) + v).astype(BF)
        low[place, :] = rounded
        for i, add in enumerate((back * normal, back, rounded.astype(F32))):
            sums[i] = sums[i] + col_sum(add)
    leave(low)
    g[...] = nt(low[...], wo[...]).astype(BF)
    leave(g)
    grad_own[...] = tg_own[...] + work[rows_at(sc[0] * 128, 128), :]
    vec[...] = jnp.concatenate(sums + [jnp.zeros((5, 1024), F32)], axis=0)


def self_backward_kernel(
    sc, g, q, kvo, kvs, mixed, totals, dq, own, other, q_stack, g_stack, p0, s0, p1, s1, delta
):
    delta[...] = delta_of(mixed[...], g[...])
    masked_stack(g[...], g_stack)
    masked_stack(q[...], q_stack)
    lengths, diagonals = causal_biases(sc, 0)
    keys_t = [kv[:, 0:256].T for kv in (kvo, kvs)]
    for a in range(2):
        n = (a + 1) * 256
        probs, scores = ((p0, s0), (p1, s1))[a]
        grad = jnp.zeros((256, 256), F32)
        for i, kv in enumerate((kvo, kvs)):
            bias = pair_bias(lengths[i], diagonals[i], a, 0)
            grad = grad + pair_backward(
                a, q_stack, g_stack, totals, delta, kv[0:n, 0:256], kv[0:n, 256:512], keys_t[i][:, 0:n], bias,
                probs.at[i], scores.at[i],
            )
        dq[a * 256 : (a + 1) * 256, :] = grad.T.astype(BF)
    leave(dq)
    for i, out in ((1, other), (0, own)):
        kind = out.dtype
        for cols, first, second, stack in (
            (slice(0, 256), s0, s1, q_stack),
            (slice(256, 512), p0, p1, g_stack),
        ):
            out[0:256, cols] = (nn(first[i], stack[0]) + nn(second[i, 0:256, :], stack[1])).astype(kind)
            out[256:512, cols] = nn(second[i, 256:512, :], stack[1]).astype(kind)
        leave(out)


def first_back_kernel(sc, dq, dkv, w, b0, b1, b2, b3, work):
    part = SCALE * nn(dq[...], w[0:256, :]) + nn(dkv[:, 0:256], w[256:512, :]) + nn(dkv[:, 256:512], w[512:768, :])
    store_rel(sc, part, work, (b0, b1, b2, b3))


def tokens_grad_kernel(sc, p0, p1, p2, p3, tokens, vecs, grad, out):
    normal, inverse = normal_of(tokens[...].astype(F32))
    out[...] = grad[...] + norm_back(
        total_of((p0, p1, p2, p3)), normal, inverse, vector(vecs, "first_gain")
    )


def memory_back_kernel(sc, grad, w, hidden, w0, w1, w2, w3, b0, b1, b2, b3, order, work):
    outs = (b0, b1, b2, b3)
    for s, part in enumerate((w0, w1, w2, w3)):
        order[s * 256 : (s + 1) * 256, :] = part[...]
    store_rel(sc, nn(hidden[...], order[...]), work, [b.at[0:128] for b in outs])
    value = nn(grad[:, 0:256], w[0:256, :]) + nn(grad[:, 256:512], w[256:512, :])
    store_rel(sc, value, work, [b.at[128:256] for b in outs])


def store_pieces(out, z, start, block):
    for i in range(8):
        out[i, z, start : start + block.shape[0], :] = block[:, i * 128 : (i + 1) * 128].astype(BF)


def store_bias(out, z, start, values, vectors=()):
    wide = jnp.concatenate([values, jnp.zeros((1, 1024 - values.shape[1]), F32)], axis=1)
    rows = [wide] + list(vectors)
    rows.append(jnp.zeros((16 - sum(v.shape[0] for v in rows), 1024), F32))
    store_pieces(out, z, start, jnp.concatenate(rows, axis=0))


def ffn_weight_kernel(sc, pre, third, hidden, og, keep, send):
    zh = sc[2]
    for s in range(4):
        out = keep if s < 2 else send
        z = zh if s % 2 == 0 else 1 - zh
        cols = slice(s * 256, (s + 1) * 256)
        store_pieces(out, z, 0, tn(pre[:, cols], third[...]))
        store_pieces(out, z, 256, tn(hidden[:, cols], og[...]))
        store_bias(out, z, 512, col_sum(pre[:, cols].astype(F32)))


def cross_weight_kernel(sc, own, other, mixed, tg, dq, second, mem, vec, dkv, keep, send, product):
    dkv[...] = (own[...].astype(F32) + other[...].astype(F32)).astype(BF)
    leave(dkv)
    sides = ((keep, sc[1]), (send, 1 - sc[1]))
    ones = jnp.ones((8, 512), BF)
    q_bias = SCALE * nn(ones, dq[...])[0:1, :]
    v_bias = nn(ones, dkv[:, 256:512])[0:1, :]
    for m in range(4):
        if m == 0:
            product[...] = tn(mixed[...], tg[...])
        elif m == 1:
            product[...] = SCALE * tn(dq[...], second[...])
        else:
            product[...] = tn(dkv[:, (m - 2) * 256 : (m - 1) * 256], mem[...])
        for z in range(2):
            for out, core in sides:
                store_pieces(out, z, m * 64, product[rows_at((2 * z + core) * 64, 64), :])
    for z in range(2):
        for out, core in sides:
            store_head_bias(out, z, core, q_bias, v_bias, [vec[0:4, :]])


def store_head_bias(out, z, core, q_bias, v_bias, vectors):
    rows = [
        jnp.concatenate([v[:, s * 64 : (s + 1) * 64] for v in (q_bias, v_bias)], axis=1) for s in (2 * z, 2 * z + 1)
    ]
    store_bias(out, z, 256, jnp.where(core == 0, rows[0], rows[1]), vectors)


def self_weight_kernel(sc, dq, own, other, tok, w, mixed, sg, vecs, vec2, dkv, keep, send, vec, normal, product):
    gain, shift = vector(vecs, "first_gain"), vector(vecs, "first_shift")
    dkv[...] = (own[...].astype(F32) + other[...].astype(F32)).astype(BF)
    leave(dkv)
    for j in range(4):
        place = slice(j * 128, (j + 1) * 128)
        normal[place, :] = normal_of(tok[place, :].astype(F32))[0].astype(BF)
    ones = jnp.ones((8, 512), BF)
    gain_sum = jnp.zeros((1, 1024), F32)
    shift_sum = jnp.zeros((1, 1024), F32)
    q_bias = v_bias = None
    for m, (grad, factor) in enumerate(((dq[...], SCALE), (dkv[:, 0:256], 1.0), (dkv[:, 256:512], 1.0))):
        sums = factor * tn(grad, ones.T)[:, 0:1]
        product[...] = factor * tn(grad, normal[...])
        weight = w[m * 256 : (m + 1) * 256, :].astype(F32)
        gain_sum = gain_sum + col_sum(weight * product[...])
        shift_sum = shift_sum + col_sum(weight * sums)
        total = product[...] * gain + sums * shift
        product[...] = total
        for z in range(2):
            for out, core in ((keep, sc[1]), (send, 1 - sc[1])):
                store_pieces(out, z, (m + 1) * 64, product[rows_at((2 * z + core) * 64, 64), :])
        if m != 1:
            flat = factor * nn(ones, grad)[0:1, :]
            if m == 0:
                q_bias = flat
            else:
                v_bias = flat
    sums_rows = split_rows(jnp.concatenate([gain_sum, shift_sum], axis=0))[0:4, :].astype(F32)
    product[...] = tn(mixed[...], sg[...])
    for z in range(2):
        for out, core in ((keep, sc[1]), (send, 1 - sc[1])):
            store_pieces(out, z, 0, product[rows_at((2 * z + core) * 64, 64), :])
            store_head_bias(out, z, core, q_bias, v_bias, [vec2[0:3, :], sums_rows])
    vec[...] = jnp.concatenate([gain_sum, shift_sum, jnp.zeros((6, 1024), F32)], axis=0)


def add_kernel(sc, *refs):
    out, start = refs[-1], 0
    for a, b in zip(refs[:-1:2], refs[1:-1:2]):
        rows = a.shape[2]
        for i in range(8):
            out[i, :, start : start + rows, :] = (a[i].astype(F32) + b[i].astype(F32)).astype(BF)
        start += rows


def piece_sum(got):
    total = got[0].astype(F32)
    for i in range(1, 16):
        total = total + got[i].astype(F32)
    return total.astype(BF)


def sum_kernel(sc, ffn, cross, out):
    out[0:528, :] = piece_sum(ffn)
    out[528:800, :] = piece_sum(cross)


def spread_kernel(sc, *refs):
    start, out = 0, refs[-1]
    for got in refs[:-1]:
        total = piece_sum(got) if len(got.shape) == 3 else got[...]
        rows = total.shape[0]
        for i in range(8):
            out[i, start : start + rows, :] = total
        start += rows


def ffn_result(got, start, fin, fout, fb):
    for i in range(8):
        fout[:, i * 128 : (i + 1) * 128] = got[i, start + 256 : start + 512, :].astype(F32)
    leave(fout)
    for i in range(8):
        fin[i * 128 : (i + 1) * 128, :] = got[i, start : start + 256, :].astype(F32).T
    leave(fin)
    rows = [got[i, start + 512 : start + 528, :].astype(F32)[0:1, :] for i in range(2)]
    fb[...] = jnp.concatenate(rows, axis=1).reshape(256)


def result_kernel(sc, got, v1, v2, v3, *outs):
    ffn_result(got, 272, *outs[:3])
    heads_result(3, 0, got, *outs[3:12])
    heads_result(4, 800, got, *outs[12:22])
    total = sum(jnp.concatenate([v[i].astype(F32) for i in range(8)], axis=1) for v in (v1, v2, v3))
    total = total + jnp.concatenate([got[i, 256:272, :].astype(F32) for i in range(8)], axis=1)
    outs[22][...] = (total[4:5, :] + total[6:7, :]).reshape(1024)
    outs[23][...] = (total[5:6, :] + total[7:8, :]).reshape(1024)


def heads_result(count, start, got, o, q, k, v, qb, vb, *vectors):
    for m, out in enumerate((o, q, k, v)):
        for i in range(8):
            out[:, i * 128 : (i + 1) * 128] = got[i, start + m * 64 : start + (m + 1) * 64, :].astype(F32)
        leave(out)
    rows = jnp.concatenate([got[i, start + 256 : start + 272, :].astype(F32) for i in range(8)], axis=1)
    qb[...] = rows[0:1, 0:64].reshape(64)
    vb[...] = rows[0:1, 64:128].reshape(64)
    for i in range(count):
        vectors[i][...] = rows[i + 1 : i + 2, :].reshape(1024)


def core_sum(sc, *pairs, us=4.8):
    rows = sum(keep.shape[2] for keep, _ in pairs)
    return run((add_kernel, us), [((8, 2, rows, 128), BF)], sc, far(*[v for pair in pairs for v in pair]), vmem=44)[0]


def pieces(both):
    return exchange(both.reshape((16,) + both.shape[2:]), ("x", "zl", "zh"))


def per_device(
    tokens,
    memory,
    cotangent,
    tgt_len,
    src_len,
    pair_ids,
    loss_weights,
    first_gain,
    first_shift,
    self_query,
    self_query_bias,
    self_key,
    self_value,
    self_value_bias,
    self_output,
    self_output_bias,
    second_gain,
    second_shift,
    cross_query,
    cross_query_bias,
    cross_key,
    cross_value,
    cross_value_bias,
    cross_output,
    cross_output_bias,
    third_gain,
    third_shift,
    ffn_in,
    ffn_in_bias,
    ffn_out,
    ffn_out_bias,
):
    ids = jnp.stack([lax.axis_index("y"), lax.axis_index("c"), lax.axis_index("zh")] + [lax.axis_index("x"), lax.axis_index("zl")]).astype(jnp.int32)
    sc = pl.pallas_call(
        scalar_kernel,
        out_shape=jax.ShapeDtypeStruct((8,), jnp.int32),
        in_specs=[pl.BlockSpec(memory_space=pltpu.SMEM)] * 5,
        out_specs=pl.BlockSpec(memory_space=pltpu.SMEM),
    )(ids, tgt_len, src_len, pair_ids, loss_weights)

    def after(v, *others):
        return lax.optimization_barrier((v,) + others)[0]

    nothing = jnp.zeros((8,), jnp.int32)

    tok_blocks = gather_rel(tokens)
    given = {
        "first_gain": first_gain,
        "first_shift": first_shift,
        "self_output_bias": self_output_bias,
        "second_gain": second_gain,
        "second_shift": second_shift,
        "cross_output_bias": cross_output_bias,
        "third_gain": third_gain,
        "third_shift": third_shift,
        "ffn_out_bias": ffn_out_bias,
    }
    one, wow, vecs = run(
        (pack_kernel, 3.3),
        [((400, 1024), BF), ((128, 1024), BF), ((16, 1024), F32)],
        nothing,
        far(self_query.T, self_key.T, self_value.T, cross_query.T, cross_key.T, cross_value.T)
        + far(self_output, cross_output)
        + [self_query_bias, self_value_bias, cross_query_bias, cross_value_bias, ffn_in_bias]
        + [given[n] for n in VECTORS],
        vmem=60,
    )
    one_half = from_half(one)
    one_core = from_core(one)
    (more,) = run(
        (pack_more_kernel, 3),
        [((512, 1024), BF)],
        sc,
        far(ffn_in, ffn_out),
        vmem=60,
    )
    whole_wow = lax.all_gather(wow, ("zh", "y", "c"), axis=0, tiled=True)
    wide = jnp.concatenate([one[208:272], one_half[208:272]], axis=0)
    query_own = lax.all_gather(after(wide, whole_wow), "y", axis=0, tiled=True)
    query_core = from_core(query_own)
    query_sets = [(query_own, 0), (query_own, 64), (query_core, 0), (query_core, 64)]
    one_core_half = from_core(after(one_half, more, *tok_blocks))

    def one_parts(start, rows):
        return [Far(v, start, rows) for v in (one, one_half, one_core, one_core_half)]

    first, tok, q, kv, w, bias = run(
        (qkv_kernel, 5.3),
        [((512, 1024), BF), ((512, 1024), BF), ((512, 256), BF), ((512, 512), BF), ((768, 1024), BF), ((4, 512), F32)],
        sc,
        far(*tok_blocks, vecs) + one_parts(0, 208),
        lazy=True,
    )
    kvs = from_core(kv)
    self_mixed, self_totals = run(
        (self_forward_kernel, 5.8),
        [((512, 256), BF), ((8, 512), F32)],
        sc,
        far(q, kv, kvs),
        [pltpu.VMEM((512, 128), F32)],
    )
    mixed_blocks = gather_rel(self_mixed)
    more_half = from_half(after(more, self_mixed))
    cot_blocks = gather_rel(after(cotangent, *mixed_blocks))
    more_core = from_core(after(more, self_mixed))

    ckv, cw, mem_own = run(
        (source_kernel, 6),
        [((1024, 512), BF), ((768, 1024), BF), ((512, 1024), BF)],
        sc,
        [Far(memory, 0, 1024, row=2)] + one_parts(208, 192) + [Far(after(bias, wide))],
    )
    second, resid, cq, wo_own = run(
        (second_kernel, 8),
        [((512, 1024), BF), ((512, 1024), BF), ((512, 256), BF), ((256, 1024), BF)],
        sc,
        far(*mixed_blocks) + [Far(whole_wow, 0, 64, block=128)] + far(tok, vecs) + [Far(cw, 0, 256), Far(bias)],
        [pltpu.VMEM((1024, 1024), BF), pltpu.VMEM((512, 1024), F32)],
        lazy=True,
    )
    cross_mixed, cross_totals = run(
        (cross_forward_kernel, 6),
        [((512, 256), BF), ((8, 512), F32)],
        sc,
        far(after(cq, *cot_blocks), ckv),
        [pltpu.VMEM((512, 128), F32)],
    )
    cross_blocks = gather_rel(cross_mixed)
    more_core_half = from_core(after(more_half, cross_mixed))

    def more_parts(start, rows):
        return [Far(v, start, rows) for v in (more, more_half, more_core, more_core_half)]

    og, up = run(
        (upstream_kernel, 5),
        [((512, 1024), BF), ((512, 1024), BF)],
        sc,
        far(*cot_blocks) + more_parts(256, 256),
    )
    rows_out = [((128, 1024), BF)] * 4
    third, hidden, pre, b0, b1, b2, b3, resid_own, wco_own = run(
        (ffn_kernel, 11.5),
        [((512, 1024), BF)] * 3 + rows_out + [((128, 1024), F32), ((256, 1024), BF)],
        sc,
        far(*cross_blocks) + [Far(whole_wow, 64, 64, block=128)] + far(resid, vecs, up) + more_parts(0, 256) + [Far(bias)],
        [pltpu.VMEM((1024, 1024), BF), pltpu.VMEM((512, 1024), F32)],
    )
    third_parts = scatter_rel([b0, b1, b2, b3])
    ffn_keep, ffn_send = run(
        (ffn_weight_kernel, 7),
        [((8, 2, 528, 128), BF)] * 2,
        sc,
        far(pre, third, hidden, og),
        lazy=True,
    )
    third_grad, third_low = run(
        (third_grad_kernel, 20),
        [((128, 1024), F32), ((144, 1024), BF)],
        sc,
        far(*third_parts, resid_own, cotangent, vecs), vmem=44)
    tg_blocks = gather_rel(third_low)
    ffn_both = core_sum(sc, (ffn_keep, from_core(ffn_send)))

    tg, cdq, ckv_own, ckv_other, third_vec = run(
        (cross_backward_kernel, 1.5),
        [((512, 1024), BF), ((512, 256), BF), ((512, 512), BF), ((512, 512), BF), ((8, 1024), F32)],
        sc,
        far(*tg_blocks, wco_own, cq, ckv, cross_mixed, after(cross_totals, ffn_both, query_core), og),
        [
            pltpu.VMEM((2, 1024, 256), BF),
            pltpu.VMEM((2, 1024, 256), BF),
            pltpu.VMEM((2, 1024, 1024), BF),
            pltpu.VMEM((2, 1024, 1024), BF),
            pltpu.VMEM((8, 512), F32),
            pltpu.VMEM((1024, 512), F32),
        ],
    )
    cdq_blocks = gather_rel(cdq)
    ckv_got = from_core(ckv_other)
    ckv_grad, cross_keep, cross_send = run(
        (cross_weight_kernel, 1.5),
        [((512, 512), BF)] + [((8, 2, 272, 128), BF)] * 2,
        sc,
        far(ckv_own, ckv_got, cross_mixed, tg, cdq, second, mem_own, third_vec),
        [pltpu.VMEM((256, 1024), F32)],
    )
    cross_both = core_sum(sc, (cross_keep, from_core(cross_send)), us=1.5)
    ffn_pieces = pieces(ffn_both)
    cross_pieces = pieces(after(cross_both, ffn_pieces))
    sg, second_grad, self_grad, second_vec = run(
        (second_grad_kernel, 8.5),
        [((512, 1024), BF), ((128, 1024), F32), ((512, 256), BF), ((8, 1024), F32)],
        sc,
        far(*cdq_blocks) + [Far(v, s, 64, block=128) for v, s in query_sets] + far(resid, vecs, tg, third_grad, after(wo_own, cross_both, ffn_pieces)),
        [pltpu.VMEM((1024, 1024), BF), pltpu.VMEM((512, 1024), F32)],
    )

    dq, kv_own, kv_other = run(
        (self_backward_kernel, 12),
        [((512, 256), BF), ((512, 512), BF), ((512, 512), BF)],
        sc,
        far(self_grad, q, kv, kvs, self_mixed, self_totals),
        [
            pltpu.VMEM((2, 1024, 256), BF),
            pltpu.VMEM((2, 1024, 256), BF),
            pltpu.VMEM((2, 256, 1024), BF),
            pltpu.VMEM((2, 256, 1024), BF),
            pltpu.VMEM((2, 512, 1024), BF),
            pltpu.VMEM((2, 512, 1024), BF),
            pltpu.VMEM((8, 512), F32),
        ],
    )
    kv_got = from_core(kv_other)
    dkv, self_keep, self_send, first_vec = run(
        (self_weight_kernel, 8),
        [((512, 512), BF), ((8, 2, 272, 128), BF), ((8, 2, 272, 128), BF), ((8, 1024), F32)],
        sc,
        far(dq, kv_own, kv_got, after(tok, cross_pieces), w, self_mixed, sg, vecs, second_vec),
        [pltpu.VMEM((512, 1024), BF), pltpu.VMEM((256, 1024), F32)],
    )
    self_recv = from_core(self_send)
    late_part = run(
        (memory_back_kernel, 2),
        [((256, 1024), BF)] * 4,
        sc,
        far(after(ckv_grad, self_recv)) + [Far(cw, 256, 512), Far(hidden)] + more_parts(256, 256),
        [pltpu.VMEM((1024, 1024), BF), pltpu.VMEM((512, 1024), F32)],
    )
    late_parts = scatter_rel(late_part)
    self_both = core_sum(sc, (self_keep, self_recv))
    (early_piece,) = run(
        (sum_kernel, 2), [((800, 128), BF)], sc, far(after(ffn_pieces, self_both), cross_pieces)
    )
    (copies,) = run(
        (spread_kernel, 4), [((8, 1072, 128), BF)], sc, far(after(pieces(self_both), late_part[0]), early_piece)
    )
    got = exchange(copies, ("x", "zl"))
    first_part = run(
        (first_back_kernel, 2),
        rows_out,
        sc,
        far(dq, after(dkv, copies), w),
        [pltpu.VMEM((512, 1024), F32)],
    )
    first_parts = scatter_rel(first_part)
    (tokens_grad,) = run(
        (tokens_grad_kernel, 15), [((128, 1024), F32)], sc, far(*first_parts, tokens, vecs, second_grad)
    )
    block_out, memory_grad = run(
        (late_rows_kernel, 15), [((128, 1024), BF), ((128, 1024), F32)], sc, far(*late_parts, resid_own, vecs)
    )
    got = after(got, block_out, tokens_grad)
    first_sums = gather_rel(got[:, 256:272, :])
    heads_out = [((64, 1024), F32)] * 4 + [((64,), F32)] * 2
    heads_out = heads_out + [((1024,), F32)] * 3 + heads_out + [((1024,), F32)] * 4
    heads_out = [((1024, 256), F32), ((256, 1024), F32), ((256,), F32)] + heads_out + [((1024,), F32)] * 2
    ffn_in_grad, ffn_out_grad, ffn_in_bias_grad, *outs = run(
        (result_kernel, 7), heads_out, sc, far(got, *first_sums[1:])
    )
    self_out, cross_out = outs[:9], outs[9:]
    return (
        block_out,
        tokens_grad,
        memory_grad,
        outs[19],
        outs[20],
        self_out[1].T,
        self_out[4],
        self_out[2].T,
        self_out[3].T,
        self_out[5],
        self_out[0],
        self_out[8],
        self_out[6],
        self_out[7],
        cross_out[1].T,
        cross_out[4],
        cross_out[2].T,
        cross_out[3].T,
        cross_out[5],
        cross_out[0],
        cross_out[9],
        cross_out[6],
        cross_out[7],
        ffn_in_grad,
        ffn_in_bias_grad,
        ffn_out_grad,
        cross_out[8],
    )


def solution(mesh):
    fine = Mesh(mesh.devices.reshape(4, 2, 2, 4, 2), ("x", "zl", "zh", "y", "c"))
    dp = ("x", "zl")
    mp = ("zh", "y", "c")
    rows, cols, part, down, whole = P(dp + mp, None), P(None, mp), P(mp), P(mp, None), P()
    placed = (rows, P(dp, None), rows, P(dp), P(dp), P(dp), whole, whole, whole)
    placed += (cols, part, cols, cols, part, down, whole, whole, whole)
    placed += (cols, part, cols, cols, part, down, whole, whole, whole)
    placed += (cols, part, down, whole)
    attention = (cols, part, cols, cols, part, down, whole)
    given = (rows, rows, rows, whole, whole) + attention + (whole, whole) + attention + (whole, whole)
    given += (cols, part, down, whole)
    return jax.shard_map(per_device, mesh=fine, in_specs=placed, out_specs=given, check_vma=False)
```

```python
import functools

import jax
import jax.numpy as jnp
from jax import lax
from jax.experimental import pallas as pl
from jax.experimental.pallas import tpu as pltpu
from jax.sharding import Mesh, PartitionSpec as P

BF = jnp.bfloat16
F32 = jnp.float32
NEG = -1e30
SCALE = 0.125


def nn(a, b):
    return jnp.dot(a, b, preferred_element_type=F32)


def nt(a, b):
    return lax.dot_general(a, b, (((1,), (1,)), ((), ())), preferred_element_type=F32)


def tn(a, b):
    return lax.dot_general(a, b, (((0,), (0,)), ((), ())), preferred_element_type=F32)


def ring(n, k):
    return [(i, (i + k) % n) for i in range(n)]


def from_core(v):
    return lax.ppermute(v, "c", ring(2, 1))


def from_half(v):
    return lax.ppermute(v, ("zl", "zh"), [(i, 3 - i) for i in range(4)])


def gather_rel(v):
    return [v] + [lax.ppermute(v, "y", ring(4, 4 - r)) for r in range(1, 4)]


def scatter_rel(blocks):
    return [blocks[0]] + [lax.ppermute(blocks[r], "y", ring(4, r)) for r in range(1, 4)]


def exchange(v, axes):
    return lax.all_to_all(v, axes, 0, 0)


class Far:
    def __init__(self, array, start=0, rows=None, row=None, block=None):
        self.array = array
        self.row = row
        self.block = block
        self.start = start
        self.rows = array.shape[0] if rows is None else rows
        self.shape = (self.rows,) + array.shape[1:]
        if array.ndim > 2:
            self.shape = array.shape if rows is None else (array.shape[0], rows) + array.shape[2:]
        if block is not None:
            self.array = array.reshape((array.shape[0] // block, block) + array.shape[1:])
            self.shape = (array.shape[0] // block,) + self.shape


def far(*arrays):
    return [Far(v) for v in arrays]


class Arriving:
    def __init__(self, ref, copy):
        self.ref = ref
        self.copy = copy
        self.shape = ref.shape

    def here(self):
        if self.copy is not None:
            self.copy.wait()
            self.copy = None
        return self.ref

    def __getitem__(self, index):
        return self.here()[index]


class Leaving:
    def __init__(self, ref, copy):
        self.ref = ref
        self.copy = copy
        self.started = False
        self.shape = ref.shape
        self.dtype = ref.dtype

    def __getitem__(self, index):
        return self.ref[index]

    def __setitem__(self, index, value):
        assert not self.started
        self.ref[index] = value

    @property
    def at(self):
        return self.ref.at

    def leave(self):
        if not self.started:
            self.started = True
            self.copy.start()


def leave(*refs):
    for ref in refs:
        ref.leave()


def whole_block(shape):
    return pl.BlockSpec(shape, lambda i: (0,) * len(shape), pipeline_mode=pl.Buffered(1))


def run(kernel, outs, scalars, inputs, scratch=(), vmem=60, lazy=False):
    body, us = kernel
    away = [isinstance(v, Far) for v in inputs]
    specs = [pl.BlockSpec(memory_space=pltpu.HBM) if a else whole_block(v.shape) for a, v in zip(away, inputs)]
    arrays = [v.array if a else v for a, v in zip(away, inputs)]
    staged = [pltpu.VMEM(v.shape, v.array.dtype) for a, v in zip(away, inputs) if a]
    shapes = [jax.ShapeDtypeStruct(s, d) for s, d in outs]
    back = [len(s) > 1 for s, _ in outs]
    held = [pltpu.VMEM(s, d) for (s, d), b in zip(outs, back) if b]
    scratch = list(scratch)

    def whole_body(sc, *refs):
        count = len(inputs)
        given, rest = list(refs[:count]), refs[count:]
        results, rest = list(rest[: len(outs)]), rest[len(outs) :]
        own, rest = rest[: len(scratch)], rest[len(scratch) :]
        kept, rest = rest[: len(held)], rest[len(held) :]
        leaving = []
        for i in range(len(outs)):
            if back[i]:
                n = len(leaving)
                leaving.append(Leaving(kept[n], pltpu.make_async_copy(kept[n], results[i], rest[-1].at[len(staged) + n])))
                results[i] = leaving[-1]
        copies = []
        for i, v in enumerate(inputs):
            if not away[i]:
                continue
            n = len(copies)
            source = given[i]
            if v.array.ndim > 2 and v.shape == v.array.shape:
                pass
            elif v.array.ndim > 2:
                source = given[i].at[:, pl.ds(v.start, v.rows)]
            elif v.row is None and v.shape != v.array.shape:
                source = given[i].at[pl.ds(v.start, v.rows)]
            elif v.row is not None:
                source = given[i].at[pl.ds(pl.multiple_of(sc[v.row] * v.rows, v.rows), v.rows)]
            copies.append(Arriving(rest[n], pltpu.make_async_copy(source, rest[n], rest[-1].at[n])))
            given[i] = copies[-1]
        for v in copies:
            v.copy.start()
        if not lazy:
            for v in copies:
                v.here()
        body(sc, *given, *results, *own)
        for v in copies:
            v.here()
        leave(*leaving)
        for v in leaving:
            v.copy.wait()

    scratch_shapes = scratch + held + staged + [pltpu.SemaphoreType.DMA((max(len(staged) + len(held), 1),))]
    return pl.pallas_call(
        whole_body,
        out_shape=shapes,
        in_specs=[pl.BlockSpec(memory_space=pltpu.SMEM)] + specs,
        out_specs=[
            pl.BlockSpec(memory_space=pltpu.HBM) if b else whole_block(s.shape) for b, s in zip(back, shapes)
        ],
        grid=(1,),
        scratch_shapes=scratch_shapes,
        compiler_params=pltpu.CompilerParams(vmem_limit_bytes=vmem * 2**20),
        cost_estimate=pl.CostEstimate(flops=int(us * 1.15e9), bytes_accessed=0, transcendentals=0),
    )(scalars, *arrays)


def rows_at(start, count):
    return pl.ds(pl.multiple_of(start, count), count)


def row(ref):
    return ref[...].reshape(1, -1)


def normal_of(v):
    center = v - jnp.mean(v, axis=-1, keepdims=True)
    inverse = lax.rsqrt(jnp.mean(center * center, axis=-1, keepdims=True) + 1e-05)
    return center * inverse, inverse


def norm_back(gradient, normal, inverse, gain):
    scaled = gradient * gain
    adjusted = (
        scaled
        - jnp.mean(scaled, axis=-1, keepdims=True)
        - normal * jnp.mean(scaled * normal, axis=-1, keepdims=True)
    )
    return adjusted * inverse


def col_sum(v):
    return jnp.sum(v, axis=0, keepdims=True)


def set_places(sc):
    c, zh = sc[1], sc[2]
    return [2 * zh + c, 2 * (1 - zh) + c, 2 * zh + 1 - c, 2 * (1 - zh) + 1 - c]


def head_masks(width=256):
    lane = lax.broadcasted_iota(jnp.int32, (1, width), 1) // 64
    return [lane == h for h in range(4)]


def scalar_kernel(ids, tgt_len, src_len, pair_ids, loss_weights, out):
    for i in range(3):
        out[i] = ids[i]
    out[3] = tgt_len[ids[2]]
    out[4] = src_len[ids[2]]
    out[5] = loss_weights[pair_ids[ids[2]]]
    out[6] = ids[3]
    out[7] = ids[4]


VECTORS = ("first_gain", "first_shift", "self_output_bias", "second_gain", "second_shift")
VECTORS += ("cross_output_bias", "third_gain", "third_shift", "ffn_out_bias")


def vector(vecs, name):
    i = VECTORS.index(name)
    return vecs[i : i + 1, :]


def pack_kernel(sc, q, k, v, cq, ck, cv, o, co, qb, vb, cqb, cvb, fb, *refs):
    vectors, (one, wow, vecs) = refs[: len(VECTORS)], refs[len(VECTORS) :]
    for i, m in enumerate((q, k, v)):
        one[i * 64 : (i + 1) * 64, :] = m[...]
    for i, m in enumerate((cq, ck, cv)):
        one[208 + i * 64 : 272 + i * 64, :] = m[...]
    vec = jnp.concatenate([row(qb), row(vb), row(cqb), row(cvb), row(fb)], axis=1)
    high = vec.astype(BF).astype(F32)
    both = jnp.concatenate([high, vec - high], axis=1)
    first = lax.broadcasted_iota(jnp.int32, (16, 1024), 0) == 0
    one[192:208, :] = jnp.where(first, both, 0.0).astype(BF)
    wow[0:64, :] = o[...]
    wow[64:128, :] = co[...]
    for i, v in enumerate(vectors):
        vecs[i : i + 1, :] = row(v)
    vecs[len(VECTORS) : 16, :] = jnp.zeros((16 - len(VECTORS), 1024), F32)


def pack_more_kernel(sc, fin, fout, out):
    out[0:256, :] = fin[...].astype(F32).T.astype(BF)
    out[256:512, :] = fout[...]


def qkv_kernel(sc, t0, t1, t2, t3, vecs, a0, a1, a2, a3, first, tok, q, kv, w, bias):
    gain, shift = vector(vecs, "first_gain"), vector(vecs, "first_shift")
    for r, t in enumerate((t0, t1, t2, t3)):
        place = rows_at(lax.rem(sc[0] + r, 4) * 128, 128)
        tok[place, :] = t[...]
        normal, _ = normal_of(t[...].astype(F32))
        first[place, :] = (normal * gain + shift).astype(BF)
    for part, place in zip((a0, a1, a2, a3), set_places(sc)):
        for m in range(3):
            w[rows_at(m * 256 + place * 64, 64), :] = part[m * 64 : (m + 1) * 64, :]
        vec = part[192:208, :].astype(F32)[0:1, :]
        bias[pl.ds(place, 1), :] = vec[:, :512] + vec[:, 512:]
    x = first[...]

    def bias_of(i):
        return jnp.concatenate([bias[h : h + 1, i * 64 : (i + 1) * 64] for h in range(4)], axis=1)

    leave(first, tok, w, bias)
    kv[:, 0:256] = nt(x, w[256:512, :]).astype(BF)
    kv[:, 256:512] = (nt(x, w[512:768, :]) + bias_of(1)).astype(BF)
    leave(kv)
    q[...] = (SCALE * (nt(x, w[0:256, :]) + bias_of(0))).astype(BF)


def source_kernel(sc, mem, a0, a1, a2, a3, bias, ckv, w, own):
    for part, place in zip((a0, a1, a2, a3), set_places(sc)):
        for m in range(3):
            w[rows_at(m * 256 + place * 64, 64), :] = part[m * 64 : (m + 1) * 64, :]
    vb = jnp.concatenate([bias[h : h + 1, 192:256] for h in range(4)], axis=1)
    ckv[:, 0:256] = nt(mem[...], w[256:512, :]).astype(BF)
    ckv[:, 256:512] = (nt(mem[...], w[512:768, :]) + vb).astype(BF)
    for j in range(4):
        own[j * 128 : (j + 1) * 128, :] = mem[rows_at((2 * j + sc[1]) * 128, 128), :]


def key_bias(core, length, axis):
    k = lax.broadcasted_iota(jnp.int32, (1, 512) if axis == 1 else (512, 1), axis)
    position = ((k >> 7) * 2 + core) * 128 + (k & 127)
    return jnp.where(position < length, 0.0, NEG)


def diagonal_bias(key_core, query_core, transposed):
    q = lax.broadcasted_iota(jnp.int32, (256, 256), 1 if transposed else 0)
    k = lax.broadcasted_iota(jnp.int32, (256, 256), 0 if transposed else 1)
    q = ((q >> 7) * 2 + query_core) * 128 + (q & 127)
    k = ((k >> 7) * 2 + key_core) * 128 + (k & 127)
    return jnp.where(k <= q, 0.0, NEG)


def attend(q_rows, sources, biases):
    masks = head_masks()
    lane = lax.broadcasted_iota(jnp.int32, (1, 128), 1)
    count = q_rows.shape[0]
    mixed = jnp.zeros((count, 256), F32)
    totals = jnp.zeros((count, 128), F32)
    for h in range(4):
        qh = jnp.where(masks[h], q_rows, jnp.zeros_like(q_rows))
        scores = [nt(qh, k) + b for (k, _), b in zip(sources, biases)]
        top = functools.reduce(jnp.maximum, [jnp.max(s, axis=1, keepdims=True) for s in scores])
        raised = [jnp.exp(s - top) for s in scores]
        total = sum(jnp.sum(p, axis=1, keepdims=True) for p in raised)
        out = sum(nn(p.astype(BF), v) for p, (_, v) in zip(raised, sources))
        mixed = jnp.where(masks[h], out * (1.0 / total), mixed)
        totals = jnp.where(lane == h, top + jnp.log(total), totals)
    return mixed, totals


def causal_biases(sc, axis):
    c, length = sc[1], sc[3]
    transposed = axis == 0
    return (
        [key_bias(c, length, axis), key_bias(1 - c, length, axis)],
        [diagonal_bias(c, c, transposed), diagonal_bias(1 - c, c, transposed)],
    )


def pair_bias(length_bias, diagonal, a, axis):
    if axis == 1:
        last = length_bias[:, a * 256 : (a + 1) * 256] + diagonal
        if a == 0:
            return last
        return jnp.concatenate([jnp.broadcast_to(length_bias[:, 0:256], (256, 256)), last], axis=1)
    last = length_bias[a * 256 : (a + 1) * 256, :] + diagonal
    if a == 0:
        return last
    return jnp.concatenate([jnp.broadcast_to(length_bias[0:256, :], (256, 256)), last], axis=0)


def self_forward_kernel(sc, q, kvo, kvs, mixed, totals, stat):
    lengths, diagonals = causal_biases(sc, 1)
    for a in range(2):
        n = (a + 1) * 256
        sources = [(kvo[0:n, 0:256], kvo[0:n, 256:512]), (kvs[0:n, 0:256], kvs[0:n, 256:512])]
        biases = [pair_bias(lengths[i], diagonals[i], a, 1) for i in range(2)]
        out, total = attend(q[a * 256 : (a + 1) * 256, :], sources, biases)
        mixed[a * 256 : (a + 1) * 256, :] = out.astype(BF)
        stat[a * 256 : (a + 1) * 256, :] = total
    totals[...] = stat[...].T[0:8, :]


def cross_forward_kernel(sc, q, ckv, mixed, totals, stat):
    key = lax.broadcasted_iota(jnp.int32, (1, 1024), 1)
    bias = jnp.where(key < sc[4], 0.0, NEG)
    for a in range(2):
        out, total = attend(q[a * 256 : (a + 1) * 256, :], [(ckv[:, 0:256], ckv[:, 256:512])], [bias])
        mixed[a * 256 : (a + 1) * 256, :] = out.astype(BF)
        stat[a * 256 : (a + 1) * 256, :] = total
    totals[...] = stat[...].T[0:8, :]


def chip_rows(sc, whole, order):
    for r in range(4):
        chip = lax.rem(sc[0] + r, 4)
        for z in range(2):
            for core in range(2):
                place = r * 256 + z * 128 + core * 64
                order[place : place + 64, :] = whole[z * 8 + chip * 2 + core]


def set_rows(sc, sets, order):
    for r in range(4):
        chip = lax.rem(sc[0] + r, 4)
        for part, place in zip(sets, set_places(sc)):
            order[rows_at(r * 256 + place * 64, 64), :] = part[chip]


def second_kernel(
    sc, m0, m1, m2, m3, wo, tok, vecs, cw, bias, second, resid, cq, wo_own, order, work
):
    ob, gain, shift = (vector(vecs, n) for n in ("self_output_bias", "second_gain", "second_shift"))
    chip_rows(sc, wo, order)
    wo_own[...] = order[0:256, :]
    work[...] = nn(jnp.concatenate([m0[...], m1[...], m2[...], m3[...]], axis=1), order[...])
    for j in range(4):
        place = slice(j * 128, (j + 1) * 128)
        v = tok[place, :].astype(F32) + (work[place, :] + ob)
        resid[place, :] = v.astype(BF)
        normal, _ = normal_of(v)
        second[place, :] = (normal * gain + shift).astype(BF)
    leave(second, resid, wo_own)
    qb = jnp.concatenate([bias[h : h + 1, 128:192] for h in range(4)], axis=1)
    cq[...] = (SCALE * (nt(second[...], cw[0:256, :]) + qb)).astype(BF)


def upstream_kernel(sc, c0, c1, c2, c3, w0, w1, w2, w3, og, up):
    weight = 0.5 * sc[5].astype(F32)
    for r, t in enumerate((c0, c1, c2, c3)):
        chip = lax.rem(sc[0] + r, 4)
        position = (2 * chip + sc[1]) * 128 + lax.broadcasted_iota(jnp.int32, (128, 1), 0)
        og[rows_at(chip * 128, 128), :] = (t[...].astype(F32) * jnp.where(position < sc[3], weight, 0.0)).astype(BF)
    for s, w in enumerate((w0, w1, w2, w3)):
        up[:, s * 256 : (s + 1) * 256] = nt(og[...], w[...]).astype(BF)


def ffn_kernel(
    sc, m0, m1, m2, m3, wco, resid, vecs, up, w0, w1, w2, w3, bias,
    third, hidden, pre, back0, back1, back2, back3, own, wco_own, order, work,
):
    y = sc[0]
    ob, gain, shift = (vector(vecs, n) for n in ("cross_output_bias", "third_gain", "third_shift"))
    chip_rows(sc, wco, order)
    wco_own[...] = order[0:256, :]
    work[...] = nn(jnp.concatenate([m0[...], m1[...], m2[...], m3[...]], axis=1), order[...])
    for s, w in enumerate((w0, w1, w2, w3)):
        order[s * 256 : (s + 1) * 256, :] = w[...]
    for j in range(4):
        place = slice(j * 128, (j + 1) * 128)
        v = resid[place, :].astype(F32) + (work[place, :] + ob)
        work[place, :] = v
        normal, _ = normal_of(v)
        third[place, :] = (normal * gain + shift).astype(BF)
    own[...] = work[rows_at(y * 128, 128), :]
    leave(third, own, wco_own)
    places = set_places(sc)
    for s in range(4):
        cols = slice(s * 256, (s + 1) * 256)
        u = nt(third[...], order[cols, :]) + bias[pl.ds(places[s], 1), 256:512]
        square = u * u
        t = jnp.tanh(0.7978845608028654 * (u + 0.044715 * (square * u)))
        hidden[:, cols] = (0.5 * u * (1.0 + t)).astype(BF)
        slope = 0.5 * (1.0 + t) + 0.5 * u * (1.0 - t * t) * (0.7978845608028654 * (1.0 + 0.134145 * square))
        pre[:, cols] = (up[:, cols].astype(F32) * slope).astype(BF)
    leave(hidden, pre)
    store_rel(sc, nn(pre[...], order[...]), work, (back0, back1, back2, back3))


def store_rel(sc, value, work, outs):
    work[...] = value
    for r, out in enumerate(outs):
        out[...] = work[rows_at(lax.rem(sc[0] + r, 4) * 128, 128), :].astype(BF)


def total_of(parts):
    p = [v[...].astype(F32) for v in parts]
    return (p[0] + p[1]) + (p[2] + p[3])


def late_rows_kernel(sc, p0, p1, p2, p3, own, vecs, out, mem):
    total = total_of((p0, p1, p2, p3))
    out[...] = (own[...] + (total[0:128, :] + vector(vecs, "ffn_out_bias"))).astype(BF)
    mem[...] = total[128:256, :]


def split_rows(values):
    high = values.astype(BF).astype(F32)
    return jnp.concatenate([high, values - high, jnp.zeros((12, values.shape[1]), F32)], axis=0).astype(BF)


def joined_rows(block):
    f = block.astype(F32)
    return f[0:2, :] + f[2:4, :]


def third_grad_kernel(sc, p0, p1, p2, p3, own, cot, vecs, grad, low):
    position = (2 * sc[0] + sc[1]) * 128 + lax.broadcasted_iota(jnp.int32, (128, 1), 0)
    og = cot[...].astype(F32) * jnp.where(position < sc[3], 0.5 * sc[5].astype(F32), 0.0)
    back = total_of((p0, p1, p2, p3))
    normal, inverse = normal_of(own[...])
    total = og + norm_back(back, normal, inverse, vector(vecs, "third_gain"))
    grad[...] = total
    low[0:128, :] = total.astype(BF)
    low[128:144, :] = split_rows(jnp.concatenate([col_sum(back * normal), col_sum(back)], axis=0))


def masked_stack(v, stack):
    masks = head_masks()
    for a in range(2):
        rows = v[a * 256 : (a + 1) * 256, :]
        for h in range(4):
            stack[a, h * 256 : (h + 1) * 256, :] = jnp.where(masks[h], rows, jnp.zeros_like(rows))


def delta_of(mixed, grad):
    head = lax.broadcasted_iota(jnp.int32, (8, 256), 0)
    lane = lax.broadcasted_iota(jnp.int32, (8, 256), 1) // 64
    ones = jnp.where(head == lane, 1.0, 0.0)
    product = mixed.astype(F32) * grad.astype(F32)
    return lax.dot_general(
        ones, product, (((1,), (1,)), ((), ())), preferred_element_type=F32, precision=lax.Precision.HIGHEST
    )


def pair_backward(a, q_stack, g_stack, totals, delta, keys, values, keys_t, bias, probs, scores):
    cols = slice(a * 256, (a + 1) * 256)
    dq = []
    for h in range(4):
        place = slice(h * 256, (h + 1) * 256)
        qh, gh = q_stack[a, place, :], g_stack[a, place, :]
        for k in range(keys.shape[0] // 256):
            some = slice(k * 256, (k + 1) * 256)
            s = nt(keys[some, :], qh) + bias[some, :]
            p = jnp.exp(s - totals[h : h + 1, cols])
            ds = (p * (nt(values[some, :], gh) - delta[h : h + 1, cols])).astype(BF)
            probs[some, place] = p.astype(BF)
            scores[some, place] = ds
        dq.append(nn(keys_t[h * 64 : (h + 1) * 64, :], scores[:, place]))
    return jnp.concatenate(dq, axis=0)


def cross_backward_kernel(
    sc, t0, t1, t2, t3, wco, cq, ckv, mixed, totals, og, tg, dq, own, other, vec,
    q_stack, g_stack, probs, scores, delta, part,
):
    norm_sums = jnp.zeros((2, 1024), F32)
    for r, t in enumerate((t0, t1, t2, t3)):
        tg[rows_at(lax.rem(sc[0] + r, 4) * 128, 128), :] = t[0:128, :]
        norm_sums = norm_sums + joined_rows(t[128:144, :])
    vec[0:2, :] = norm_sums
    vec[2:3, :] = col_sum(og[...].astype(F32))
    vec[3:4, :] = col_sum(tg[...].astype(F32))
    vec[4:8, :] = jnp.zeros((4, 1024), F32)
    leave(tg, vec)
    g = nt(tg[...], wco[...]).astype(BF)
    delta[...] = delta_of(mixed[...], g)
    masked_stack(g, g_stack)
    masked_stack(cq[...], q_stack)
    key = lax.broadcasted_iota(jnp.int32, (1024, 1), 0)
    bias = jnp.where(key < sc[4], 0.0, NEG)
    keys_t = ckv[:, 0:256].T
    for a in range(2):
        grad = pair_backward(
            a, q_stack, g_stack, totals, delta, ckv[:, 0:256], ckv[:, 256:512], keys_t, bias, probs.at[a], scores.at[a]
        )
        dq[a * 256 : (a + 1) * 256, :] = grad.T.astype(BF)
    leave(dq)
    part[:, 0:256] = nn(scores[0], q_stack[0]) + nn(scores[1], q_stack[1])
    part[:, 256:512] = nn(probs[0], g_stack[0]) + nn(probs[1], g_stack[1])
    for j in range(4):
        place = slice(j * 128, (j + 1) * 128)
        own[place, :] = part[rows_at((2 * j + sc[1]) * 128, 128), :].astype(BF)
        other[place, :] = part[rows_at((2 * j + 1 - sc[1]) * 128, 128), :].astype(BF)


def second_grad_kernel(
    sc, d0, d1, d2, d3, a0, a1, a2, a3, resid, vecs, tg, tg_own, wo,
    low, grad_own, g, vec, order, work,
):
    gain = vector(vecs, "second_gain")
    set_rows(sc, (a0, a1, a2, a3), order)
    work[...] = nn(jnp.concatenate([d0[...], d1[...], d2[...], d3[...]], axis=1), order[...])
    sums = [jnp.zeros((1, 1024), F32)] * 3
    for j in range(4):
        place = slice(j * 128, (j + 1) * 128)
        normal, inverse = normal_of(resid[place, :].astype(F32))
        back = SCALE * work[place, :]
        v = norm_back(back, normal, inverse, gain)
        work[place, :] = v
        rounded = (tg[place, :].astype(F32) + v).astype(BF)
        low[place, :] = rounded
        for i, add in enumerate((back * normal, back, rounded.astype(F32))):
            sums[i] = sums[i] + col_sum(add)
    leave(low)
    g[...] = nt(low[...], wo[...]).astype(BF)
    leave(g)
    grad_own[...] = tg_own[...] + work[rows_at(sc[0] * 128, 128), :]
    vec[...] = jnp.concatenate(sums + [jnp.zeros((5, 1024), F32)], axis=0)


def self_backward_kernel(
    sc, g, q, kvo, kvs, mixed, totals, dq, own, other, q_stack, g_stack, p0, s0, p1, s1, delta
):
    delta[...] = delta_of(mixed[...], g[...])
    masked_stack(g[...], g_stack)
    masked_stack(q[...], q_stack)
    lengths, diagonals = causal_biases(sc, 0)
    keys_t = [kv[:, 0:256].T for kv in (kvo, kvs)]
    for a in range(2):
        n = (a + 1) * 256
        probs, scores = ((p0, s0), (p1, s1))[a]
        grad = jnp.zeros((256, 256), F32)
        for i, kv in enumerate((kvo, kvs)):
            bias = pair_bias(lengths[i], diagonals[i], a, 0)
            grad = grad + pair_backward(
                a, q_stack, g_stack, totals, delta, kv[0:n, 0:256], kv[0:n, 256:512], keys_t[i][:, 0:n], bias,
                probs.at[i], scores.at[i],
            )
        dq[a * 256 : (a + 1) * 256, :] = grad.T.astype(BF)
    leave(dq)
    for i, out in ((1, other), (0, own)):
        kind = out.dtype
        for cols, first, second, stack in (
            (slice(0, 256), s0, s1, q_stack),
            (slice(256, 512), p0, p1, g_stack),
        ):
            out[0:256, cols] = (nn(first[i], stack[0]) + nn(second[i, 0:256, :], stack[1])).astype(kind)
            out[256:512, cols] = nn(second[i, 256:512, :], stack[1]).astype(kind)
        leave(out)


def first_back_kernel(sc, dq, dkv, w, b0, b1, b2, b3, work):
    part = SCALE * nn(dq[...], w[0:256, :]) + nn(dkv[:, 0:256], w[256:512, :]) + nn(dkv[:, 256:512], w[512:768, :])
    store_rel(sc, part, work, (b0, b1, b2, b3))


def tokens_grad_kernel(sc, p0, p1, p2, p3, tokens, vecs, grad, out):
    normal, inverse = normal_of(tokens[...].astype(F32))
    out[...] = grad[...] + norm_back(
        total_of((p0, p1, p2, p3)), normal, inverse, vector(vecs, "first_gain")
    )


def memory_back_kernel(sc, grad, w, hidden, w0, w1, w2, w3, b0, b1, b2, b3, order, work):
    outs = (b0, b1, b2, b3)
    for s, part in enumerate((w0, w1, w2, w3)):
        order[s * 256 : (s + 1) * 256, :] = part[...]
    store_rel(sc, nn(hidden[...], order[...]), work, [b.at[0:128] for b in outs])
    value = nn(grad[:, 0:256], w[0:256, :]) + nn(grad[:, 256:512], w[256:512, :])
    store_rel(sc, value, work, [b.at[128:256] for b in outs])


def store_pieces(out, z, start, block):
    for i in range(8):
        out[i, z, start : start + block.shape[0], :] = block[:, i * 128 : (i + 1) * 128].astype(BF)


def store_bias(out, z, start, values, vectors=()):
    wide = jnp.concatenate([values, jnp.zeros((1, 1024 - values.shape[1]), F32)], axis=1)
    rows = [wide] + list(vectors)
    rows.append(jnp.zeros((16 - sum(v.shape[0] for v in rows), 1024), F32))
    store_pieces(out, z, start, jnp.concatenate(rows, axis=0))


def ffn_weight_kernel(sc, pre, third, hidden, og, keep, send):
    zh = sc[2]
    for s in range(4):
        out = keep if s < 2 else send
        z = zh if s % 2 == 0 else 1 - zh
        cols = slice(s * 256, (s + 1) * 256)
        store_pieces(out, z, 0, tn(pre[:, cols], third[...]))
        store_pieces(out, z, 256, tn(hidden[:, cols], og[...]))
        store_bias(out, z, 512, col_sum(pre[:, cols].astype(F32)))


def cross_weight_kernel(sc, own, other, mixed, tg, dq, second, mem, vec, dkv, keep, send, product):
    dkv[...] = (own[...].astype(F32) + other[...].astype(F32)).astype(BF)
    leave(dkv)
    sides = ((keep, sc[1]), (send, 1 - sc[1]))
    ones = jnp.ones((8, 512), BF)
    q_bias = SCALE * nn(ones, dq[...])[0:1, :]
    v_bias = nn(ones, dkv[:, 256:512])[0:1, :]
    for m in range(4):
        if m == 0:
            product[...] = tn(mixed[...], tg[...])
        elif m == 1:
            product[...] = SCALE * tn(dq[...], second[...])
        else:
            product[...] = tn(dkv[:, (m - 2) * 256 : (m - 1) * 256], mem[...])
        for z in range(2):
            for out, core in sides:
                store_pieces(out, z, m * 64, product[rows_at((2 * z + core) * 64, 64), :])
    for z in range(2):
        for out, core in sides:
            store_head_bias(out, z, core, q_bias, v_bias, [vec[0:4, :]])


def store_head_bias(out, z, core, q_bias, v_bias, vectors):
    rows = [
        jnp.concatenate([v[:, s * 64 : (s + 1) * 64] for v in (q_bias, v_bias)], axis=1) for s in (2 * z, 2 * z + 1)
    ]
    store_bias(out, z, 256, jnp.where(core == 0, rows[0], rows[1]), vectors)


def self_weight_kernel(sc, dq, own, other, tok, w, mixed, sg, vecs, vec2, dkv, keep, send, vec, normal, product):
    gain, shift = vector(vecs, "first_gain"), vector(vecs, "first_shift")
    dkv[...] = (own[...].astype(F32) + other[...].astype(F32)).astype(BF)
    leave(dkv)
    for j in range(4):
        place = slice(j * 128, (j + 1) * 128)
        normal[place, :] = normal_of(tok[place, :].astype(F32))[0].astype(BF)
    ones = jnp.ones((8, 512), BF)
    gain_sum = jnp.zeros((1, 1024), F32)
    shift_sum = jnp.zeros((1, 1024), F32)
    q_bias = v_bias = None
    for m, (grad, factor) in enumerate(((dq[...], SCALE), (dkv[:, 0:256], 1.0), (dkv[:, 256:512], 1.0))):
        sums = factor * tn(grad, ones.T)[:, 0:1]
        product[...] = factor * tn(grad, normal[...])
        weight = w[m * 256 : (m + 1) * 256, :].astype(F32)
        gain_sum = gain_sum + col_sum(weight * product[...])
        shift_sum = shift_sum + col_sum(weight * sums)
        total = product[...] * gain + sums * shift
        product[...] = total
        for z in range(2):
            for out, core in ((keep, sc[1]), (send, 1 - sc[1])):
                store_pieces(out, z, (m + 1) * 64, product[rows_at((2 * z + core) * 64, 64), :])
        if m != 1:
            flat = factor * nn(ones, grad)[0:1, :]
            if m == 0:
                q_bias = flat
            else:
                v_bias = flat
    sums_rows = split_rows(jnp.concatenate([gain_sum, shift_sum], axis=0))[0:4, :].astype(F32)
    product[...] = tn(mixed[...], sg[...])
    for z in range(2):
        for out, core in ((keep, sc[1]), (send, 1 - sc[1])):
            store_pieces(out, z, 0, product[rows_at((2 * z + core) * 64, 64), :])
            store_head_bias(out, z, core, q_bias, v_bias, [vec2[0:3, :], sums_rows])
    vec[...] = jnp.concatenate([gain_sum, shift_sum, jnp.zeros((6, 1024), F32)], axis=0)


def add_kernel(sc, *refs):
    out, start = refs[-1], 0
    for a, b in zip(refs[:-1:2], refs[1:-1:2]):
        rows = a.shape[2]
        for i in range(8):
            out[i, :, start : start + rows, :] = (a[i].astype(F32) + b[i].astype(F32)).astype(BF)
        start += rows


def piece_sum(got):
    total = got[0].astype(F32)
    for i in range(1, 16):
        total = total + got[i].astype(F32)
    return total.astype(BF)


def sum_kernel(sc, ffn, cross, out):
    out[0:528, :] = piece_sum(ffn)
    out[528:800, :] = piece_sum(cross)


def spread_kernel(sc, *refs):
    start, out = 0, refs[-1]
    for got in refs[:-1]:
        total = piece_sum(got) if len(got.shape) == 3 else got[...]
        rows = total.shape[0]
        for i in range(8):
            out[i, start : start + rows, :] = total
        start += rows


def ffn_result(got, start, fin, fout, fb):
    for i in range(8):
        fout[:, i * 128 : (i + 1) * 128] = got[i, start + 256 : start + 512, :].astype(F32)
    leave(fout)
    for i in range(8):
        fin[i * 128 : (i + 1) * 128, :] = got[i, start : start + 256, :].astype(F32).T
    leave(fin)
    rows = [got[i, start + 512 : start + 528, :].astype(F32)[0:1, :] for i in range(2)]
    fb[...] = jnp.concatenate(rows, axis=1).reshape(256)


def result_kernel(sc, got, *outs):
    ffn_result(got, 272, *outs[:3])
    heads_result(3, 0, got, *outs[3:12])
    heads_result(4, 800, got, *outs[12:22])


def first_total_kernel(sc, v0, v1, v2, v3, gain, shift):
    total = sum(jnp.concatenate([v[i].astype(F32) for i in range(8)], axis=1) for v in (v0, v1, v2, v3))
    gain[...] = (total[4:5, :] + total[6:7, :]).reshape(1024)
    shift[...] = (total[5:6, :] + total[7:8, :]).reshape(1024)


def heads_result(count, start, got, o, q, k, v, qb, vb, *vectors):
    for m, out in enumerate((o, q, k, v)):
        for i in range(8):
            out[:, i * 128 : (i + 1) * 128] = got[i, start + m * 64 : start + (m + 1) * 64, :].astype(F32)
        leave(out)
    rows = jnp.concatenate([got[i, start + 256 : start + 272, :].astype(F32) for i in range(8)], axis=1)
    qb[...] = rows[0:1, 0:64].reshape(64)
    vb[...] = rows[0:1, 64:128].reshape(64)
    for i in range(count):
        vectors[i][...] = rows[i + 1 : i + 2, :].reshape(1024)


def core_sum(sc, *pairs, us=4.8):
    rows = sum(keep.shape[2] for keep, _ in pairs)
    return run((add_kernel, us), [((8, 2, rows, 128), BF)], sc, far(*[v for pair in pairs for v in pair]), vmem=44)[0]


def pieces(both):
    return exchange(both.reshape((16,) + both.shape[2:]), ("x", "zl", "zh"))


def per_device(
    tokens,
    memory,
    cotangent,
    tgt_len,
    src_len,
    pair_ids,
    loss_weights,
    first_gain,
    first_shift,
    self_query,
    self_query_bias,
    self_key,
    self_value,
    self_value_bias,
    self_output,
    self_output_bias,
    second_gain,
    second_shift,
    cross_query,
    cross_query_bias,
    cross_key,
    cross_value,
    cross_value_bias,
    cross_output,
    cross_output_bias,
    third_gain,
    third_shift,
    ffn_in,
    ffn_in_bias,
    ffn_out,
    ffn_out_bias,
):
    ids = jnp.stack([lax.axis_index("y"), lax.axis_index("c"), lax.axis_index("zh")] + [lax.axis_index("x"), lax.axis_index("zl")]).astype(jnp.int32)
    sc = pl.pallas_call(
        scalar_kernel,
        out_shape=jax.ShapeDtypeStruct((8,), jnp.int32),
        in_specs=[pl.BlockSpec(memory_space=pltpu.SMEM)] * 5,
        out_specs=pl.BlockSpec(memory_space=pltpu.SMEM),
    )(ids, tgt_len, src_len, pair_ids, loss_weights)

    def after(v, *others):
        return lax.optimization_barrier((v,) + others)[0]

    nothing = jnp.zeros((8,), jnp.int32)

    tok_blocks = gather_rel(tokens)
    given = {
        "first_gain": first_gain,
        "first_shift": first_shift,
        "self_output_bias": self_output_bias,
        "second_gain": second_gain,
        "second_shift": second_shift,
        "cross_output_bias": cross_output_bias,
        "third_gain": third_gain,
        "third_shift": third_shift,
        "ffn_out_bias": ffn_out_bias,
    }
    one, wow, vecs = run(
        (pack_kernel, 3.3),
        [((400, 1024), BF), ((128, 1024), BF), ((16, 1024), F32)],
        nothing,
        far(self_query.T, self_key.T, self_value.T, cross_query.T, cross_key.T, cross_value.T)
        + far(self_output, cross_output)
        + [self_query_bias, self_value_bias, cross_query_bias, cross_value_bias, ffn_in_bias]
        + [given[n] for n in VECTORS],
        vmem=60,
    )
    one_half = from_half(one)
    one_core = from_core(one)
    (more,) = run(
        (pack_more_kernel, 3),
        [((512, 1024), BF)],
        sc,
        far(ffn_in, ffn_out),
        vmem=60,
    )
    whole_wow = lax.all_gather(wow, ("zh", "y", "c"), axis=0, tiled=True)
    wide = jnp.concatenate([one[208:272], one_half[208:272]], axis=0)
    query_own = lax.all_gather(after(wide, whole_wow), "y", axis=0, tiled=True)
    query_core = from_core(query_own)
    query_sets = [(query_own, 0), (query_own, 64), (query_core, 0), (query_core, 64)]
    one_core_half = from_core(after(one_half, more, *tok_blocks))

    def one_parts(start, rows):
        return [Far(v, start, rows) for v in (one, one_half, one_core, one_core_half)]

    first, tok, q, kv, w, bias = run(
        (qkv_kernel, 5.3),
        [((512, 1024), BF), ((512, 1024), BF), ((512, 256), BF), ((512, 512), BF), ((768, 1024), BF), ((4, 512), F32)],
        sc,
        far(*tok_blocks, vecs) + one_parts(0, 208),
        lazy=True,
    )
    kvs = from_core(kv)
    self_mixed, self_totals = run(
        (self_forward_kernel, 5.8),
        [((512, 256), BF), ((8, 512), F32)],
        sc,
        far(q, kv, kvs),
        [pltpu.VMEM((512, 128), F32)],
    )
    mixed_blocks = gather_rel(self_mixed)
    more_half = from_half(after(more, self_mixed))
    cot_blocks = gather_rel(after(cotangent, *mixed_blocks))
    more_core = from_core(after(more, self_mixed))

    ckv, cw, mem_own = run(
        (source_kernel, 6),
        [((1024, 512), BF), ((768, 1024), BF), ((512, 1024), BF)],
        sc,
        [Far(memory, 0, 1024, row=2)] + one_parts(208, 192) + [Far(after(bias, wide))],
    )
    second, resid, cq, wo_own = run(
        (second_kernel, 8),
        [((512, 1024), BF), ((512, 1024), BF), ((512, 256), BF), ((256, 1024), BF)],
        sc,
        far(*mixed_blocks) + [Far(whole_wow, 0, 64, block=128)] + far(tok, vecs) + [Far(cw, 0, 256), Far(bias)],
        [pltpu.VMEM((1024, 1024), BF), pltpu.VMEM((512, 1024), F32)],
        lazy=True,
    )
    cross_mixed, cross_totals = run(
        (cross_forward_kernel, 6),
        [((512, 256), BF), ((8, 512), F32)],
        sc,
        far(after(cq, *cot_blocks), ckv),
        [pltpu.VMEM((512, 128), F32)],
    )
    cross_blocks = gather_rel(cross_mixed)
    more_core_half = from_core(after(more_half, cross_mixed))

    def more_parts(start, rows):
        return [Far(v, start, rows) for v in (more, more_half, more_core, more_core_half)]

    og, up = run(
        (upstream_kernel, 5),
        [((512, 1024), BF), ((512, 1024), BF)],
        sc,
        far(*cot_blocks) + more_parts(256, 256),
    )
    rows_out = [((128, 1024), BF)] * 4
    third, hidden, pre, b0, b1, b2, b3, resid_own, wco_own = run(
        (ffn_kernel, 11.5),
        [((512, 1024), BF)] * 3 + rows_out + [((128, 1024), F32), ((256, 1024), BF)],
        sc,
        far(*cross_blocks) + [Far(whole_wow, 64, 64, block=128)] + far(resid, vecs, up) + more_parts(0, 256) + [Far(bias)],
        [pltpu.VMEM((1024, 1024), BF), pltpu.VMEM((512, 1024), F32)],
    )
    third_parts = scatter_rel([b0, b1, b2, b3])
    ffn_keep, ffn_send = run(
        (ffn_weight_kernel, 7),
        [((8, 2, 528, 128), BF)] * 2,
        sc,
        far(pre, third, hidden, og),
        lazy=True,
    )
    third_grad, third_low = run(
        (third_grad_kernel, 20),
        [((128, 1024), F32), ((144, 1024), BF)],
        sc,
        far(*third_parts, resid_own, cotangent, vecs), vmem=44)
    tg_blocks = gather_rel(third_low)
    ffn_both = core_sum(sc, (ffn_keep, from_core(ffn_send)))

    tg, cdq, ckv_own, ckv_other, third_vec = run(
        (cross_backward_kernel, 1.5),
        [((512, 1024), BF), ((512, 256), BF), ((512, 512), BF), ((512, 512), BF), ((8, 1024), F32)],
        sc,
        far(*tg_blocks, wco_own, cq, ckv, cross_mixed, after(cross_totals, ffn_both, query_core), og),
        [
            pltpu.VMEM((2, 1024, 256), BF),
            pltpu.VMEM((2, 1024, 256), BF),
            pltpu.VMEM((2, 1024, 1024), BF),
            pltpu.VMEM((2, 1024, 1024), BF),
            pltpu.VMEM((8, 512), F32),
            pltpu.VMEM((1024, 512), F32),
        ],
    )
    cdq_blocks = gather_rel(cdq)
    ckv_got = from_core(ckv_other)
    ckv_grad, cross_keep, cross_send = run(
        (cross_weight_kernel, 1.5),
        [((512, 512), BF)] + [((8, 2, 272, 128), BF)] * 2,
        sc,
        far(ckv_own, ckv_got, cross_mixed, tg, cdq, second, mem_own, third_vec),
        [pltpu.VMEM((256, 1024), F32)],
    )
    cross_both = core_sum(sc, (cross_keep, from_core(cross_send)), us=1.5)
    ffn_pieces = pieces(ffn_both)
    cross_pieces = pieces(after(cross_both, ffn_pieces))
    sg, second_grad, self_grad, second_vec = run(
        (second_grad_kernel, 8.5),
        [((512, 1024), BF), ((128, 1024), F32), ((512, 256), BF), ((8, 1024), F32)],
        sc,
        far(*cdq_blocks) + [Far(v, s, 64, block=128) for v, s in query_sets] + far(resid, vecs, tg, third_grad, after(wo_own, cross_keep, ffn_pieces)),
        [pltpu.VMEM((1024, 1024), BF), pltpu.VMEM((512, 1024), F32)],
    )

    dq, kv_own, kv_other = run(
        (self_backward_kernel, 12),
        [((512, 256), BF), ((512, 512), BF), ((512, 512), BF)],
        sc,
        far(self_grad, q, kv, kvs, self_mixed, after(self_totals, cross_both)),
        [
            pltpu.VMEM((2, 1024, 256), BF),
            pltpu.VMEM((2, 1024, 256), BF),
            pltpu.VMEM((2, 256, 1024), BF),
            pltpu.VMEM((2, 256, 1024), BF),
            pltpu.VMEM((2, 512, 1024), BF),
            pltpu.VMEM((2, 512, 1024), BF),
            pltpu.VMEM((8, 512), F32),
        ],
    )
    kv_got = from_core(kv_other)
    dkv, self_keep, self_send, first_vec = run(
        (self_weight_kernel, 8),
        [((512, 512), BF), ((8, 2, 272, 128), BF), ((8, 2, 272, 128), BF), ((8, 1024), F32)],
        sc,
        far(dq, kv_own, kv_got, after(tok, cross_pieces), w, self_mixed, sg, vecs, second_vec),
        [pltpu.VMEM((512, 1024), BF), pltpu.VMEM((256, 1024), F32)],
    )
    self_recv = from_core(self_send)
    late_part = run(
        (memory_back_kernel, 2),
        [((256, 1024), BF)] * 4,
        sc,
        far(after(ckv_grad, self_recv)) + [Far(cw, 256, 512), Far(hidden)] + more_parts(256, 256),
        [pltpu.VMEM((1024, 1024), BF), pltpu.VMEM((512, 1024), F32)],
    )
    late_parts = scatter_rel(late_part)
    self_both = core_sum(sc, (self_keep, self_recv))
    (early_piece,) = run(
        (sum_kernel, 2), [((800, 128), BF)], sc, far(after(ffn_pieces, self_both), cross_pieces)
    )
    (copies,) = run(
        (spread_kernel, 4), [((8, 1072, 128), BF)], sc, far(after(pieces(self_both), late_part[0]), early_piece)
    )
    got = exchange(copies, ("x", "zl"))
    first_part = run(
        (first_back_kernel, 2),
        rows_out,
        sc,
        far(dq, after(dkv, copies), w),
        [pltpu.VMEM((512, 1024), F32)],
    )
    first_parts = scatter_rel(first_part)
    (tokens_grad,) = run(
        (tokens_grad_kernel, 15), [((128, 1024), F32)], sc, far(*first_parts, tokens, vecs, second_grad)
    )
    block_out, memory_grad = run(
        (late_rows_kernel, 15), [((128, 1024), BF), ((128, 1024), F32)], sc, far(*late_parts, resid_own, vecs)
    )
    got = after(got, block_out, tokens_grad)
    first_sums = gather_rel(got[:, 256:272, :])
    heads_out = [((64, 1024), F32)] * 4 + [((64,), F32)] * 2
    heads_out = heads_out + [((1024,), F32)] * 3 + heads_out + [((1024,), F32)] * 4
    heads_out = [((1024, 256), F32), ((256, 1024), F32), ((256,), F32)] + heads_out
    ffn_in_grad, ffn_out_grad, ffn_in_bias_grad, *outs = run((result_kernel, 7), heads_out, sc, far(got))
    first_gain_grad, first_shift_grad = run(
        (first_total_kernel, 1.5), [((1024,), F32)] * 2, sc, far(*first_sums)
    )
    self_out, cross_out = outs[:9], outs[9:]
    return (
        block_out,
        tokens_grad,
        memory_grad,
        first_gain_grad,
        first_shift_grad,
        self_out[1].T,
        self_out[4],
        self_out[2].T,
        self_out[3].T,
        self_out[5],
        self_out[0],
        self_out[8],
        self_out[6],
        self_out[7],
        cross_out[1].T,
        cross_out[4],
        cross_out[2].T,
        cross_out[3].T,
        cross_out[5],
        cross_out[0],
        cross_out[9],
        cross_out[6],
        cross_out[7],
        ffn_in_grad,
        ffn_in_bias_grad,
        ffn_out_grad,
        cross_out[8],
    )


def solution(mesh):
    fine = Mesh(mesh.devices.reshape(4, 2, 2, 4, 2), ("x", "zl", "zh", "y", "c"))
    dp = ("x", "zl")
    mp = ("zh", "y", "c")
    rows, cols, part, down, whole = P(dp + mp, None), P(None, mp), P(mp), P(mp, None), P()
    placed = (rows, P(dp, None), rows, P(dp), P(dp), P(dp), whole, whole, whole)
    placed += (cols, part, cols, cols, part, down, whole, whole, whole)
    placed += (cols, part, cols, cols, part, down, whole, whole, whole)
    placed += (cols, part, down, whole)
    attention = (cols, part, cols, cols, part, down, whole)
    given = (rows, rows, rows, whole, whole) + attention + (whole, whole) + attention + (whole, whole)
    given += (cols, part, down, whole)
    return jax.shard_map(per_device, mesh=fine, in_specs=placed, out_specs=given, check_vma=False)
```
